32 devices in a mesh: head: 4 (over z), batch: 4 (over x, core), rep: 2 (over y).
Axes of the slice: x: 2, y: 2, z: 4, core: 2. Of those that a mesh axis runs over, the one named last changes fastest.
Arguments:
- tokens_in: bfloat16 [8192, 512], P(('batch', 'rep')), may hold values from -6 to 6
- out_grad: float32 [8192, 512], P(('batch', 'rep')), may hold values from -6 to 6
- lengths: int32 [64], P(('batch', 'rep')), may hold values from 32 to 128
- labels: int32 [64], P(('batch', 'rep')), may hold values from 0 to 2
- task_id: int32 [64], P(('batch', 'rep')), may hold values from 0 to 8
- qkv_weight: float32 [3, 512, 512], P(None, None, 'head')
- qkv_first: float32 [3, 512, 512], P(None, None, 'head')
- qkv_second: float32 [3, 512, 512], P(None, None, 'head'), as said below
- out_weight: float32 [512, 512], P('head')
- out_first: float32 [512, 512], P('head')
- out_second: float32 [512, 512], P('head'), as said below
- up_weight: float32 [512, 4, 512], P(None, None, 'head')
- up_first: float32 [512, 4, 512], P(None, None, 'head')
- up_second: float32 [512, 4, 512], P(None, None, 'head'), as said below
- down_weight: float32 [4, 512, 512], P(None, 'head')
- down_first: float32 [4, 512, 512], P(None, 'head')
- down_second: float32 [4, 512, 512], P(None, 'head'), as said below
- split_bias: float32 [6, 512], P(None, 'head'), may hold values from -3 to 3
- split_first: float32 [6, 512], P(None, 'head')
- split_second: float32 [6, 512], P(None, 'head'), as said below
- norm_params: float32 [6, 512], replicated
- norm_first: float32 [6, 512], replicated
- norm_second: float32 [6, 512], replicated, as said below
- class_weight: float32 [9, 512, 3], replicated, may hold values from -0.25 to 0.25
- class_first: float32 [9, 512, 3], replicated
- class_second: float32 [9, 512, 3], replicated, as said below
Outputs:
- output: float32 [8192, 512], P(('batch', 'rep'))
- input_grad: float32 [8192, 512], P(('batch', 'rep'))
- grad_norm: float32 [], replicated
- qkv_first_out: float32 [3, 512, 512], P(None, None, 'head')
- qkv_second_out: float32 [3, 512, 512], P(None, None, 'head')
- qkv_weight_out: float32 [3, 512, 512], P(None, None, 'head')
- out_first_out: float32 [512, 512], P('head')
- out_second_out: float32 [512, 512], P('head')
- out_weight_out: float32 [512, 512], P('head')
- up_first_out: float32 [512, 4, 512], P(None, None, 'head')
- up_second_out: float32 [512, 4, 512], P(None, None, 'head')
- up_weight_out: float32 [512, 4, 512], P(None, None, 'head')
- down_first_out: float32 [4, 512, 512], P(None, 'head')
- down_second_out: float32 [4, 512, 512], P(None, 'head')
- down_weight_out: float32 [4, 512, 512], P(None, 'head')
- split_first_out: float32 [6, 512], P(None, 'head')
- split_second_out: float32 [6, 512], P(None, 'head')
- split_bias_out: float32 [6, 512], P(None, 'head')
- norm_first_out: float32 [6, 512], replicated
- norm_second_out: float32 [6, 512], replicated
- norm_params_out: float32 [6, 512], replicated
- class_first_out: float32 [9, 512, 3], replicated
- class_second_out: float32 [9, 512, 3], replicated
- class_weight_out: float32 [9, 512, 3], replicated
The draws below stay inside these ranges and needn't reach their ends.
Inputs may be any that keep to these rules, and one draw needn't show every extreme that they name: `qkv_second`: positive. `out_second`: positive. `up_second`: positive. `down_second`: positive. `split_second`: positive. `norm_second`: positive. `class_second`: positive.
All inputs are finite; a program needn't handle non-finite values.
Results may differ from the reference program's by a relative error of at most 0.012.
The reference program's roundings to bfloat16 on the way count: a program that leaves them out, or rounds other values in their place, can miss the bound.
Values sent between devices are 32-bit elements; how exact they have to be, the bound alone decides.
No kernel may reach another device: no remote copies, remote signals or barrier semaphores. Data moves between devices by JAX's collectives and lax.ppermute only.
A program may use at most 128 MiB of HBM per device.

```python
import math
import jax
import jax.numpy as jnp
from jax import lax

D = 512
HEADS = 8
HEAD_DIM = 64
FF = 2048
SEQ_LEN = 128
TASKS = 9
CLASSES = 3
STEP = 10
SEQS = 64
TOKENS = 8192


def base_law(key, shape):
    return jnp.clip(jax.random.normal(key, shape, jnp.float32), -6.0, 6.0)


def rising(count):
    strength = 2.0
    position = jnp.arange(count, dtype=jnp.float32) / float(max(count - 1, 1))
    return jnp.sqrt(1.0 + strength * position)


def gradient_size(weight_kind):
    total_params = 4 * D * D + 2 * D * FF + 12 * D + TASKS * D * CLASSES
    return weight_kind / math.sqrt(total_params)


def first_law(key, shape, weight_kind):
    return jnp.clip(jax.random.normal(key, shape, jnp.float32), -6.0, 6.0) * (gradient_size(weight_kind) / 9.0)


def second_law(key, shape, weight_kind):
    expected = gradient_size(weight_kind)
    spread = jax.random.uniform(key, shape, jnp.float32)
    return expected * expected / 999.0 * 0.5 * jnp.exp(spread * math.log(16.0))


def draw_qkv_weight(key, part):
    key = jax.random.fold_in(key, 101)
    values = base_law(key, (3, D, D)) / math.sqrt(D)
    slot_index = jnp.arange(3)[:, None, None]
    factor = jnp.where(slot_index == 2, rising(D)[None, None, :], 1.0)
    return values * factor


def draw_out_weight(key, part):
    key = jax.random.fold_in(key, 102)
    return base_law(key, (D, D)) * math.sqrt(16.0 / D) * rising(D)[:, None]


def draw_up_weight(key, part):
    key = jax.random.fold_in(key, 103)
    return base_law(key, (D, 4, D)) / math.sqrt(D) * rising(D)[None, None, :]


def draw_down_weight(key, part):
    key = jax.random.fold_in(key, 104)
    return base_law(key, (4, D, D)) / math.sqrt(FF) * rising(D)[None, :, None]


def draw_norm_params(key, part):
    key = jax.random.fold_in(key, 105)
    spread = jax.random.uniform(key, (6, D), jnp.float32, -1.0, 1.0)
    row_index = jnp.arange(6)[:, None]
    return jnp.where((row_index == 1) | (row_index == 4), 1.0 + 0.3 * spread, 0.5 * spread)


def draw_qkv_first(key, part):
    key = jax.random.fold_in(key, 201)
    return first_law(key, (3, D, D), 1.0)


def draw_qkv_second(key, part):
    key = jax.random.fold_in(key, 202)
    return second_law(key, (3, D, D), 1.0)


def draw_out_first(key, part):
    key = jax.random.fold_in(key, 203)
    return first_law(key, (D, D), 1.0)


def draw_out_second(key, part):
    key = jax.random.fold_in(key, 204)
    return second_law(key, (D, D), 1.0)


def draw_up_first(key, part):
    key = jax.random.fold_in(key, 205)
    return first_law(key, (D, 4, D), 1.0)


def draw_up_second(key, part):
    key = jax.random.fold_in(key, 206)
    return second_law(key, (D, 4, D), 1.0)


def draw_down_first(key, part):
    key = jax.random.fold_in(key, 207)
    return first_law(key, (4, D, D), 1.0)


def draw_down_second(key, part):
    key = jax.random.fold_in(key, 208)
    return second_law(key, (4, D, D), 1.0)


def draw_split_first(key, part):
    key = jax.random.fold_in(key, 209)
    return first_law(key, (6, D), 4.0)


def draw_split_second(key, part):
    key = jax.random.fold_in(key, 210)
    return second_law(key, (6, D), 4.0)


def draw_norm_first(key, part):
    key = jax.random.fold_in(key, 211)
    return first_law(key, (6, D), 4.0)


def draw_norm_second(key, part):
    key = jax.random.fold_in(key, 212)
    return second_law(key, (6, D), 4.0)


def draw_class_first(key, part):
    key = jax.random.fold_in(key, 213)
    return first_law(key, (TASKS, D, CLASSES), 1.0 / math.sqrt(TASKS * SEQ_LEN))


def draw_class_second(key, part):
    key = jax.random.fold_in(key, 214)
    return second_law(key, (TASKS, D, CLASSES), 1.0 / math.sqrt(TASKS * SEQ_LEN))


def set_ends(entries, own_key, smallest, high):
    spot = [jax.random.randint(jax.random.fold_in(own_key, axis), (), 0, length) for axis, length in enumerate(entries.shape)]
    main_axis = entries.shape.index(max(entries.shape))
    beside = spot[:main_axis] + [(spot[main_axis] + 1) % entries.shape[main_axis]] + spot[main_axis + 1:]
    return entries.at[tuple(spot)].set(smallest).at[tuple(beside)].set(high)


def steps_of(stream_key, dims, shards, low, top_value):
    gain = 1.0
    for dim, blocks in shards:
        steps = jax.random.uniform(jax.random.fold_in(jax.random.fold_in(stream_key, 6), dim), (blocks,), jnp.float32, low / len(shards), top_value / len(shards))
        gain = gain * jnp.repeat(jnp.exp(steps), dims[dim] // blocks).reshape((-1,) + (1,) * (len(dims) - 1 - dim))
    return gain


def noise(stream_key, extent, deviation, most, shards=(), kind=jnp.bfloat16):
    result = deviation * jax.random.normal(stream_key, extent, jnp.float32)
    if shards:
        result = result * steps_of(stream_key, extent, shards, -0.22, 0.18)
    return jnp.clip(result, -most, most).astype(kind)


def setup_inputs(seed: int = 0) -> dict:
    seeds = jax.random.split(jax.random.key(seed), 27)
    tokens_in = noise(seeds[0], (TOKENS, D), 1.0, 6.0, ((0, 8),))
    out_grad = noise(seeds[1], (TOKENS, D), 1.0, 6.0, ((0, 8),), jnp.float32)
    lengths = set_ends(jax.random.randint(seeds[2], (SEQS,), SEQ_LEN // 4, SEQ_LEN + 1), jax.random.fold_in(seeds[2], 1), SEQ_LEN // 4, SEQ_LEN).astype(jnp.int32)
    labels = set_ends(jax.random.randint(seeds[3], (SEQS,), 0, CLASSES), jax.random.fold_in(seeds[3], 1), 0, CLASSES - 1).astype(jnp.int32)
    task_id = set_ends(jax.random.randint(seeds[4], (SEQS,), 0, TASKS), jax.random.fold_in(seeds[4], 1), 0, TASKS - 1).astype(jnp.int32)
    qkv_weight = draw_qkv_weight(jax.random.fold_in(seeds[26], 71), 0)
    qkv_first = draw_qkv_first(jax.random.fold_in(seeds[26], 71), 0)
    qkv_second = draw_qkv_second(jax.random.fold_in(seeds[26], 71), 0)
    out_weight = draw_out_weight(jax.random.fold_in(seeds[26], 71), 0)
    out_first = draw_out_first(jax.random.fold_in(seeds[26], 71), 0)
    out_second = draw_out_second(jax.random.fold_in(seeds[26], 71), 0)
    up_weight = draw_up_weight(jax.random.fold_in(seeds[26], 71), 0)
    up_first = draw_up_first(jax.random.fold_in(seeds[26], 71), 0)
    up_second = draw_up_second(jax.random.fold_in(seeds[26], 71), 0)
    down_weight = draw_down_weight(jax.random.fold_in(seeds[26], 71), 0)
    down_first = draw_down_first(jax.random.fold_in(seeds[26], 71), 0)
    down_second = draw_down_second(jax.random.fold_in(seeds[26], 71), 0)
    split_bias = noise(seeds[17], (6, D), 0.5, 3.0, ((1, 4),), jnp.float32)
    split_first = draw_split_first(jax.random.fold_in(seeds[26], 71), 0)
    split_second = draw_split_second(jax.random.fold_in(seeds[26], 71), 0)
    norm_params = draw_norm_params(jax.random.fold_in(seeds[26], 71), 0)
    norm_first = draw_norm_first(jax.random.fold_in(seeds[26], 71), 0)
    norm_second = draw_norm_second(jax.random.fold_in(seeds[26], 71), 0)
    class_weight = noise(seeds[23], (TASKS, D, CLASSES), D ** -0.5, 0.25, (), jnp.float32)
    class_first = draw_class_first(jax.random.fold_in(seeds[26], 71), 0)
    class_second = draw_class_second(jax.random.fold_in(seeds[26], 71), 0)
    return {"tokens_in": tokens_in, "out_grad": out_grad, "lengths": lengths, "labels": labels, "task_id": task_id, "qkv_weight": qkv_weight, "qkv_first": qkv_first, "qkv_second": qkv_second, "out_weight": out_weight, "out_first": out_first, "out_second": out_second, "up_weight": up_weight, "up_first": up_first, "up_second": up_second, "down_weight": down_weight, "down_first": down_first, "down_second": down_second, "split_bias": split_bias, "split_first": split_first, "split_second": split_second, "norm_params": norm_params, "norm_first": norm_first, "norm_second": norm_second, "class_weight": class_weight, "class_first": class_first, "class_second": class_second}


@jax.custom_vjp
def low(v):
    return lax.optimization_barrier(v.astype(jnp.bfloat16)).astype(jnp.float32)

@jax.custom_vjp
def low_back(v):
    return v

def low_keep(v):
    return (low(v), None)

def low_pass(kept, grad):
    return (grad,)

def back_keep(v):
    return (v, None)

def back_low(kept, grad):
    return (low(grad),)
low.defvjp(low_keep, low_pass)
low_back.defvjp(back_keep, back_low)
beta_one = 0.9
beta_two = 0.999
learn_rate = 0.05
vector_rate = 0.4
weight_decay = 0.01
adam_eps = 1e-08
clip_at = 1.0
norm_eps = 1e-12
masked = -1e+30

def matmul(left, right):
    return jnp.dot(left, right, precision=lax.Precision.HIGHEST)

def layer_norm(values, gain_row, shift_row):
    row_mean = lax.optimization_barrier(jnp.mean(values, -1, keepdims=True))
    centred = values - row_mean
    spread = lax.optimization_barrier(jnp.mean(centred * centred, -1, keepdims=True))
    return centred * lax.rsqrt(spread + norm_eps) * gain_row + shift_row

def forward(weights, rows_in, grad_rows, len_rows, label_rows, task_rows):
    qkv_weight, out_weight, up_weight, down_weight, split_bias, norm_params, class_weight = weights
    row_count = rows_in.shape[0]
    seq_count = row_count // SEQ_LEN
    qkv_low = low(qkv_weight)
    query = low_back(low(matmul(rows_in, qkv_low[0]) + split_bias[0]))
    key_low = low_back(low(matmul(rows_in, qkv_low[1])))
    value = low_back(low(matmul(rows_in, qkv_low[2]) + split_bias[1]))

    def per_head(matrix):
        return matrix.reshape(seq_count, SEQ_LEN, HEADS, HEAD_DIM)
    raw = jnp.einsum('sqhd,skhd->shqk', per_head(query), per_head(key_low), precision=lax.Precision.HIGHEST)
    raw = low_back(raw)
    position = jnp.arange(SEQ_LEN, dtype=jnp.int32)
    visible = (position[None, :] < len_rows[:, None])[:, None, None, :]
    scores = jnp.where(visible, raw * (1.0 / math.sqrt(HEAD_DIM)), masked)
    row_top = lax.optimization_barrier(jnp.max(scores, -1, keepdims=True))
    exponent = jnp.exp(scores - row_top)
    attn_prob = exponent / lax.optimization_barrier(jnp.sum(exponent, -1, keepdims=True))
    context = jnp.einsum('shqk,skhd->sqhd', low(attn_prob), per_head(value), precision=lax.Precision.HIGHEST)
    context = low_back(low(context.reshape(row_count, D)))
    attn = low_back(matmul(context, low(out_weight)))
    pre_one = rows_in + attn + norm_params[0]
    hidden_one = layer_norm(pre_one, norm_params[1], norm_params[2])
    pre_act = low_back(matmul(low(hidden_one), low(up_weight).reshape(D, FF)) + split_bias[2:].reshape(FF))
    act_low = low(jax.nn.gelu(pre_act, approximate=False))
    ffn = low_back(matmul(act_low, low(down_weight).reshape(FF, D)))
    pre_two = hidden_one + ffn + norm_params[3]
    output = layer_norm(pre_two, norm_params[4], norm_params[5])
    first_rows = output.reshape(seq_count, SEQ_LEN, D)[:, 0]
    task_pick = (jnp.arange(TASKS, dtype=jnp.int32)[None, :] == task_rows[:, None]).astype(jnp.float32)
    task_table = jnp.einsum('st,tdc->sdc', task_pick, class_weight, precision=lax.Precision.HIGHEST)
    logits = jnp.einsum('sd,sdc->sc', first_rows, task_table, precision=lax.Precision.HIGHEST)
    top_logit = lax.optimization_barrier(jnp.max(logits, -1, keepdims=True))
    log_total = top_logit[:, 0] + jnp.log(lax.optimization_barrier(jnp.sum(jnp.exp(logits - top_logit), -1)))
    target = (jnp.arange(CLASSES, dtype=jnp.int32)[None, :] == label_rows[:, None]).astype(jnp.float32)
    loss = jnp.sum(log_total - lax.optimization_barrier(jnp.sum(logits * target, -1)))
    return (jnp.sum(output * grad_rows) + loss, output)

def adam_step(weight, first, second, grad, factor, with_decay):
    clipped = grad * factor
    first_new = beta_one * first + (1.0 - beta_one) * clipped
    second_new = beta_two * second + (1.0 - beta_two) * clipped * clipped
    first_hat = first_new / (1.0 - beta_one ** STEP)
    second_hat = second_new / (1.0 - beta_two ** STEP)
    update = first_hat / (jnp.sqrt(second_hat) + adam_eps)
    if with_decay:
        update = update + weight_decay * weight
        rate = learn_rate
    else:
        rate = vector_rate
    return (first_new, second_new, weight - rate * update)

def reference(tokens_in, out_grad, lengths, labels, task_id, qkv_weight, qkv_first, qkv_second, out_weight, out_first, out_second, up_weight, up_first, up_second, down_weight, down_first, down_second, split_bias, split_first, split_second, norm_params, norm_first, norm_second, class_weight, class_first, class_second):
    params = (qkv_weight, out_weight, up_weight, down_weight, split_bias, norm_params, class_weight)
    group_size = math.gcd(SEQS, 4096 // SEQ_LEN)
    blocks = SEQS // group_size
    block_rows = group_size * SEQ_LEN
    tokens_f = tokens_in.astype(jnp.float32).reshape(blocks, block_rows, D)
    grads_in = out_grad.reshape(blocks, block_rows, D)
    len_blocks = lengths.reshape(blocks, group_size)
    label_blocks = labels.reshape(blocks, group_size)
    task_blocks = task_id.reshape(blocks, group_size)

    def one_block(totals, pieces):
        rows_in, grad_rows, len_rows, label_rows, task_rows = pieces

        def objective(weights, inputs):
            return forward(weights, inputs, grad_rows, len_rows, label_rows, task_rows)
        value_out, pull_back, output = jax.vjp(objective, params, rows_in, has_aux=True)
        weight_grads, input_grad = pull_back(jnp.ones((), value_out.dtype))
        return (jax.tree.map(jnp.add, totals, weight_grads), (output, input_grad))
    zero_grads = jax.tree.map(jnp.zeros_like, params)
    totals, (outputs, input_grads) = lax.scan(one_block, zero_grads, (tokens_f, grads_in, len_blocks, label_blocks, task_blocks))
    squares = sum((jnp.sum(element * element) for element in totals))
    grad_norm = jnp.sqrt(squares)
    factor = jnp.minimum(1.0, clip_at / (grad_norm + 1e-06))
    states = ((qkv_first, qkv_second, True), (out_first, out_second, True), (up_first, up_second, True), (down_first, down_second, True), (split_first, split_second, False), (norm_first, norm_second, False), (class_first, class_second, True))
    results = ()
    for weight, grad, state in zip(params, totals, states):
        results = results + adam_step(weight, state[0], state[1], grad, factor, state[2])
    return (outputs.reshape(TOKENS, D), input_grads.reshape(TOKENS, D), grad_norm) + results
```

```python
import functools
import math

import jax
import jax.numpy as jnp
from jax import lax
from jax.experimental import pallas as pl
from jax.experimental.pallas import tpu as pltpu
from jax.sharding import PartitionSpec as P

HEAD_DIM = 64
STEP = 10
LANES = 128
BLOCK = 256

F32 = jnp.float32
LOW = jnp.bfloat16

beta_one = 0.9
beta_two = 0.999
learn_rate = 0.05
vector_rate = 0.4
weight_decay = 0.01
adam_eps = 1e-08
clip_at = 1.0
norm_eps = 1e-12
masked = -1e30


def mul(left, right, left_dim=1, right_dim=0):
    return lax.dot_general(
        left, right, (((left_dim,), (right_dim,)), ((), ())), preferred_element_type=F32
    )


def whole(array):
    rank = len(array.shape)
    return pl.BlockSpec(array.shape, lambda *_: (0,) * rank, pipeline_mode=pl.Buffered(1))


def params(mib=52):
    return pltpu.CompilerParams(vmem_limit_bytes=mib << 20)


def shape(dims, kind=F32):
    return jax.ShapeDtypeStruct(tuple(dims), kind)


def centred_parts(values):
    centred = values - jnp.mean(values, -1, keepdims=True)
    spread = jnp.mean(centred * centred, -1, keepdims=True)
    scale = lax.rsqrt(spread + norm_eps)
    return centred * scale, scale


def norm_back(grad, hat, scale, gain):
    scaled = grad * gain
    inner = jnp.mean(scaled * hat, -1, keepdims=True)
    return scale * (scaled - jnp.mean(scaled, -1, keepdims=True) - hat * inner)


def gelu_parts(x):
    density = jnp.exp(x * x * -0.5)
    t = 1.0 / (jnp.abs(x) * (0.3275911 * math.sqrt(0.5)) + 1.0)
    poly = 0.5 * 1.061405429 * t + 0.5 * -1.453152027
    poly = poly * t + 0.5 * 1.421413741
    poly = poly * t + 0.5 * -0.284496736
    poly = poly * t + 0.5 * 0.254829592
    tail = poly * t * density
    below = jnp.where(x < 0.0, tail, 1.0 - tail)
    return x * below, below + x * density * (1.0 / math.sqrt(2.0 * math.pi))


def head_masks():
    lane = lax.broadcasted_iota(jnp.int32, (1, LANES), 1)
    return [(lane // HEAD_DIM == h).astype(LOW) for h in range(LANES // HEAD_DIM)]


def stacked(matrix, masks):
    return jnp.concatenate([matrix * m for m in masks], 0)


def side_by_side(matrix, rows):
    return jnp.concatenate([matrix[:rows], matrix[rows:]], 1)


def adam_math(weight, first, second, grad, factor, with_decay):
    clipped = grad * factor
    first_new = beta_one * first + (1.0 - beta_one) * clipped
    second_new = beta_two * second + (1.0 - beta_two) * clipped * clipped
    first_hat = first_new / (1.0 - beta_one**STEP)
    second_hat = second_new / (1.0 - beta_two**STEP)
    update = first_hat / (jnp.sqrt(second_hat) + adam_eps)
    if with_decay:
        return first_new, second_new, weight - learn_rate * (update + weight_decay * weight)
    return first_new, second_new, weight - vector_rate * update


def pairs(size, bit):
    return [(i, i ^ bit) for i in range(size)]


class Plane:
    def __init__(self, mesh):
        self.heads = mesh.shape["head"]
        self.batch = mesh.shape["batch"]
        self.rep = mesh.shape["rep"]

    def core(self, value):
        return lax.ppermute(value, "batch", pairs(self.batch, 1))

    def side(self, value):
        return lax.ppermute(value, "batch", pairs(self.batch, 2))

    def other(self, value):
        return lax.ppermute(value, "rep", pairs(self.rep, 1))

    def corner(self, value):
        return lax.ppermute(value, ("batch", "rep"), pairs(self.batch * self.rep, 2 * self.rep + 1))

    def along(self, value, bit):
        return lax.ppermute(value, "head", pairs(self.heads, bit))

    def spread(self, block):
        half = block.shape[0] // 2
        from_side, from_other = self.side(block), self.other(block)
        corner = (self.other(from_side[:half]), self.side(from_other[half:]))
        near = (block, from_side, from_other) + corner
        return near[1:] + tuple(self.core(v) for v in near)

    def total(self, keep, send, quarter):
        both = keep + self.core(send)
        rows = both.shape[0] // 4

        def part(bits):
            return lax.dynamic_slice_in_dim(both, (quarter ^ bits) * rows, rows, 0)

        own = part(0) + self.side(part(2)) + self.other(part(1)) + self.corner(part(3))
        near = (own, self.other(own), self.side(own), self.corner(own))
        return near + tuple(self.core(v) for v in near)


def pack_kernel(meta, qkv, out, bias, up, down, a_send, b_send):
    rows = qkv.shape[1]
    width = out.shape[1] // LANES
    for j in range(3):
        a_send[j * rows : (j + 1) * rows, :] = qkv[j]
    base = 3 * rows
    few = out.shape[0]
    for b in range(width):
        a_send[base + b * few : base + (b + 1) * few, :] = out[:, b * LANES : (b + 1) * LANES]
    base += width * few
    a_send[base : base + bias.shape[0], :] = bias[...]
    a_send[base + bias.shape[0] :, :] = jnp.zeros((a_send.shape[0] - base - bias.shape[0], LANES), F32)
    b_send[: up.shape[0], :] = up[...]
    base = up.shape[0]
    few = down.shape[0]
    for b in range(width):
        b_send[base + b * few : base + (b + 1) * few, :] = down[:, b * LANES : (b + 1) * LANES]


def pack(meta, qkv, out, bias, up, down, places):
    width = out.shape[1]
    a_rows = 4 * width // places + 8
    b_rows = (up.shape[0] + down.shape[0] * width // LANES) // places
    grid = pltpu.PrefetchScalarGridSpec(
        num_scalar_prefetch=1,
        grid=(1,),
        in_specs=[
            pl.BlockSpec((3, width // places, LANES), lambda i, m: (0, m[1], 0)),
            pl.BlockSpec((LANES // places, width), lambda i, m: (m[1], 0)),
            whole(bias),
            pl.BlockSpec((up.shape[0] // places, LANES), lambda i, m: (m[1], 0)),
            pl.BlockSpec((down.shape[0] // places, width), lambda i, m: (m[1], 0)),
        ],
        out_specs=[
            pl.BlockSpec((a_rows, LANES), lambda i, m: (0, 0)),
            pl.BlockSpec((b_rows, LANES), lambda i, m: (0, 0)),
        ],
    )
    return pl.pallas_call(
        pack_kernel,
        grid_spec=grid,
        out_shape=[shape((a_rows, LANES)), shape((b_rows, LANES))],
        compiler_params=params(),
        name="pack",
    )(meta, qkv, out, bias, up, down)


def gathered(meta, refs, first_refs):
    here, place = meta[0], meta[1]
    side, other, corner_top, corner_end = refs[:4]
    far = refs[4:]
    groups = [
        (0, None, None),
        (4, side, None),
        (1, other, None),
        (5, corner_top, corner_end),
        (2, far[0], None),
        (6, far[1], None),
        (3, far[2], None),
        (7, far[3], far[4]),
    ]
    for bits, top, end in groups:
        for r in range(1, len(first_refs) + 1):

            def take(row, count, stride=1, top=top, end=end, r=r, bits=bits):
                def read(ref, start):
                    return ref[pl.ds(start, count, stride=stride), :] if stride > 1 else ref[start : start + count, :]

                if bits == 0:
                    return read(first_refs[r - 1], row)
                share = top.shape[0] // (len(first_refs) if end is None else 1)
                if end is None:
                    return read(top, (r - 1) * share + row)
                total = top.shape[0] + end.shape[0]
                start = (r - 1) * (total // len(first_refs)) + row
                if start < top.shape[0]:
                    return read(top, start)
                return read(end, start - top.shape[0])

            yield place ^ bits, here ^ r, take


def at(start, size):
    return pl.ds(pl.multiple_of(start, size), size)


def attention_forward(count, given, meta, lengths, *refs):
    tokens, norm = refs[0], refs[1]
    step = pl.program_id(0)
    if given:
        wqkv, wout, bias = refs[2:5]
        qkv_out, prob_out, context_out, pre_out = refs[5:]
    else:
        own_qkv, own_out, own_bias = refs[2:5]
        first_refs = refs[5 : 5 + count]
        moved = refs[5 + count : 14 + count]
        qkv_out, prob_out, context_out, pre_out, wqkv, wout, bias = refs[14 + count :]
    width = norm.shape[1]

    if not given:

        @pl.when(step == 0)
        def unpack():
            here = meta[0]
            for j in range(3):
                wqkv[here, :, j * LANES : (j + 1) * LANES] = own_qkv[j].astype(LOW)
            wout[at(here * LANES, LANES), :] = own_out[...].astype(LOW)
            bias[here, : own_bias.shape[0], :] = own_bias[...]
            for r in range(1, count + 1):
                piece = first_refs[r - 1]
                bias[here ^ r] = piece[piece.shape[0] - 8 :, :]
            places = 8
            rows = width // places
            few = LANES // places
            for place, shard, take in gathered(meta, moved, first_refs):
                for j in range(3):
                    wqkv[shard, at(place * rows, rows), j * LANES : (j + 1) * LANES] = take(j * rows, rows).astype(LOW)
                for b in range(width // LANES):
                    wout[at(shard * LANES + place * few, few), b * LANES : (b + 1) * LANES] = take(
                        3 * rows + b * few, few
                    ).astype(LOW)

    rows_in = tokens[...]
    groups = wqkv.shape[0]
    masks = head_masks()
    seq_len = LANES
    per_step = rows_in.shape[0] // seq_len
    heads = len(masks)
    col = lax.broadcasted_iota(jnp.int32, (heads * seq_len, seq_len), 1)
    for g in range(groups):
        projected = mul(rows_in, wqkv[g])
        query = (projected[:, :LANES] + bias[g, 0:1, :]).astype(LOW)
        key = projected[:, LANES : 2 * LANES].astype(LOW)
        value = (projected[:, 2 * LANES :] + bias[g, 1:2, :]).astype(LOW)
        qkv_out[g, :, :LANES] = query
        qkv_out[g, :, LANES : 2 * LANES] = key
        qkv_out[g, :, 2 * LANES :] = value
        for t in range(per_step):
            part = slice(t * seq_len, (t + 1) * seq_len)
            scores = mul(stacked(query[part], masks), key[part], 1, 1) * (1.0 / math.sqrt(HEAD_DIM))
            scores = jnp.where(col < lengths[step * per_step + t], scores, masked)
            exponent = jnp.exp(scores - jnp.max(scores, -1, keepdims=True))
            prob = exponent * (1.0 / jnp.sum(exponent, -1, keepdims=True))
            prob_out[g, t] = prob
            low_prob = side_by_side(prob.astype(LOW), seq_len)
            context_out[part, g * LANES : (g + 1) * LANES] = mul(low_prob, stacked(value[part], masks)).astype(LOW)
    attn = mul(context_out[...], wout[...])
    pre_out[...] = rows_in.astype(F32) + attn + norm[0:1, :]


def run_attention_forward(meta, lengths, tokens, norm, weights, first, moved, given):
    rows, width = tokens.shape
    groups = width // LANES
    steps = rows // BLOCK
    seqs = BLOCK // LANES
    heads = LANES // HEAD_DIM
    args = (tokens, norm) + tuple(weights) + tuple(first) + tuple(moved)
    in_specs = [pl.BlockSpec((BLOCK, width), lambda i, *_: (i, 0))] + [whole(a) for a in args[1:]]
    out_shape = [
        shape((groups, rows, 3 * LANES), LOW),
        shape((groups, rows // LANES, heads * LANES, LANES)),
        shape((rows, width), LOW),
        shape((rows, width)),
    ]
    out_specs = [
        pl.BlockSpec((groups, BLOCK, 3 * LANES), lambda i, *_: (0, i, 0)),
        pl.BlockSpec((groups, seqs, heads * LANES, LANES), lambda i, *_: (0, i, 0, 0)),
        pl.BlockSpec((BLOCK, width), lambda i, *_: (i, 0)),
        pl.BlockSpec((BLOCK, width), lambda i, *_: (i, 0)),
    ]
    scratch = []
    if not given:
        extra = [shape((groups, width, 3 * LANES), LOW), shape((width, width), LOW)]
        out_shape += extra
        out_specs += [whole(e) for e in extra]
        scratch = [pltpu.VMEM((groups, 8, LANES), F32)]
    flops = 2 * rows * width * 4 * width + 4 * rows * LANES * width * 2
    return pl.pallas_call(
        functools.partial(attention_forward, len(first), given),
        grid_spec=pltpu.PrefetchScalarGridSpec(
            num_scalar_prefetch=2,
            grid=(steps,),
            in_specs=in_specs,
            out_specs=out_specs,
            scratch_shapes=scratch,
        ),
        out_shape=out_shape,
        compiler_params=params(),
        cost_estimate=pl.CostEstimate(flops=flops, bytes_accessed=16 << 20, transcendentals=0),
        name="attention_forward",
    )(meta, lengths, *args)


def feed_kernel(count, given, meta, labels, tasks, *refs):
    pre_one_ref, out_grad_ref, norm, classes = refs[:4]
    step = pl.program_id(0)
    last = pl.num_programs(0) - 1
    if given:
        wup, wdown, bias = refs[4:7]
        output_ref, back_ref, norm_grad, class_grad, bias_grad, up_grad, down_grad = refs[7:14]
        act_keep, slope_keep, grad_keep = refs[14:]
    else:
        own_up, own_down, own_bias = refs[4:7]
        bias_refs = refs[7 : 7 + count]
        first_refs = refs[7 + count : 7 + 2 * count]
        moved = refs[7 + 2 * count : 16 + 2 * count]
        output_ref, back_ref, norm_grad, class_grad, bias_grad, keep, send = refs[16 + 2 * count : 23 + 2 * count]
        act_keep, slope_keep, grad_keep, wup, wdown, bias, up_grad, down_grad = refs[23 + 2 * count :]
    width = norm.shape[1]
    here = meta[0]

    @pl.when(step == 0)
    def start():
        norm_grad[...] = jnp.zeros_like(norm_grad)
        class_grad[...] = jnp.zeros_like(class_grad)
        bias_grad[...] = jnp.zeros_like(bias_grad)
        up_grad[...] = jnp.zeros_like(up_grad)
        down_grad[...] = jnp.zeros_like(down_grad)

    if not given:

        @pl.when(step == 0)
        def unpack():
            for r in range(4):
                wup[here, :, r * LANES : (r + 1) * LANES] = own_up[pl.ds(r, width, stride=4), :].astype(LOW)
                bias[here, 0:1, r * LANES : (r + 1) * LANES] = own_bias[2 + r : 3 + r, :]
            wdown[here] = own_down[...].astype(LOW)
            for j in range(1, count + 1):
                piece = bias_refs[j - 1]
                base = piece.shape[0] - 6
                for r in range(4):
                    bias[here ^ j, 0:1, r * LANES : (r + 1) * LANES] = piece[base + r : base + r + 1, :]
            rows = width // 8
            for place, shard, take in gathered(meta, moved, first_refs):
                for r in range(4):
                    wup[shard, at(place * rows, rows), r * LANES : (r + 1) * LANES] = take(r, rows, 4).astype(LOW)
                for b in range(width // LANES):
                    wdown[shard, at(place * rows, rows), b * LANES : (b + 1) * LANES] = take(
                        4 * rows + b * rows, rows
                    ).astype(LOW)

    shards = wup.shape[0]
    hat_one, scale_one = centred_parts(pre_one_ref[...])
    hidden = hat_one * norm[1:2, :] + norm[2:3, :]
    low_hidden = hidden.astype(LOW)
    ffn = None
    for s in range(shards):
        act, slope = gelu_parts(mul(low_hidden, wup[s]) + bias[s, 0:1, :])
        low_act = act.astype(LOW)
        act_keep[s] = low_act
        slope_keep[s] = slope
        term = mul(low_act, wdown[s])
        ffn = term if ffn is None else ffn + term
    hat_two, scale_two = centred_parts(hidden + ffn + norm[3:4, :])
    output = hat_two * norm[4:5, :] + norm[5:6, :]
    output_ref[...] = output

    grad = out_grad_ref[...]
    per_step = grad.shape[0] // LANES
    row = lax.broadcasted_iota(jnp.int32, grad.shape, 0)
    class_row = lax.broadcasted_iota(jnp.int32, (classes.shape[1], 1), 0)
    for t in range(per_step):
        task = tasks[step * per_step + t]
        table = classes[task]
        first_row = output[t * LANES : t * LANES + 1, :]
        logits = jnp.sum(table * first_row, -1, keepdims=True)
        logit_exp = jnp.exp(logits - jnp.max(logits, 0, keepdims=True))
        class_prob = logit_exp / jnp.sum(logit_exp, 0, keepdims=True)
        logit_grad = class_prob - (class_row == labels[step * per_step + t]).astype(F32)
        class_grad[task] += logit_grad * first_row
        grad = jnp.where(row == t * LANES, grad + jnp.sum(logit_grad * table, 0, keepdims=True), grad)

    norm_grad[4:5, :] += jnp.sum(grad * hat_two, 0, keepdims=True)
    norm_grad[5:6, :] += jnp.sum(grad, 0, keepdims=True)
    back_two = norm_back(grad, hat_two, scale_two, norm[4:5, :])
    norm_grad[3:4, :] += jnp.sum(back_two, 0, keepdims=True)
    low_back = back_two.astype(LOW)
    back_hidden = back_two
    for s in range(shards):
        up_back = (mul(low_back, wdown[s], 1, 1) * slope_keep[s]).astype(LOW)
        grad_keep[s] = up_back
        back_hidden = back_hidden + mul(up_back, wup[s], 1, 1)
    own_back = grad_keep[here]
    down_grad[...] += mul(act_keep[here], low_back, 0, 0)
    up_grad[...] += mul(low_hidden, own_back, 0, 0)
    bias_grad[0:1, :] += jnp.sum(own_back.astype(F32), 0, keepdims=True)

    norm_grad[1:2, :] += jnp.sum(back_hidden * hat_one, 0, keepdims=True)
    norm_grad[2:3, :] += jnp.sum(back_hidden, 0, keepdims=True)
    back_one = norm_back(back_hidden, hat_one, scale_one, norm[1:2, :])
    norm_grad[0:1, :] += jnp.sum(back_one, 0, keepdims=True)
    back_ref[...] = back_one

    if not given:

        def give_up(ref):
            for r in range(4):
                ref[pl.ds(r, width, stride=4), :] = up_grad[:, r * LANES : (r + 1) * LANES]

        def give_down(ref):
            for b in range(width // LANES):
                ref[b * 4 * LANES : (b + 1) * 4 * LANES, :] = down_grad[:, b * LANES : (b + 1) * LANES]

        @pl.when((step == last) & (meta[2] == 0))
        def give_first():
            give_up(keep)
            give_down(send)

        @pl.when((step == last) & (meta[2] == 1))
        def give_second():
            give_up(send)
            give_down(keep)


def run_feed(meta, labels, tasks, pre_one, out_grad, norm, classes, weights, biases, first, moved, given):
    rows, width = pre_one.shape
    steps = rows // BLOCK
    if given:
        shards, _, hidden = weights[0].shape
    else:
        shards, hidden = len(first) + 1, 4 * LANES
    args = (pre_one, out_grad, norm, classes) + tuple(weights) + tuple(biases) + tuple(first) + tuple(moved)
    by_rows = pl.BlockSpec((BLOCK, width), lambda i, *_: (i, 0))
    in_specs = [by_rows, by_rows] + [whole(a) for a in args[2:]]
    fixed = [shape((8, width)), shape(classes.shape), shape((8, hidden))]
    scratch = [
        pltpu.VMEM((shards, BLOCK, hidden), LOW),
        pltpu.VMEM((shards, BLOCK, hidden), F32),
        pltpu.VMEM((shards, BLOCK, hidden), LOW),
    ]
    if given:
        fixed += [shape((width, hidden)), shape((hidden, width))]
    else:
        half = hidden * width // LANES
        fixed += [shape((half, LANES)), shape((half, LANES))]
        scratch += [
            pltpu.VMEM((shards, width, hidden), LOW),
            pltpu.VMEM((shards, hidden, width), LOW),
            pltpu.VMEM((shards, 8, hidden), F32),
            pltpu.VMEM((width, hidden), F32),
            pltpu.VMEM((hidden, width), F32),
        ]
    flops = 2 * rows * width * hidden * (4 * shards + 2)
    return pl.pallas_call(
        functools.partial(feed_kernel, len(first), given),
        grid_spec=pltpu.PrefetchScalarGridSpec(
            num_scalar_prefetch=3,
            grid=(steps,),
            in_specs=in_specs,
            out_specs=[by_rows, by_rows] + [whole(f) for f in fixed],
            scratch_shapes=scratch,
        ),
        out_shape=[shape((rows, width)), shape((rows, width))] + fixed,
        compiler_params=params(),
        cost_estimate=pl.CostEstimate(flops=4 * flops, bytes_accessed=20 << 20, transcendentals=0),
        name="feed_both",
    )(meta, labels, tasks, *args)


def pair_back(qkv, prob, context_back, masks):
    query, key, value = (qkv[:, j * LANES : (j + 1) * LANES] for j in range(3))
    seq_len = query.shape[0]
    wide_back = stacked(context_back, masks)
    prob_back = mul(wide_back, value, 1, 1)
    value_back = mul(prob.astype(LOW), wide_back, 0, 0).astype(LOW)
    inner = jnp.sum(prob * prob_back, -1, keepdims=True)
    raw = (prob * (prob_back - inner) * (1.0 / math.sqrt(HEAD_DIM))).astype(LOW)
    query_back = mul(side_by_side(raw, seq_len), stacked(key, masks)).astype(LOW)
    key_back = mul(raw, stacked(query, masks), 0, 0).astype(LOW)
    return query_back, key_back, value_back


def group_back(low_back, qkv_ref, prob_ref, wout_rows, masks, store):
    context_back = mul(low_back, wout_rows, 1, 1).astype(LOW)
    for t in range(low_back.shape[0] // LANES):
        part = slice(t * LANES, (t + 1) * LANES)
        for j, grad in enumerate(pair_back(qkv_ref[part, :], prob_ref[t], context_back[part], masks)):
            store(part, j, grad)


def own_kernel(given, meta, back_ref, tokens, qkv, prob, context, wout, *refs):
    if given:
        grads, qkv_grad, out_grad, split_grad = refs
    else:
        norm_grad, class_grad, up_bias, grads, keep, send, qkv_grad, out_grad, split_grad, packed = refs
    step = pl.program_id(0)
    last = pl.num_programs(0) - 1

    @pl.when(step == 0)
    def start():
        qkv_grad[...] = jnp.zeros_like(qkv_grad)
        out_grad[...] = jnp.zeros_like(out_grad)
        split_grad[...] = jnp.zeros_like(split_grad)

    masks = head_masks()
    low_back = back_ref[...].astype(LOW)

    def store(part, j, grad):
        grads[part, j * LANES : (j + 1) * LANES] = grad

    group_back(low_back, qkv.at[0], prob.at[0], wout[...], masks, store)
    out_grad[...] += mul(context[...], low_back, 0, 0)
    both = grads[...]
    qkv_grad[...] += mul(tokens[...], both, 0, 0)
    split_grad[0:1, :] += jnp.sum(both[:, :LANES].astype(F32), 0, keepdims=True)
    split_grad[1:2, :] += jnp.sum(both[:, 2 * LANES :].astype(F32), 0, keepdims=True)

    if not given:
        width = back_ref.shape[1]
        blocks = width // LANES

        @pl.when(step == last)
        def fill():
            for j in range(3):
                packed[j * width : (j + 1) * width, :] = qkv_grad[:, j * LANES : (j + 1) * LANES]
            base = 3 * width
            for b in range(blocks):
                packed[base + b * LANES : base + (b + 1) * LANES, :] = out_grad[:, b * LANES : (b + 1) * LANES]
            base += width
            packed[base:, :] = jnp.zeros((packed.shape[0] - base, LANES), F32)
            packed[base : base + 2, :] = split_grad[0:2, :]
            for r in range(4):
                packed[base + 2 + r : base + 3 + r, :] = up_bias[0:1, r * LANES : (r + 1) * LANES]
            base += 8
            for b in range(blocks):
                packed[base + 8 * b : base + 8 * b + 6, :] = norm_grad[0:6, b * LANES : (b + 1) * LANES]
            base += 8 * blocks
            tasks, kinds, _ = class_grad.shape
            each = small_rows(tasks, kinds)
            for b in range(blocks):
                for t in range(tasks):
                    row = base + each * b + kinds * t
                    packed[row : row + kinds, :] = class_grad[t, :, b * LANES : (b + 1) * LANES]

        half = keep.shape[0]

        @pl.when((step == last) & (meta[2] == 0))
        def give_first():
            keep[...] = packed[:half, :]
            send[...] = packed[half:, :]

        @pl.when((step == last) & (meta[2] == 1))
        def give_second():
            keep[...] = packed[half:, :]
            send[...] = packed[:half, :]


def small_rows(tasks, kinds):
    return -(-tasks * kinds // 8) * 8


def packed_rows(width, tasks, kinds):
    blocks = width // LANES
    rows = 4 * width + 8 + 8 * blocks + blocks * small_rows(tasks, kinds)
    return -(-rows // 64) * 64


def run_own(meta, back, tokens, qkv, prob, context, wout, smalls, given):
    rows, width = back.shape
    steps = rows // BLOCK
    seqs = BLOCK // LANES
    heads = LANES // HEAD_DIM
    by_rows = pl.BlockSpec((BLOCK, width), lambda i, m: (i, 0))
    in_specs = [
        by_rows,
        by_rows,
        pl.BlockSpec((1, BLOCK, 3 * LANES), lambda i, m: (m[3], i, 0)),
        pl.BlockSpec((1, seqs, heads * LANES, LANES), lambda i, m: (m[3], i, 0, 0)),
        pl.BlockSpec((BLOCK, LANES), lambda i, m: (i, m[3])),
        pl.BlockSpec((LANES, width), lambda i, m: (m[3], 0)),
    ] + [whole(s) for s in smalls]
    out_shape = [shape((rows, 3 * LANES), LOW)]
    out_specs = [pl.BlockSpec((BLOCK, 3 * LANES), lambda i, m: (i, 0))]
    sums = [shape((width, 3 * LANES)), shape((LANES, width)), shape((8, LANES))]
    scratch = []
    if given:
        fixed = sums
    else:
        count = packed_rows(width, *smalls[1].shape[:2])
        fixed = [shape((count // 2, LANES))] * 2
        scratch = [pltpu.VMEM(s.shape, F32) for s in sums] + [pltpu.VMEM((count, LANES), F32)]
    return pl.pallas_call(
        functools.partial(own_kernel, given),
        grid_spec=pltpu.PrefetchScalarGridSpec(
            num_scalar_prefetch=1,
            grid=(steps,),
            in_specs=in_specs,
            out_specs=out_specs + [whole(f) for f in fixed],
            scratch_shapes=scratch,
        ),
        out_shape=out_shape + fixed,
        compiler_params=params(),
        cost_estimate=pl.CostEstimate(flops=4 << 30, bytes_accessed=8 << 20, transcendentals=0),
        name="attention_own",
    )(meta, back, tokens, qkv, prob, context, wout, *smalls)


def rest_kernel(meta, back_ref, qkv, prob, wout, wqkv, own, input_grad, grads):
    group = meta[3]
    groups = qkv.shape[0]
    masks = head_masks()
    back = back_ref[...]
    low_back = back.astype(LOW)
    grads[group] = own[...]
    for r in range(1, groups):
        g = group ^ r

        def store(part, j, grad, g=g):
            grads[g, part, j * LANES : (j + 1) * LANES] = grad

        group_back(low_back, qkv.at[g], prob.at[g], wout[at(g * LANES, LANES), :], masks, store)
    total = None
    for g in range(groups):
        term = mul(grads[g], wqkv[g], 1, 1)
        total = term if total is None else total + term
    input_grad[...] = back + total


def run_rest(meta, back, qkv, prob, wout, wqkv, own):
    rows, width = back.shape
    groups = width // LANES
    seqs = BLOCK // LANES
    heads = LANES // HEAD_DIM
    by_rows = pl.BlockSpec((BLOCK, width), lambda i, m: (i, 0))
    return pl.pallas_call(
        rest_kernel,
        grid_spec=pltpu.PrefetchScalarGridSpec(
            num_scalar_prefetch=1,
            grid=(rows // BLOCK,),
            in_specs=[
                by_rows,
                pl.BlockSpec((groups, BLOCK, 3 * LANES), lambda i, m: (0, i, 0)),
                pl.BlockSpec((groups, seqs, heads * LANES, LANES), lambda i, m: (0, i, 0, 0)),
                whole(wout),
                whole(wqkv),
                pl.BlockSpec((BLOCK, 3 * LANES), lambda i, m: (i, 0)),
            ],
            out_specs=by_rows,
            scratch_shapes=[pltpu.VMEM((groups, BLOCK, 3 * LANES), LOW)],
        ),
        out_shape=shape((rows, width)),
        compiler_params=params(),
        cost_estimate=pl.CostEstimate(flops=8 << 30, bytes_accessed=12 << 20, transcendentals=0),
        name="attention_rest",
    )(meta, back, qkv, prob, wout, wqkv, own)


def collect_kernel(split_rows, meta, *refs):
    parts, full, squares = refs[:8], refs[8], refs[9]
    rows = parts[0].shape[0]
    for half in range(2):
        for bits in range(4):
            place = (meta[2] ^ half) * 4 + (meta[4] ^ bits)
            full[pl.ds(pl.multiple_of(place * rows, 8), rows), :] = parts[half * 4 + bits][...]
    squares[...] = jnp.zeros_like(squares)
    head = full[:split_rows, :]
    squares[0:1, :] = jnp.sum(head * head, 0, keepdims=True)
    if split_rows < full.shape[0]:
        tail = full[split_rows:, :]
        squares[1:2, :] = jnp.sum(tail * tail, 0, keepdims=True)


def collect(meta, parts, split_rows=None):
    rows = 8 * parts[0].shape[0]
    outs = [shape((rows, LANES)), shape((8, LANES))]
    return pl.pallas_call(
        functools.partial(collect_kernel, split_rows or rows),
        grid_spec=pltpu.PrefetchScalarGridSpec(
            num_scalar_prefetch=1,
            grid=(1,),
            in_specs=[whole(p) for p in parts],
            out_specs=[whole(o) for o in outs],
        ),
        out_shape=outs,
        compiler_params=params(),
        name="collect",
    )(meta, *parts)


def adam_kernel(count, meta, squares, *refs):
    moved = refs[:count]
    a_full, b_full = refs[count : count + 2]
    states = refs[count + 2 : count + 23]
    norm_ref = refs[count + 23]
    outs = refs[count + 24 : count + 45]
    sums = refs[count + 45]
    sums[meta[0]] = squares[...]
    for r in range(1, count + 1):
        sums[meta[0] ^ r] = moved[r - 1][...]
    total = sums[0]
    for s in range(1, count + 1):
        total = total + sums[s]
    all_squares = jnp.sum(total[0:1, :], -1, keepdims=True) + jnp.sum(squares[1:2, :], -1, keepdims=True)
    grad_norm = jnp.sqrt(all_squares)
    norm_ref[...] = grad_norm
    factor = jnp.minimum(1.0, clip_at / (grad_norm + 1e-06))
    width = states[5 * 3].shape[1]
    blocks = width // LANES

    def update(index, where, grad, with_decay):
        first, second, weight = (states[3 * index + j][where] for j in range(3))
        for j, value in enumerate(adam_math(weight, first, second, grad, factor, with_decay)):
            outs[3 * index + j][where] = value

    for j in range(3):
        update(0, (j,), a_full[j * width : (j + 1) * width, :], True)
    base = 3 * width
    for b in range(blocks):
        lanes = slice(b * LANES, (b + 1) * LANES)
        update(1, (slice(None), lanes), a_full[base + b * LANES : base + (b + 1) * LANES, :], True)
    base += width
    update(4, (slice(None), slice(None)), a_full[base : base + 6, :], False)
    base += 8
    for b in range(blocks):
        lanes = slice(b * LANES, (b + 1) * LANES)
        update(5, (slice(None), lanes), a_full[base + 8 * b : base + 8 * b + 6, :], False)
    base += 8 * blocks
    tasks, kinds, _ = states[6 * 3].shape
    each = small_rows(tasks, kinds)
    for b in range(blocks):
        lanes = slice(b * LANES, (b + 1) * LANES)
        for t in range(tasks):
            row = base + each * b + kinds * t
            update(6, (t, slice(None), lanes), a_full[row : row + kinds, :], True)
    rows = 4 * width
    update(2, (slice(None), slice(None)), b_full[:rows, :], True)
    for b in range(blocks):
        lanes = slice(b * LANES, (b + 1) * LANES)
        update(3, (slice(None), lanes), b_full[rows + b * 4 * LANES : rows + (b + 1) * 4 * LANES, :], True)


def run_adam(meta, squares, moved, a_full, b_full, states):
    outs = [shape((1, 1))] + [shape(s.shape) for s in states]
    args = (squares,) + tuple(moved) + (a_full, b_full) + tuple(states)
    return pl.pallas_call(
        functools.partial(adam_kernel, len(moved)),
        grid_spec=pltpu.PrefetchScalarGridSpec(
            num_scalar_prefetch=1,
            grid=(1,),
            in_specs=[whole(a) for a in args],
            out_specs=[whole(o) for o in outs],
            scratch_shapes=[pltpu.VMEM((len(moved) + 1, 8, LANES), F32)],
        ),
        out_shape=outs,
        compiler_params=params(),
        name="adam",
    )(meta, *args)


def shares(mesh, *args):
    fast = (
        mesh.shape["batch"] == 4
        and mesh.shape["rep"] == 2
        and args[5].shape[2] == LANES
        and mesh.shape["head"] * LANES == args[0].shape[1]
    )
    return (by_permutes if fast else by_gathers)(mesh, *args)


def by_permutes(
    mesh,
    tokens_in,
    out_grad,
    lengths,
    labels,
    task_id,
    qkv_weight,
    qkv_first,
    qkv_second,
    out_weight,
    out_first,
    out_second,
    up_weight,
    up_first,
    up_second,
    down_weight,
    down_first,
    down_second,
    split_bias,
    split_first,
    split_second,
    norm_params,
    norm_first,
    norm_second,
    class_weight,
    class_first,
    class_second,
):
    plane = Plane(mesh)
    width = tokens_in.shape[1]
    here = lax.axis_index("head")
    batch = lax.axis_index("batch")
    rep = lax.axis_index("rep")
    quarter = (batch // 2) * 2 + rep
    meta = jnp.stack([here, batch * plane.rep + rep, batch % 2, here, quarter]).astype(jnp.int32)

    def flat_up(value):
        return value.reshape(-1, LANES)

    def flat_down(value):
        return value.reshape(-1, width)

    def flat_class(value):
        return jnp.transpose(value, (0, 2, 1))

    up_flat, down_flat, classes = flat_up(up_weight), flat_down(down_weight), flat_class(class_weight)
    a_send, b_send = pack(meta, qkv_weight, out_weight, split_bias, up_flat, down_flat, plane.batch * plane.rep)
    turns = range(1, plane.heads)
    a_first = [plane.along(a_send, r) for r in turns]
    b_first = [plane.along(b_send, r) for r in turns]
    a_moved = plane.spread(jnp.concatenate([v[:-8] for v in a_first], 0))
    b_moved = plane.spread(jnp.concatenate(b_first, 0))

    qkv, prob, context, pre_one, wqkv, wout = run_attention_forward(
        meta, lengths, tokens_in, norm_params, (qkv_weight, out_weight, split_bias), a_first, a_moved, False
    )
    output, back_one, norm_grad, class_grad, up_bias_grad, b_keep, b_give = run_feed(
        meta,
        labels,
        task_id,
        pre_one,
        out_grad,
        norm_params,
        classes,
        (up_flat, down_flat, split_bias),
        a_first,
        b_first,
        b_moved,
        False,
    )
    own, a_keep, a_give = run_own(
        meta, back_one, tokens_in, qkv, prob, context, wout, (norm_grad, class_grad, up_bias_grad), False
    )
    input_grad = run_rest(meta, back_one, qkv, prob, wout, wqkv, own)
    b_full, b_squares = collect(meta, plane.total(b_keep, b_give, quarter))
    a_full, a_squares = collect(meta, plane.total(a_keep, a_give, quarter), 4 * width + 8)
    squares = a_squares + b_squares
    states = (
        (qkv_first, qkv_second, qkv_weight)
        + (out_first, out_second, out_weight)
        + (flat_up(up_first), flat_up(up_second), up_flat)
        + (flat_down(down_first), flat_down(down_second), down_flat)
        + (split_first, split_second, split_bias)
        + (norm_first, norm_second, norm_params)
        + (flat_class(class_first), flat_class(class_second), classes)
    )
    grad_norm, *new = run_adam(meta, squares, [plane.along(squares, r) for r in turns], a_full, b_full, states)
    new[6:9] = [v.reshape(up_weight.shape) for v in new[6:9]]
    new[9:12] = [v.reshape(down_weight.shape) for v in new[9:12]]
    new[18:21] = [jnp.transpose(v, (0, 2, 1)) for v in new[18:21]]
    return (output, input_grad, grad_norm[0, 0]) + tuple(new)


def by_gathers(
    mesh,
    tokens_in,
    out_grad,
    lengths,
    labels,
    task_id,
    qkv_weight,
    qkv_first,
    qkv_second,
    out_weight,
    out_first,
    out_second,
    up_weight,
    up_first,
    up_second,
    down_weight,
    down_first,
    down_second,
    split_bias,
    split_first,
    split_second,
    norm_params,
    norm_first,
    norm_second,
    class_weight,
    class_first,
    class_second,
):
    width = tokens_in.shape[1]
    cols = qkv_weight.shape[2]
    groups = width // LANES
    hidden = 4 * cols
    here = lax.axis_index("head")
    zero = jnp.zeros_like(here)
    meta = jnp.stack([here, zero, zero, here * cols // LANES, zero]).astype(jnp.int32)
    full_qkv = lax.all_gather(qkv_weight, "head", axis=2, tiled=True)
    full_out = lax.all_gather(out_weight, "head", axis=0, tiled=True)
    full_up = lax.all_gather(up_weight.reshape(width, hidden), "head", axis=0)
    full_down = lax.all_gather(down_weight.reshape(hidden, width), "head", axis=0)
    full_bias = lax.all_gather(split_bias, "head", axis=1, tiled=True)
    full_qkv, full_out, full_up, full_down, full_bias = lax.optimization_barrier(
        (full_qkv, full_out, full_up, full_down, full_bias)
    )
    wqkv = full_qkv.reshape(3, width, groups, LANES).transpose(2, 1, 0, 3).reshape(groups, width, 3 * LANES).astype(LOW)
    wout = full_out.astype(LOW)
    qv_bias = jnp.pad(full_bias[:2].reshape(2, groups, LANES).transpose(1, 0, 2), ((0, 0), (0, 6), (0, 0)))
    shards = width // cols
    up_bias = full_bias[2:].reshape(4, shards, cols).transpose(1, 0, 2).reshape(shards, 1, hidden)
    up_bias = jnp.pad(up_bias, ((0, 0), (0, 7), (0, 0)))
    classes = jnp.transpose(class_weight, (0, 2, 1))

    qkv, prob, context, pre_one = run_attention_forward(
        meta, lengths, tokens_in, norm_params, (wqkv, wout, qv_bias), (), (), True
    )
    output, back_one, norm_grad, class_grad, up_bias_grad, up_grad, down_grad = run_feed(
        meta,
        labels,
        task_id,
        pre_one,
        out_grad,
        norm_params,
        classes,
        (full_up.astype(LOW), full_down.astype(LOW), up_bias),
        (),
        (),
        (),
        True,
    )
    own, qkv_grad, out_w_grad, split_grad = run_own(meta, back_one, tokens_in, qkv, prob, context, wout, (), True)
    input_grad = run_rest(meta, back_one, qkv, prob, wout, wqkv, own)
    start = here * cols % LANES
    qkv_grad = qkv_grad.reshape(width, 3, LANES).transpose(1, 0, 2)
    qkv_grad = lax.dynamic_slice_in_dim(qkv_grad, start, cols, 2)
    out_w_grad = lax.dynamic_slice_in_dim(out_w_grad, start, cols, 0)
    split_grad = lax.dynamic_slice_in_dim(split_grad[:2], start, cols, 1)
    split_grad = jnp.concatenate([split_grad, up_bias_grad[0].reshape(4, cols)], 0)
    summed = lax.psum(
        (
            qkv_grad,
            out_w_grad,
            up_grad.reshape(up_weight.shape),
            down_grad.reshape(down_weight.shape),
            split_grad,
            norm_grad[:6],
            jnp.transpose(class_grad, (0, 2, 1)),
        ),
        ("batch", "rep"),
    )
    split_square = lax.psum(sum(jnp.sum(v * v) for v in summed[:5]), "head")
    grad_norm = jnp.sqrt(split_square + sum(jnp.sum(v * v) for v in summed[5:]))
    factor = jnp.minimum(1.0, clip_at / (grad_norm + 1e-06))
    states = (
        (qkv_weight, qkv_first, qkv_second, True),
        (out_weight, out_first, out_second, True),
        (up_weight, up_first, up_second, True),
        (down_weight, down_first, down_second, True),
        (split_bias, split_first, split_second, False),
        (norm_params, norm_first, norm_second, False),
        (class_weight, class_first, class_second, True),
    )
    results = ()
    for grad, (weight, first, second, decay) in zip(summed, states):
        results += adam_math(weight, first, second, grad, factor, decay)
    return (output, input_grad, grad_norm) + results


def solution(mesh):
    rows = P(("batch", "rep"), None)
    seqs = P(("batch", "rep"))
    kinds = (
        (P(None, None, "head"),) * 3
        + (P("head", None),) * 3
        + (P(None, None, "head"),) * 3
        + (P(None, "head", None),) * 3
        + (P(None, "head"),) * 3
        + (P(),) * 6
    )
    return jax.shard_map(
        functools.partial(shares, mesh),
        mesh=mesh,
        in_specs=(rows, rows, seqs, seqs, seqs) + kinds,
        out_specs=(rows, rows, P()) + kinds,
        check_vma=False,
    )
```

```python
import functools
import math

import jax
import jax.numpy as jnp
from jax import lax
from jax.experimental import pallas as pl
from jax.experimental.pallas import tpu as pltpu
from jax.sharding import PartitionSpec as P

HEAD_DIM = 64
STEP = 10
LANES = 128
BLOCK = 512

F32 = jnp.float32
LOW = jnp.bfloat16

beta_one = 0.9
beta_two = 0.999
learn_rate = 0.05
vector_rate = 0.4
weight_decay = 0.01
adam_eps = 1e-08
clip_at = 1.0
norm_eps = 1e-12
masked = -1e30


def mul(left, right, left_dim=1, right_dim=0):
    return lax.dot_general(
        left, right, (((left_dim,), (right_dim,)), ((), ())), preferred_element_type=F32
    )


def whole(array):
    rank = len(array.shape)
    return pl.BlockSpec(array.shape, lambda *_: (0,) * rank, pipeline_mode=pl.Buffered(1))


def params(mib=52):
    return pltpu.CompilerParams(vmem_limit_bytes=mib << 20)


def in_hbm(value):
    return pltpu.with_memory_space_constraint(value, pltpu.HBM)


def in_vmem(value):
    return pltpu.with_memory_space_constraint(value, pltpu.VMEM)


def shape(dims, kind=F32):
    return jax.ShapeDtypeStruct(tuple(dims), kind)


def centred_parts(values):
    centred = values - jnp.mean(values, -1, keepdims=True)
    spread = jnp.mean(centred * centred, -1, keepdims=True)
    scale = lax.rsqrt(spread + norm_eps)
    return centred * scale, scale


def norm_back(grad, hat, scale, gain):
    scaled = grad * gain
    inner = jnp.mean(scaled * hat, -1, keepdims=True)
    return scale * (scaled - jnp.mean(scaled, -1, keepdims=True) - hat * inner)


def gelu_parts(x):
    below = lax.erf(x * math.sqrt(0.5)) * 0.5 + 0.5
    density = jnp.exp2(x * x * (-0.5 * math.log2(math.e))) * (1.0 / math.sqrt(2.0 * math.pi))
    return x * below, below + x * density


def head_masks():
    lane = lax.broadcasted_iota(jnp.int32, (1, LANES), 1)
    return [(lane // HEAD_DIM == h).astype(LOW) for h in range(LANES // HEAD_DIM)]


def stacked(matrix, masks):
    return jnp.concatenate([matrix * m for m in masks], 0)


def side_by_side(matrix, rows):
    return jnp.concatenate([matrix[:rows], matrix[rows:]], 1)


def adam_math(weight, first, second, grad, factor, with_decay):
    clipped = grad * factor
    first_new = beta_one * first + (1.0 - beta_one) * clipped
    second_new = beta_two * second + (1.0 - beta_two) * clipped * clipped
    first_hat = first_new / (1.0 - beta_one**STEP)
    second_hat = second_new / (1.0 - beta_two**STEP)
    update = first_hat / (jnp.sqrt(second_hat) + adam_eps)
    if with_decay:
        return first_new, second_new, weight - learn_rate * (update + weight_decay * weight)
    return first_new, second_new, weight - vector_rate * update


def pairs(size, bit):
    return [(i, i ^ bit) for i in range(size)]


class Plane:
    def __init__(self, mesh):
        self.heads = mesh.shape["head"]
        self.batch = mesh.shape["batch"]
        self.rep = mesh.shape["rep"]

    def core(self, value):
        return lax.ppermute(value, "batch", pairs(self.batch, 1))

    def side(self, value):
        return lax.ppermute(value, "batch", pairs(self.batch, 2))

    def other(self, value):
        return lax.ppermute(value, "rep", pairs(self.rep, 1))

    def corner(self, value):
        return lax.ppermute(value, ("batch", "rep"), pairs(self.batch * self.rep, 2 * self.rep + 1))

    def along(self, value, bit):
        return lax.ppermute(value, "head", pairs(self.heads, bit))

    def round(self, block):
        return self.along(block, 1), self.along(block, 2), lax.ppermute(block, "head", [(1, 2), (2, 1)])

    def round_on(self, got):
        near, far, last = got
        return near, far, last + lax.ppermute(far, "head", [(1, 0), (2, 3)])

    def spread(self, block):
        return block, self.side(block), self.other(block)

    def corners(self, near):
        block, from_side, from_other = near
        half = block.shape[0] // 2
        return self.other(from_side[:half]), self.side(from_other[half:])

    def shared(self, near, corner):
        near = near + corner
        return near[1:] + tuple(self.core(v) for v in near)

    def quarters(self, keep, send, quarter, *others):
        both = keep + after(self.core(send), *others)
        rows = both.shape[0] // 4
        return tuple(lax.dynamic_slice_in_dim(both, (quarter ^ bits) * rows, rows, 0) for bits in range(4))

    def scatter(self, parts, *others):
        moved = (self.side(parts[2]), self.other(parts[1]), self.corner(parts[3]))
        moved = after(moved, *others)
        return parts[0] + moved[0] + moved[1] + moved[2]

    def rejoin(self, own):
        return self.core(own), (self.other(own), self.side(own), self.corner(own))

    def rejoin_on(self, own, crossed, near):
        return (own,) + near + (crossed,) + tuple(self.core(v) for v in near)


def after(value, *others):
    return lax.optimization_barrier((value, others))[0]


def pack_kernel(meta, qkv, out, bias, up, down, a_send, b_send, done):
    place = meta[1]
    places = 8
    rows = qkv.shape[1] // places
    few = out.shape[0] // places
    moves = [(qkv.at[j, at(place * rows, rows), :], a_send.at[j * rows : (j + 1) * rows, :]) for j in range(3)]
    base = 3 * rows
    for b in range(out.shape[1] // LANES):
        lanes = slice(b * LANES, (b + 1) * LANES)
        moves.append((out.at[at(place * few, few), lanes], a_send.at[base + b * few : base + (b + 1) * few, :]))
    moves.append((bias, a_send.at[a_send.shape[0] - 8 : a_send.shape[0] - 2, :]))
    base = up.shape[0] // places
    moves.append((up.at[at(place * base, base), :], b_send.at[:base, :]))
    few = down.shape[0] // places
    for b in range(down.shape[1] // LANES):
        lanes = slice(b * LANES, (b + 1) * LANES)
        moves.append((down.at[at(place * few, few), lanes], b_send.at[base + b * few : base + (b + 1) * few, :]))
    copies = [pltpu.make_async_copy(source, target, done.at[n]) for n, (source, target) in enumerate(moves)]
    for copy in copies:
        copy.start()
    for copy in copies:
        copy.wait()


def pack(meta, qkv, out, bias, up, down):
    places = 8
    width = out.shape[1]
    outs = [
        shape((4 * width // places + 8, LANES)),
        shape(((up.shape[0] + down.shape[0] * width // LANES) // places, LANES)),
    ]
    held = pl.BlockSpec(memory_space=pltpu.HBM)
    return pl.pallas_call(
        pack_kernel,
        grid_spec=pltpu.PrefetchScalarGridSpec(
            num_scalar_prefetch=1,
            grid=(1,),
            in_specs=[held] * 5,
            out_specs=[held] * 2,
            scratch_shapes=[pltpu.SemaphoreType.DMA((5 + 2 * (width // LANES),))],
        ),
        out_shape=outs,
        compiler_params=params(),
        name="pack",
    )(meta, *(in_hbm(v) for v in (qkv, out, bias, up, down)))


def gathered(meta, refs, first_refs):
    here, place = meta[0], meta[1]
    side, other, corner_top, corner_end = refs[:4]
    far = refs[4:]
    groups = [
        (0, None, None),
        (4, side, None),
        (1, other, None),
        (5, corner_top, corner_end),
        (2, far[0], None),
        (6, far[1], None),
        (3, far[2], None),
        (7, far[3], far[4]),
    ]
    for bits, top, end in groups:
        for r in range(1, len(first_refs) + 1):

            def take(row, count, stride=1, top=top, end=end, r=r, bits=bits):
                def read(ref, start):
                    return ref[pl.ds(start, count, stride=stride), :] if stride > 1 else ref[start : start + count, :]

                if bits == 0:
                    return read(first_refs[r - 1], row)
                share = top.shape[0] // (len(first_refs) if end is None else 1)
                if end is None:
                    return read(top, (r - 1) * share + row)
                total = top.shape[0] + end.shape[0]
                start = (r - 1) * (total // len(first_refs)) + row
                if start < top.shape[0]:
                    return read(top, start)
                return read(end, start - top.shape[0])

            yield place ^ bits, here ^ r, take


def at(start, size):
    return pl.ds(pl.multiple_of(start, size), size)


def attention_forward(count, given, meta, lengths, *refs):
    tokens, norm = refs[0], refs[1]
    step = pl.program_id(0)
    if given:
        wqkv, wout, bias = refs[2:5]
        qkv_out, prob_out, context_out, pre_out = refs[5:]
    else:
        own_qkv, own_out, own_bias = refs[2:5]
        first_refs = refs[5 : 5 + count]
        moved = refs[5 + count : 14 + count]
        qkv_out, prob_out, context_out, pre_out, wqkv, wout, bias = refs[14 + count :]
    width = norm.shape[1]

    if not given:

        @pl.when(step == 0)
        def unpack():
            here = meta[0]
            for j in range(3):
                wqkv[here, :, j * LANES : (j + 1) * LANES] = own_qkv[j].astype(LOW)
            wout[at(here * LANES, LANES), :] = own_out[...].astype(LOW)
            bias[here, : own_bias.shape[0], :] = own_bias[...]
            for r in range(1, count + 1):
                piece = first_refs[r - 1]
                bias[here ^ r] = piece[piece.shape[0] - 8 :, :]
            places = 8
            rows = width // places
            few = LANES // places
            for place, shard, take in gathered(meta, moved, first_refs):
                for j in range(3):
                    wqkv[shard, at(place * rows, rows), j * LANES : (j + 1) * LANES] = take(j * rows, rows).astype(LOW)
                for b in range(width // LANES):
                    wout[at(shard * LANES + place * few, few), b * LANES : (b + 1) * LANES] = take(
                        3 * rows + b * few, few
                    ).astype(LOW)

    rows_in = tokens[...]
    groups = wqkv.shape[0]
    masks = head_masks()
    seq_len = LANES
    per_step = rows_in.shape[0] // seq_len
    heads = len(masks)
    col = lax.broadcasted_iota(jnp.int32, (heads * seq_len, seq_len), 1)
    for g in range(groups):
        projected = mul(rows_in, wqkv[g])
        query = (projected[:, :LANES] + bias[g, 0:1, :]).astype(LOW)
        key = projected[:, LANES : 2 * LANES].astype(LOW)
        value = (projected[:, 2 * LANES :] + bias[g, 1:2, :]).astype(LOW)
        qkv_out[g, :, :LANES] = query
        qkv_out[g, :, LANES : 2 * LANES] = key
        qkv_out[g, :, 2 * LANES :] = value
        for t in range(per_step):
            part = slice(t * seq_len, (t + 1) * seq_len)
            scores = mul(stacked(query[part], masks), key[part], 1, 1) * (1.0 / math.sqrt(HEAD_DIM))
            scores = jnp.where(col < lengths[step * per_step + t], scores, masked)
            exponent = jnp.exp(scores - jnp.max(scores, -1, keepdims=True))
            prob = exponent * (1.0 / jnp.sum(exponent, -1, keepdims=True))
            prob_out[g, t] = prob
            low_prob = side_by_side(prob.astype(LOW), seq_len)
            context_out[part, g * LANES : (g + 1) * LANES] = mul(low_prob, stacked(value[part], masks)).astype(LOW)
    attn = mul(context_out[...], wout[...])
    pre_out[...] = rows_in.astype(F32) + attn + norm[0:1, :]


def run_attention_forward(meta, lengths, tokens, norm, weights, first, moved, given):
    rows, width = tokens.shape
    groups = width // LANES
    steps = rows // BLOCK
    seqs = BLOCK // LANES
    heads = LANES // HEAD_DIM
    args = (tokens, norm) + tuple(weights) + tuple(first) + tuple(moved)
    in_specs = [pl.BlockSpec((BLOCK, width), lambda i, *_: (i, 0))] + [whole(a) for a in args[1:]]
    out_shape = [
        pltpu.HBM((groups, rows, 3 * LANES), LOW),
        pltpu.HBM((groups, rows // LANES, heads * LANES, LANES), F32),
        pltpu.HBM((rows, width), LOW),
        pltpu.HBM((rows, width), F32),
    ]
    out_specs = [
        pl.BlockSpec((groups, BLOCK, 3 * LANES), lambda i, *_: (0, i, 0)),
        pl.BlockSpec((groups, seqs, heads * LANES, LANES), lambda i, *_: (0, i, 0, 0)),
        pl.BlockSpec((BLOCK, width), lambda i, *_: (i, 0)),
        pl.BlockSpec((BLOCK, width), lambda i, *_: (i, 0)),
    ]
    scratch = []
    if not given:
        extra = [shape((groups, width, 3 * LANES), LOW), shape((width, width), LOW)]
        out_shape += extra
        out_specs += [whole(e) for e in extra]
        scratch = [pltpu.VMEM((groups, 8, LANES), F32)]
    flops = 2 * rows * width * 4 * width + 4 * rows * LANES * width * 2
    return pl.pallas_call(
        functools.partial(attention_forward, len(first), given),
        grid_spec=pltpu.PrefetchScalarGridSpec(
            num_scalar_prefetch=2,
            grid=(steps,),
            in_specs=in_specs,
            out_specs=out_specs,
            scratch_shapes=scratch,
        ),
        out_shape=out_shape,
        compiler_params=params(32),
        cost_estimate=pl.CostEstimate(flops=flops, bytes_accessed=16 << 20, transcendentals=0),
        name="attention_forward",
    )(meta, lengths, *args)


def feed_kernel(count, given, meta, labels, tasks, *refs):
    pre_one_ref, out_grad_ref, norm, classes = refs[:4]
    step = pl.program_id(0)
    last = pl.num_programs(0) - 1
    if given:
        wup, wdown, bias = refs[4:7]
        output_ref, back_ref, norm_grad, class_grad, bias_grad, up_grad, down_grad = refs[7:14]
        act_keep, slope_keep, grad_keep = refs[14:]
    else:
        own_up, own_down, own_bias = refs[4:7]
        bias_refs = refs[7 : 7 + count]
        first_refs = refs[7 + count : 7 + 2 * count]
        moved = refs[7 + 2 * count : 16 + 2 * count]
        output_ref, back_ref, norm_grad, class_grad, bias_grad, keep, send = refs[16 + 2 * count : 23 + 2 * count]
        act_keep, slope_keep, grad_keep, wup, wdown, bias, up_grad, down_grad = refs[23 + 2 * count :]
    width = norm.shape[1]
    here = meta[0]

    @pl.when(step == 0)
    def start():
        norm_grad[...] = jnp.zeros_like(norm_grad)
        class_grad[...] = jnp.zeros_like(class_grad)
        bias_grad[...] = jnp.zeros_like(bias_grad)
        up_grad[...] = jnp.zeros_like(up_grad)
        down_grad[...] = jnp.zeros_like(down_grad)

    if not given:

        @pl.when(step == 0)
        def unpack():
            for r in range(4):
                wup[here, :, r * LANES : (r + 1) * LANES] = own_up[pl.ds(r, width, stride=4), :].astype(LOW)
                bias[here, 0:1, r * LANES : (r + 1) * LANES] = own_bias[2 + r : 3 + r, :]
            wdown[here] = own_down[...].astype(LOW)
            for j in range(1, count + 1):
                piece = bias_refs[j - 1]
                base = piece.shape[0] - 6
                for r in range(4):
                    bias[here ^ j, 0:1, r * LANES : (r + 1) * LANES] = piece[base + r : base + r + 1, :]
            rows = width // 8
            for place, shard, take in gathered(meta, moved, first_refs):
                for r in range(4):
                    wup[shard, at(place * rows, rows), r * LANES : (r + 1) * LANES] = take(r, rows, 4).astype(LOW)
                for b in range(width // LANES):
                    wdown[shard, at(place * rows, rows), b * LANES : (b + 1) * LANES] = take(
                        4 * rows + b * rows, rows
                    ).astype(LOW)

    shards = wup.shape[0]
    hat_one, scale_one = centred_parts(pre_one_ref[...])
    hidden = hat_one * norm[1:2, :] + norm[2:3, :]
    low_hidden = hidden.astype(LOW)
    ffn = None
    for s in range(shards):
        act, slope = gelu_parts(mul(low_hidden, wup[s]) + bias[s, 0:1, :])
        low_act = act.astype(LOW)
        act_keep[s] = low_act
        slope_keep[s] = slope
        term = mul(low_act, wdown[s])
        ffn = term if ffn is None else ffn + term
    hat_two, scale_two = centred_parts(hidden + ffn + norm[3:4, :])
    output = hat_two * norm[4:5, :] + norm[5:6, :]
    output_ref[...] = output

    grad = out_grad_ref[...]
    per_step = grad.shape[0] // LANES
    row = lax.broadcasted_iota(jnp.int32, grad.shape, 0)
    class_row = lax.broadcasted_iota(jnp.int32, (classes.shape[1], 1), 0)
    for t in range(per_step):
        task = tasks[step * per_step + t]
        table = classes[task]
        first_row = output[t * LANES : t * LANES + 1, :]
        logits = jnp.sum(table * first_row, -1, keepdims=True)
        logit_exp = jnp.exp(logits - jnp.max(logits, 0, keepdims=True))
        class_prob = logit_exp / jnp.sum(logit_exp, 0, keepdims=True)
        logit_grad = class_prob - (class_row == labels[step * per_step + t]).astype(F32)
        class_grad[task] += logit_grad * first_row
        grad = jnp.where(row == t * LANES, grad + jnp.sum(logit_grad * table, 0, keepdims=True), grad)

    norm_grad[4:5, :] += jnp.sum(grad * hat_two, 0, keepdims=True)
    norm_grad[5:6, :] += jnp.sum(grad, 0, keepdims=True)
    back_two = norm_back(grad, hat_two, scale_two, norm[4:5, :])
    norm_grad[3:4, :] += jnp.sum(back_two, 0, keepdims=True)
    low_back = back_two.astype(LOW)
    back_hidden = back_two
    for s in range(shards):
        up_back = (mul(low_back, wdown[s], 1, 1) * slope_keep[s]).astype(LOW)
        grad_keep[s] = up_back
        back_hidden = back_hidden + mul(up_back, wup[s], 1, 1)
    own_back = grad_keep[here]
    down_grad[...] += mul(act_keep[here], low_back, 0, 0)
    up_grad[...] += mul(low_hidden, own_back, 0, 0)
    bias_grad[0:1, :] += jnp.sum(own_back.astype(F32), 0, keepdims=True)

    norm_grad[1:2, :] += jnp.sum(back_hidden * hat_one, 0, keepdims=True)
    norm_grad[2:3, :] += jnp.sum(back_hidden, 0, keepdims=True)
    back_one = norm_back(back_hidden, hat_one, scale_one, norm[1:2, :])
    norm_grad[0:1, :] += jnp.sum(back_one, 0, keepdims=True)
    back_ref[...] = back_one

    if not given:

        def give_up(ref):
            for r in range(4):
                ref[pl.ds(r, width, stride=4), :] = up_grad[:, r * LANES : (r + 1) * LANES]

        def give_down(ref):
            for b in range(width // LANES):
                ref[b * 4 * LANES : (b + 1) * 4 * LANES, :] = down_grad[:, b * LANES : (b + 1) * LANES]

        @pl.when((step == last) & (meta[2] == 0))
        def give_first():
            give_up(keep)
            give_down(send)

        @pl.when((step == last) & (meta[2] == 1))
        def give_second():
            give_up(send)
            give_down(keep)


def run_feed(meta, labels, tasks, pre_one, out_grad, norm, classes, weights, biases, first, moved, given):
    rows, width = pre_one.shape
    steps = rows // BLOCK
    if given:
        shards, _, hidden = weights[0].shape
    else:
        shards, hidden = len(first) + 1, 4 * LANES
    args = (pre_one, out_grad, norm, classes) + tuple(weights) + tuple(biases) + tuple(first) + tuple(moved)
    by_rows = pl.BlockSpec((BLOCK, width), lambda i, *_: (i, 0))
    in_specs = [by_rows, by_rows] + [whole(a) for a in args[2:]]
    fixed = [shape((8, width)), shape(classes.shape), shape((8, hidden))]
    scratch = [
        pltpu.VMEM((shards, BLOCK, hidden), LOW),
        pltpu.VMEM((shards, BLOCK, hidden), F32),
        pltpu.VMEM((shards, BLOCK, hidden), LOW),
    ]
    if given:
        fixed += [shape((width, hidden)), shape((hidden, width))]
    else:
        half = hidden * width // LANES
        fixed += [pltpu.HBM((half, LANES), F32), pltpu.HBM((half, LANES), F32)]
        scratch += [
            pltpu.VMEM((shards, width, hidden), LOW),
            pltpu.VMEM((shards, hidden, width), LOW),
            pltpu.VMEM((shards, 8, hidden), F32),
            pltpu.VMEM((width, hidden), F32),
            pltpu.VMEM((hidden, width), F32),
        ]
    flops = 2 * rows * width * hidden * (4 * shards + 2)
    return pl.pallas_call(
        functools.partial(feed_kernel, len(first), given),
        grid_spec=pltpu.PrefetchScalarGridSpec(
            num_scalar_prefetch=3,
            grid=(steps,),
            in_specs=in_specs,
            out_specs=[by_rows, by_rows] + [whole(f) for f in fixed],
            scratch_shapes=scratch,
        ),
        out_shape=[pltpu.HBM((rows, width), F32), pltpu.HBM((rows, width), F32)] + fixed,
        compiler_params=params(44),
        cost_estimate=pl.CostEstimate(flops=4 * flops, bytes_accessed=20 << 20, transcendentals=0),
        name="feed_both",
    )(meta, labels, tasks, *args)


def pairs_back(items, masks):
    wide = [stacked(back, masks) for _, _, back in items]
    prob_back = [mul(w, qkv[:, 2 * LANES :], 1, 1) for w, (qkv, _, _) in zip(wide, items)]
    value_back = [mul(prob.astype(LOW), w, 0, 0).astype(LOW) for w, (_, prob, _) in zip(wide, items)]
    inner = [jnp.sum(prob * b, -1, keepdims=True) for b, (_, prob, _) in zip(prob_back, items)]
    raw = [
        (prob * (b - n) * (1.0 / math.sqrt(HEAD_DIM))).astype(LOW) for b, n, (_, prob, _) in zip(prob_back, inner, items)
    ]
    query_back = [
        mul(side_by_side(r, LANES), stacked(qkv[:, LANES : 2 * LANES], masks)).astype(LOW)
        for r, (qkv, _, _) in zip(raw, items)
    ]
    key_back = [mul(r, stacked(qkv[:, :LANES], masks), 0, 0).astype(LOW) for r, (qkv, _, _) in zip(raw, items)]
    return zip(query_back, key_back, value_back)


def groups_back(low_back, sources, masks):
    seqs = low_back.shape[0] // LANES
    parts = [slice(t * LANES, (t + 1) * LANES) for t in range(seqs)]
    backs = [mul(low_back, wout, 1, 1).astype(LOW) for _, _, wout, _ in sources]
    for t, part in enumerate(parts):
        items = [(qkv[part, :], prob[t], back[part]) for (qkv, prob, _, _), back in zip(sources, backs)]
        for source, grads in zip(sources, pairs_back(items, masks)):
            for j, grad in enumerate(grads):
                source[3][part, j * LANES : (j + 1) * LANES] = grad


def own_kernel(given, meta, back_ref, tokens, qkv, prob, context, wout, *refs):
    if given:
        grads, qkv_grad, out_grad, split_grad = refs
    else:
        norm_grad, class_grad, up_bias, grads, keep, send, qkv_grad, out_grad, split_grad, packed = refs
    step = pl.program_id(0)
    last = pl.num_programs(0) - 1

    @pl.when(step == 0)
    def start():
        qkv_grad[...] = jnp.zeros_like(qkv_grad)
        out_grad[...] = jnp.zeros_like(out_grad)
        split_grad[...] = jnp.zeros_like(split_grad)

    masks = head_masks()
    low_back = back_ref[...].astype(LOW)

    groups_back(low_back, [(qkv.at[0], prob.at[0], wout[...], grads)], masks)
    out_grad[...] += mul(context[...], low_back, 0, 0)
    both = grads[...]
    qkv_grad[...] += mul(tokens[...], both, 0, 0)
    split_grad[0:1, :] += jnp.sum(both[:, :LANES].astype(F32), 0, keepdims=True)
    split_grad[1:2, :] += jnp.sum(both[:, 2 * LANES :].astype(F32), 0, keepdims=True)

    if not given:
        width = back_ref.shape[1]
        blocks = width // LANES

        @pl.when(step == last)
        def fill():
            for j in range(3):
                packed[j * width : (j + 1) * width, :] = qkv_grad[:, j * LANES : (j + 1) * LANES]
            base = 3 * width
            for b in range(blocks):
                packed[base + b * LANES : base + (b + 1) * LANES, :] = out_grad[:, b * LANES : (b + 1) * LANES]
            base += width
            packed[base:, :] = jnp.zeros((packed.shape[0] - base, LANES), F32)
            packed[base : base + 2, :] = split_grad[0:2, :]
            for r in range(4):
                packed[base + 2 + r : base + 3 + r, :] = up_bias[0:1, r * LANES : (r + 1) * LANES]
            base += 8
            for b in range(blocks):
                packed[base + 8 * b : base + 8 * b + 6, :] = norm_grad[0:6, b * LANES : (b + 1) * LANES]
            base += 8 * blocks
            tasks, kinds, _ = class_grad.shape
            each = small_rows(tasks, kinds)
            for b in range(blocks):
                for t in range(tasks):
                    row = base + each * b + kinds * t
                    packed[row : row + kinds, :] = class_grad[t, :, b * LANES : (b + 1) * LANES]

        half = keep.shape[0]

        @pl.when((step == last) & (meta[2] == 0))
        def give_first():
            keep[...] = packed[:half, :]
            send[...] = packed[half:, :]

        @pl.when((step == last) & (meta[2] == 1))
        def give_second():
            keep[...] = packed[half:, :]
            send[...] = packed[:half, :]


def small_rows(tasks, kinds):
    return -(-tasks * kinds // 8) * 8


def packed_rows(width, tasks, kinds):
    blocks = width // LANES
    rows = 4 * width + 8 + 8 * blocks + blocks * small_rows(tasks, kinds)
    return -(-rows // 64) * 64


def run_own(meta, back, tokens, qkv, prob, context, wout, smalls, given):
    rows, width = back.shape
    steps = rows // BLOCK
    seqs = BLOCK // LANES
    heads = LANES // HEAD_DIM
    by_rows = pl.BlockSpec((BLOCK, width), lambda i, m: (i, 0))
    in_specs = [
        by_rows,
        by_rows,
        pl.BlockSpec((1, BLOCK, 3 * LANES), lambda i, m: (m[3], i, 0)),
        pl.BlockSpec((1, seqs, heads * LANES, LANES), lambda i, m: (m[3], i, 0, 0)),
        pl.BlockSpec((BLOCK, LANES), lambda i, m: (i, m[3])),
        pl.BlockSpec((LANES, width), lambda i, m: (m[3], 0)),
    ] + [whole(s) for s in smalls]
    out_shape = [pltpu.HBM((rows, 3 * LANES), LOW)]
    out_specs = [pl.BlockSpec((BLOCK, 3 * LANES), lambda i, m: (i, 0))]
    sums = [shape((width, 3 * LANES)), shape((LANES, width)), shape((8, LANES))]
    scratch = []
    if given:
        fixed = sums
    else:
        count = packed_rows(width, *smalls[1].shape[:2])
        fixed = [pltpu.HBM((count // 2, LANES), F32)] * 2
        scratch = [pltpu.VMEM(s.shape, F32) for s in sums] + [pltpu.VMEM((count, LANES), F32)]
    return pl.pallas_call(
        functools.partial(own_kernel, given),
        grid_spec=pltpu.PrefetchScalarGridSpec(
            num_scalar_prefetch=1,
            grid=(steps,),
            in_specs=in_specs,
            out_specs=out_specs + [whole(f) for f in fixed],
            scratch_shapes=scratch,
        ),
        out_shape=out_shape + fixed,
        compiler_params=params(28),
        cost_estimate=pl.CostEstimate(flops=4 << 30, bytes_accessed=8 << 20, transcendentals=0),
        name="attention_own",
    )(meta, in_hbm(back), tokens, in_hbm(qkv), in_hbm(prob), in_hbm(context), wout, *smalls)


def rest_kernel(meta, back_ref, qkv, prob, wout, wqkv, own, *refs):
    input_grad, grads = refs[-2:]
    group = meta[3]
    groups = qkv.shape[0]
    back = back_ref[...]
    grads[group] = own[...]
    sources = []
    for r in range(1, groups):
        g = group ^ r
        sources.append((qkv.at[g], prob.at[g], wout[at(g * LANES, LANES), :], grads.at[g]))
    groups_back(back.astype(LOW), sources, head_masks())
    total = None
    for g in range(groups):
        term = mul(grads[g], wqkv[g], 1, 1)
        total = term if total is None else total + term
    input_grad[...] = back + total


def run_rest(meta, back, qkv, prob, wout, wqkv, own, block, before=None):
    rows, width = back.shape
    groups = width // LANES
    few = BLOCK // 2
    seqs = few // LANES
    heads = LANES // HEAD_DIM
    by_rows = pl.BlockSpec((few, width), lambda i, m: (2 * block + i, 0))
    held = () if before is None else (before,)
    return pl.pallas_call(
        rest_kernel,
        grid_spec=pltpu.PrefetchScalarGridSpec(
            num_scalar_prefetch=1,
            grid=(2,),
            in_specs=[
                by_rows,
                pl.BlockSpec((groups, few, 3 * LANES), lambda i, m: (0, 2 * block + i, 0)),
                pl.BlockSpec((groups, seqs, heads * LANES, LANES), lambda i, m: (0, 2 * block + i, 0, 0)),
                whole(wout),
                whole(wqkv),
                pl.BlockSpec((few, 3 * LANES), lambda i, m: (2 * block + i, 0)),
            ]
            + [pl.BlockSpec(memory_space=pl.ANY)] * len(held),
            out_specs=by_rows,
            scratch_shapes=[pltpu.VMEM((groups, few, 3 * LANES), LOW)],
        ),
        out_shape=shape((rows, width)),
        input_output_aliases={7: 0} if held else {},
        compiler_params=params(28),
        cost_estimate=pl.CostEstimate(flops=8 << 30, bytes_accessed=8 << 20, transcendentals=0),
        name="attention_rest",
    )(meta, in_hbm(back), in_hbm(qkv), in_hbm(prob), wout, wqkv, in_hbm(own), *held)


def places_of(meta):
    return [(meta[2] ^ half) * 4 + (meta[4] ^ bits) for half in range(2) for bits in range(4)]


def squares_kernel(split_rows, meta, *refs):
    parts, before, out, sums = refs[:8], refs[8:-2], refs[-2], refs[-1]
    rows = parts[0].shape[0]
    row = lax.broadcasted_iota(jnp.int32, (rows, LANES), 0)
    for place, part in zip(places_of(meta), parts):
        square = part[...] * part[...]
        if split_rows < 8 * rows:
            is_split = row < split_rows - place * rows
            sums[place, 1:2, :] = jnp.sum(jnp.where(is_split, 0.0, square), 0, keepdims=True)
            square = jnp.where(is_split, square, 0.0)
        sums[place, 0:1, :] = jnp.sum(square, 0, keepdims=True)
    out[...] = jnp.zeros_like(out)
    for kind in range(1 if split_rows == 8 * rows else 2):
        total = before[0][kind : kind + 1, :] if before else None
        for n in range(8):
            term = sums[n, kind : kind + 1, :]
            total = term if total is None else total + term
        out[kind : kind + 1, :] = total


def squares_of(meta, parts, split_rows=None, before=()):
    out = shape((8, LANES))
    return pl.pallas_call(
        functools.partial(squares_kernel, split_rows or 8 * parts[0].shape[0]),
        grid_spec=pltpu.PrefetchScalarGridSpec(
            num_scalar_prefetch=1,
            grid=(1,),
            in_specs=[whole(p) for p in tuple(parts) + before],
            out_specs=whole(out),
            scratch_shapes=[pltpu.VMEM((8, 8, LANES), F32)],
        ),
        out_shape=out,
        compiler_params=params(16),
        name="squares",
    )(meta, *parts, *before)


def adam_kernel(count, meta, squares, *refs):
    moved = refs[:count]
    a_parts, b_parts = refs[count : count + 8], refs[count + 8 : count + 16]
    refs = refs[count + 16 :]
    states, norm_ref, targets = refs[:21], refs[21], refs[22:43]
    sums, a_full, b_full, done = refs[43:47]
    outs = refs[47:]
    for parts, full in ((a_parts, a_full), (b_parts, b_full)):
        rows = parts[0].shape[0]
        for place, part in zip(places_of(meta), parts):
            full[pl.ds(pl.multiple_of(place * rows, 8), rows), :] = part[...]
    sums[meta[0]] = squares[...]
    for r in range(1, count + 1):
        sums[meta[0] ^ r] = moved[r - 1][...]
    total = sums[0]
    for s in range(1, count + 1):
        total = total + sums[s]
    all_squares = jnp.sum(total[0:1, :], -1, keepdims=True) + jnp.sum(squares[1:2, :], -1, keepdims=True)
    grad_norm = jnp.sqrt(all_squares)
    norm_ref[...] = grad_norm
    factor = jnp.minimum(1.0, clip_at / (grad_norm + 1e-06))
    width = states[5 * 3].shape[1]
    blocks = width // LANES
    copies = []

    def update(index, where, grad, with_decay):
        first, second, weight = (states[3 * index + j][where] for j in range(3))
        for j, value in enumerate(adam_math(weight, first, second, grad, factor, with_decay)):
            outs[3 * index + j][where] = value

    def give(index, where=None):
        for j in range(3 * index, 3 * index + 3):
            source, target = outs[j], targets[j]
            if where is not None:
                source, target = source.at[where], target.at[where]
            copies.append(pltpu.make_async_copy(source, target, done.at[len(copies)]))
            copies[-1].start()

    rows = 4 * width
    for b in range(blocks):
        part = slice(b * width, (b + 1) * width)
        update(2, (part, slice(None)), b_full[part, :], True)
        give(2, part)
    for b in range(blocks):
        lanes = slice(b * LANES, (b + 1) * LANES)
        update(3, (slice(None), lanes), b_full[rows + b * 4 * LANES : rows + (b + 1) * 4 * LANES, :], True)
        give(3, (slice(None), lanes))
    for j in range(3):
        update(0, (j,), a_full[j * width : (j + 1) * width, :], True)
        give(0, j)
    base = 3 * width
    for b in range(blocks):
        lanes = slice(b * LANES, (b + 1) * LANES)
        update(1, (slice(None), lanes), a_full[base + b * LANES : base + (b + 1) * LANES, :], True)
    give(1)
    base += width
    update(4, (slice(None), slice(None)), a_full[base : base + 6, :], False)
    give(4)
    base += 8
    for b in range(blocks):
        lanes = slice(b * LANES, (b + 1) * LANES)
        update(5, (slice(None), lanes), a_full[base + 8 * b : base + 8 * b + 6, :], False)
    give(5)
    base += 8 * blocks
    tasks, kinds, _ = states[6 * 3].shape
    each = small_rows(tasks, kinds)
    for b in range(blocks):
        lanes = slice(b * LANES, (b + 1) * LANES)
        for t in range(tasks):
            row = base + each * b + kinds * t
            update(6, (t, slice(None), lanes), a_full[row : row + kinds, :], True)
    give(6)
    for copy in copies:
        copy.wait()


def run_adam(meta, squares, moved, a_parts, b_parts, states):
    held = pl.BlockSpec(memory_space=pltpu.HBM)
    here = pl.BlockSpec(memory_space=pltpu.VMEM)
    blocks = states[-4].shape[1] // LANES
    args = (squares,) + tuple(moved) + tuple(a_parts) + tuple(b_parts)
    return pl.pallas_call(
        functools.partial(adam_kernel, len(moved)),
        in_specs=[pl.BlockSpec(memory_space=pltpu.SMEM)] + [here] * (len(args) + len(states)),
        out_specs=[here] + [held] * len(states),
        out_shape=[shape((1, 1))] + [shape(s.shape) for s in states],
        scratch_shapes=[
            pltpu.VMEM((len(moved) + 1, 8, LANES), F32),
            pltpu.VMEM((8 * a_parts[0].shape[0], LANES), F32),
            pltpu.VMEM((8 * b_parts[0].shape[0], LANES), F32),
            pltpu.SemaphoreType.DMA((6 * blocks + 3 * 3 + 3 * 4,)),
        ]
        + [pltpu.VMEM(s.shape, F32) for s in states],
        compiler_params=params(18),
        name="adam",
    )(meta, *args, *(s if n % 3 == 2 else in_vmem(s) for n, s in enumerate(states)))


def shares(mesh, *args):
    fast = (
        mesh.shape["head"] == 4
        and mesh.shape["batch"] == 4
        and mesh.shape["rep"] == 2
        and args[5].shape[2] == LANES
        and args[0].shape[0] == 2 * BLOCK
        and mesh.shape["head"] * LANES == args[0].shape[1]
    )
    return (by_permutes if fast else by_gathers)(mesh, *args)


def by_permutes(
    mesh,
    tokens_in,
    out_grad,
    lengths,
    labels,
    task_id,
    qkv_weight,
    qkv_first,
    qkv_second,
    out_weight,
    out_first,
    out_second,
    up_weight,
    up_first,
    up_second,
    down_weight,
    down_first,
    down_second,
    split_bias,
    split_first,
    split_second,
    norm_params,
    norm_first,
    norm_second,
    class_weight,
    class_first,
    class_second,
):
    plane = Plane(mesh)
    width = tokens_in.shape[1]
    here = lax.axis_index("head")
    batch = lax.axis_index("batch")
    rep = lax.axis_index("rep")
    quarter = (batch // 2) * 2 + rep
    meta = jnp.stack([here, batch * plane.rep + rep, batch % 2, here, quarter]).astype(jnp.int32)

    def flat_up(value):
        return value.reshape(-1, LANES)

    def flat_down(value):
        return value.reshape(-1, width)

    def flat_class(value):
        return jnp.transpose(value, (0, 2, 1))

    up_flat, down_flat, classes = flat_up(up_weight), flat_down(down_weight), flat_class(class_weight)
    a_send, b_send = pack(meta, qkv_weight, out_weight, split_bias, up_flat, down_flat)
    turns = range(1, plane.heads)
    a_first = [plane.along(a_send, r) for r in turns]
    b_first = plane.round(b_send)
    a_near = plane.spread(after(jnp.concatenate([v[:-8] for v in a_first], 0), b_first[0]))
    b_first = plane.round_on(b_first)
    a_corner = plane.corners(a_near)
    b_near = plane.spread(after(jnp.concatenate(b_first, 0), a_near))
    a_moved = plane.shared(a_near, a_corner)

    qkv, prob, context, pre_one, wqkv, wout = run_attention_forward(
        meta, lengths, tokens_in, norm_params, (qkv_weight, out_weight, split_bias), a_first, a_moved, False
    )
    b_near = after(b_near, pre_one)
    b_moved = plane.shared(b_near, plane.corners(b_near))
    output, back_one, norm_grad, class_grad, up_bias_grad, b_keep, b_give = run_feed(
        meta,
        labels,
        task_id,
        pre_one,
        out_grad,
        norm_params,
        classes,
        (up_flat, down_flat, split_bias),
        a_first,
        b_first,
        b_moved,
        False,
    )
    b_parts = plane.quarters(b_keep, b_give, quarter)
    back_one = after(back_one, b_parts)
    own, a_keep, a_give = run_own(
        meta, back_one, tokens_in, qkv, prob, context, wout, (norm_grad, class_grad, up_bias_grad), False
    )
    b_own = plane.scatter(b_parts, a_give)
    b_crossed, b_near = plane.rejoin(b_own)
    a_parts = plane.quarters(a_keep, a_give, quarter)
    back_one = after(back_one, a_parts, b_crossed)
    input_grad = run_rest(meta, back_one, qkv, prob, wout, wqkv, own, 0)
    b_parts = plane.rejoin_on(b_own, b_crossed, after(b_near, input_grad))
    a_own = plane.scatter(a_parts, input_grad)
    a_crossed, a_near = plane.rejoin(a_own)
    input_grad = run_rest(meta, after(back_one, a_crossed), qkv, prob, wout, wqkv, own, 1, input_grad)
    a_parts = plane.rejoin_on(a_own, a_crossed, after(a_near, input_grad))
    squares = squares_of(meta, a_parts, 4 * width + 8, (squares_of(meta, b_parts),))
    moved = tuple(plane.along(squares, r) for r in turns)
    states = (
        (qkv_first, qkv_second, qkv_weight)
        + (out_first, out_second, out_weight)
        + (flat_up(up_first), flat_up(up_second), up_flat)
        + (flat_down(down_first), flat_down(down_second), down_flat)
        + (split_first, split_second, split_bias)
        + (norm_first, norm_second, norm_params)
        + (flat_class(class_first), flat_class(class_second), classes)
    )
    grad_norm, *new = run_adam(meta, squares, moved, a_parts, b_parts, states)
    new[6:9] = [v.reshape(up_weight.shape) for v in new[6:9]]
    new[9:12] = [v.reshape(down_weight.shape) for v in new[9:12]]
    new[18:21] = [jnp.transpose(v, (0, 2, 1)) for v in new[18:21]]
    return (output, input_grad, grad_norm[0, 0]) + tuple(new)


def lower_kernel(source, target):
    target[...] = source[...].astype(LOW)


def lowered(value):
    flat = value.reshape(-1, value.shape[-1])
    out = pl.pallas_call(
        lower_kernel, out_shape=shape(flat.shape, LOW), compiler_params=params(), name="lowered"
    )(flat)
    return out.reshape(value.shape)


def by_gathers(
    mesh,
    tokens_in,
    out_grad,
    lengths,
    labels,
    task_id,
    qkv_weight,
    qkv_first,
    qkv_second,
    out_weight,
    out_first,
    out_second,
    up_weight,
    up_first,
    up_second,
    down_weight,
    down_first,
    down_second,
    split_bias,
    split_first,
    split_second,
    norm_params,
    norm_first,
    norm_second,
    class_weight,
    class_first,
    class_second,
):
    width = tokens_in.shape[1]
    cols = qkv_weight.shape[2]
    groups = width // LANES
    hidden = 4 * cols
    here = lax.axis_index("head")
    zero = jnp.zeros_like(here)
    meta = jnp.stack([here, zero, zero, here * cols // LANES, zero]).astype(jnp.int32)
    full_qkv = lax.all_gather(qkv_weight, "head", axis=2, tiled=True)
    full_out = lax.all_gather(out_weight, "head", axis=0, tiled=True)
    full_up = lax.all_gather(up_weight.reshape(width, hidden), "head", axis=0)
    full_down = lax.all_gather(down_weight.reshape(hidden, width), "head", axis=0)
    full_bias = lax.all_gather(split_bias, "head", axis=1, tiled=True)
    wqkv = full_qkv.reshape(3, width, groups, LANES).transpose(2, 1, 0, 3).reshape(groups, width, 3 * LANES)
    wqkv, wout = lowered(wqkv), lowered(full_out)
    qv_bias = jnp.pad(full_bias[:2].reshape(2, groups, LANES).transpose(1, 0, 2), ((0, 0), (0, 6), (0, 0)))
    shards = width // cols
    up_bias = full_bias[2:].reshape(4, shards, cols).transpose(1, 0, 2).reshape(shards, 1, hidden)
    up_bias = jnp.pad(up_bias, ((0, 0), (0, 7), (0, 0)))
    classes = jnp.transpose(class_weight, (0, 2, 1))

    qkv, prob, context, pre_one = run_attention_forward(
        meta, lengths, tokens_in, norm_params, (wqkv, wout, qv_bias), (), (), True
    )
    output, back_one, norm_grad, class_grad, up_bias_grad, up_grad, down_grad = run_feed(
        meta,
        labels,
        task_id,
        pre_one,
        out_grad,
        norm_params,
        classes,
        (lowered(full_up), lowered(full_down), up_bias),
        (),
        (),
        (),
        True,
    )
    own, qkv_grad, out_w_grad, split_grad = run_own(meta, back_one, tokens_in, qkv, prob, context, wout, (), True)
    input_grad = None
    for block in range(tokens_in.shape[0] // BLOCK):
        input_grad = run_rest(meta, back_one, qkv, prob, wout, wqkv, own, block, input_grad)
    start = here * cols % LANES
    qkv_grad = qkv_grad.reshape(width, 3, LANES).transpose(1, 0, 2)
    qkv_grad = lax.dynamic_slice_in_dim(qkv_grad, start, cols, 2)
    out_w_grad = lax.dynamic_slice_in_dim(out_w_grad, start, cols, 0)
    split_grad = lax.dynamic_slice_in_dim(split_grad[:2], start, cols, 1)
    split_grad = jnp.concatenate([split_grad, up_bias_grad[0].reshape(4, cols)], 0)
    summed = lax.psum(
        (
            qkv_grad,
            out_w_grad,
            up_grad.reshape(up_weight.shape),
            down_grad.reshape(down_weight.shape),
            split_grad,
            norm_grad[:6],
            jnp.transpose(class_grad, (0, 2, 1)),
        ),
        ("batch", "rep"),
    )
    split_square = lax.psum(sum(jnp.sum(v * v) for v in summed[:5]), "head")
    grad_norm = jnp.sqrt(split_square + sum(jnp.sum(v * v) for v in summed[5:]))
    factor = jnp.minimum(1.0, clip_at / (grad_norm + 1e-06))
    states = (
        (qkv_weight, qkv_first, qkv_second, True),
        (out_weight, out_first, out_second, True),
        (up_weight, up_first, up_second, True),
        (down_weight, down_first, down_second, True),
        (split_bias, split_first, split_second, False),
        (norm_params, norm_first, norm_second, False),
        (class_weight, class_first, class_second, True),
    )
    results = ()
    for grad, (weight, first, second, decay) in zip(summed, states):
        results += adam_math(weight, first, second, grad, factor, decay)
    return (output, input_grad, grad_norm) + results


def solution(mesh):
    rows = P(("batch", "rep"), None)
    seqs = P(("batch", "rep"))
    kinds = (
        (P(None, None, "head"),) * 3
        + (P("head", None),) * 3
        + (P(None, None, "head"),) * 3
        + (P(None, "head", None),) * 3
        + (P(None, "head"),) * 3
        + (P(),) * 6
    )
    return jax.shard_map(
        functools.partial(shares, mesh),
        mesh=mesh,
        in_specs=(rows, rows, seqs, seqs, seqs) + kinds,
        out_specs=(rows, rows, P()) + kinds,
        check_vma=False,
    )
```

```python
import functools
import math

import jax
import jax.numpy as jnp
from jax import lax
from jax.experimental import pallas as pl
from jax.experimental.pallas import tpu as pltpu
from jax.sharding import PartitionSpec as P

HEAD_DIM = 64
STEP = 10
LANES = 128
BLOCK = 512

F32 = jnp.float32
LOW = jnp.bfloat16

beta_one = 0.9
beta_two = 0.999
learn_rate = 0.05
vector_rate = 0.4
weight_decay = 0.01
adam_eps = 1e-08
clip_at = 1.0
norm_eps = 1e-12
masked = -1e30


def mul(left, right, left_dim=1, right_dim=0):
    return lax.dot_general(
        left, right, (((left_dim,), (right_dim,)), ((), ())), preferred_element_type=F32
    )


def whole(array):
    rank = len(array.shape)
    return pl.BlockSpec(array.shape, lambda *_: (0,) * rank, pipeline_mode=pl.Buffered(1))


def params(mib=52):
    return pltpu.CompilerParams(vmem_limit_bytes=mib << 20)


def in_hbm(value):
    return pltpu.with_memory_space_constraint(value, pltpu.HBM)


def in_vmem(value):
    return pltpu.with_memory_space_constraint(value, pltpu.VMEM)


def shape(dims, kind=F32):
    return jax.ShapeDtypeStruct(tuple(dims), kind)


def centred_parts(values):
    centred = values - jnp.mean(values, -1, keepdims=True)
    spread = jnp.mean(centred * centred, -1, keepdims=True)
    scale = lax.rsqrt(spread + norm_eps)
    return centred * scale, scale


def norm_back(grad, hat, scale, gain):
    scaled = grad * gain
    inner = jnp.mean(scaled * hat, -1, keepdims=True)
    return scale * (scaled - jnp.mean(scaled, -1, keepdims=True) - hat * inner)


def gelu_parts(x):
    below = lax.erf(x * math.sqrt(0.5)) * 0.5 + 0.5
    density = jnp.exp2(x * x * (-0.5 * math.log2(math.e))) * (1.0 / math.sqrt(2.0 * math.pi))
    return x * below, below + x * density


def head_masks():
    lane = lax.broadcasted_iota(jnp.int32, (1, LANES), 1)
    return [(lane // HEAD_DIM == h).astype(LOW) for h in range(LANES // HEAD_DIM)]


def stacked(matrix, masks):
    return jnp.concatenate([matrix * m for m in masks], 0)


def side_by_side(matrix, rows):
    return jnp.concatenate([matrix[:rows], matrix[rows:]], 1)


def adam_math(weight, first, second, grad, factor, with_decay):
    clipped = grad * factor
    first_new = beta_one * first + (1.0 - beta_one) * clipped
    second_new = beta_two * second + (1.0 - beta_two) * clipped * clipped
    first_hat = first_new / (1.0 - beta_one**STEP)
    second_hat = second_new / (1.0 - beta_two**STEP)
    update = first_hat / (jnp.sqrt(second_hat) + adam_eps)
    if with_decay:
        return first_new, second_new, weight - learn_rate * (update + weight_decay * weight)
    return first_new, second_new, weight - vector_rate * update


def pairs(size, bit):
    return [(i, i ^ bit) for i in range(size)]


class Plane:
    def __init__(self, mesh):
        self.heads = mesh.shape["head"]
        self.batch = mesh.shape["batch"]
        self.rep = mesh.shape["rep"]

    def core(self, value):
        return lax.ppermute(value, "batch", pairs(self.batch, 1))

    def side(self, value):
        return lax.ppermute(value, "batch", pairs(self.batch, 2))

    def other(self, value):
        return lax.ppermute(value, "rep", pairs(self.rep, 1))

    def corner(self, value):
        return lax.ppermute(value, ("batch", "rep"), pairs(self.batch * self.rep, 2 * self.rep + 1))

    def along(self, value, bit):
        return lax.ppermute(value, "head", pairs(self.heads, bit))

    def round(self, block):
        return self.along(block, 1), self.along(block, 2), lax.ppermute(block, "head", [(1, 2), (2, 1)])

    def round_on(self, got):
        near, far, last = got
        return near, far, last + lax.ppermute(far, "head", [(1, 0), (2, 3)])

    def spread(self, block):
        return block, self.side(block), self.other(block)

    def corners(self, near):
        block, from_side, from_other = near
        half = block.shape[0] // 2
        return self.other(from_side[:half]), self.side(from_other[half:])

    def shared(self, near, corner):
        near = near + corner
        return near[1:] + tuple(self.core(v) for v in near)

    def quarters(self, keep, send, quarter, *others):
        both = keep + after(self.core(send), *others)
        rows = both.shape[0] // 4
        return tuple(lax.dynamic_slice_in_dim(both, (quarter ^ bits) * rows, rows, 0) for bits in range(4))

    def scatter(self, parts, *others):
        moved = (self.side(parts[2]), self.other(parts[1]), self.corner(parts[3]))
        moved = after(moved, *others)
        return parts[0] + moved[0] + moved[1] + moved[2]

    def rejoin(self, own):
        return self.core(own), (self.other(own), self.side(own), self.corner(own))

    def rejoin_on(self, own, crossed, near):
        return (own,) + near + (crossed,) + tuple(self.core(v) for v in near)


def after(value, *others):
    return lax.optimization_barrier((value, others))[0]


def pack_kernel(meta, qkv, out, bias, up, down, a_send, b_send, done):
    place = meta[1]
    places = 8
    rows = qkv.shape[1] // places
    few = out.shape[0] // places
    moves = [(qkv.at[j, at(place * rows, rows), :], a_send.at[j * rows : (j + 1) * rows, :]) for j in range(3)]
    base = 3 * rows
    for b in range(out.shape[1] // LANES):
        lanes = slice(b * LANES, (b + 1) * LANES)
        moves.append((out.at[at(place * few, few), lanes], a_send.at[base + b * few : base + (b + 1) * few, :]))
    moves.append((bias, a_send.at[a_send.shape[0] - 8 : a_send.shape[0] - 2, :]))
    base = up.shape[0] // places
    moves.append((up.at[at(place * base, base), :], b_send.at[:base, :]))
    few = down.shape[0] // places
    for b in range(down.shape[1] // LANES):
        lanes = slice(b * LANES, (b + 1) * LANES)
        moves.append((down.at[at(place * few, few), lanes], b_send.at[base + b * few : base + (b + 1) * few, :]))
    copies = [pltpu.make_async_copy(source, target, done.at[n]) for n, (source, target) in enumerate(moves)]
    for copy in copies:
        copy.start()
    for copy in copies:
        copy.wait()


def pack(meta, qkv, out, bias, up, down):
    places = 8
    width = out.shape[1]
    outs = [
        shape((4 * width // places + 8, LANES)),
        shape(((up.shape[0] + down.shape[0] * width // LANES) // places, LANES)),
    ]
    held = pl.BlockSpec(memory_space=pltpu.HBM)
    return pl.pallas_call(
        pack_kernel,
        grid_spec=pltpu.PrefetchScalarGridSpec(
            num_scalar_prefetch=1,
            grid=(1,),
            in_specs=[held] * 5,
            out_specs=[held] * 2,
            scratch_shapes=[pltpu.SemaphoreType.DMA((5 + 2 * (width // LANES),))],
        ),
        out_shape=outs,
        compiler_params=params(),
        name="pack",
    )(meta, *(in_hbm(v) for v in (qkv, out, bias, up, down)))


def gathered(meta, refs, first_refs):
    here, place = meta[0], meta[1]
    side, other, corner_top, corner_end = refs[:4]
    far = refs[4:]
    groups = [
        (0, None, None),
        (4, side, None),
        (1, other, None),
        (5, corner_top, corner_end),
        (2, far[0], None),
        (6, far[1], None),
        (3, far[2], None),
        (7, far[3], far[4]),
    ]
    for bits, top, end in groups:
        for r in range(1, len(first_refs) + 1):

            def take(row, count, stride=1, top=top, end=end, r=r, bits=bits):
                def read(ref, start):
                    return ref[pl.ds(start, count, stride=stride), :] if stride > 1 else ref[start : start + count, :]

                if bits == 0:
                    return read(first_refs[r - 1], row)
                share = top.shape[0] // (len(first_refs) if end is None else 1)
                if end is None:
                    return read(top, (r - 1) * share + row)
                total = top.shape[0] + end.shape[0]
                start = (r - 1) * (total // len(first_refs)) + row
                if start < top.shape[0]:
                    return read(top, start)
                return read(end, start - top.shape[0])

            yield place ^ bits, here ^ r, take


def at(start, size):
    return pl.ds(pl.multiple_of(start, size), size)


def attention_forward(count, given, meta, lengths, *refs):
    tokens, norm = refs[0], refs[1]
    step = pl.program_id(0)
    if given:
        wqkv, wout, bias = refs[2:5]
        qkv_out, prob_out, context_out, pre_out = refs[5:]
    else:
        own_qkv, own_out, own_bias = refs[2:5]
        first_refs = refs[5 : 5 + count]
        moved = refs[5 + count : 14 + count]
        qkv_out, prob_out, context_out, pre_out, wqkv, wout, bias = refs[14 + count :]
    width = norm.shape[1]

    if not given:

        @pl.when(step == 0)
        def unpack():
            here = meta[0]
            for j in range(3):
                wqkv[here, :, j * LANES : (j + 1) * LANES] = own_qkv[j].astype(LOW)
            wout[at(here * LANES, LANES), :] = own_out[...].astype(LOW)
            bias[here, : own_bias.shape[0], :] = own_bias[...]
            for r in range(1, count + 1):
                piece = first_refs[r - 1]
                bias[here ^ r] = piece[piece.shape[0] - 8 :, :]
            places = 8
            rows = width // places
            few = LANES // places
            for place, shard, take in gathered(meta, moved, first_refs):
                for j in range(3):
                    wqkv[shard, at(place * rows, rows), j * LANES : (j + 1) * LANES] = take(j * rows, rows).astype(LOW)
                for b in range(width // LANES):
                    wout[at(shard * LANES + place * few, few), b * LANES : (b + 1) * LANES] = take(
                        3 * rows + b * few, few
                    ).astype(LOW)

    rows_in = tokens[...]
    groups = wqkv.shape[0]
    masks = head_masks()
    seq_len = LANES
    per_step = rows_in.shape[0] // seq_len
    heads = len(masks)
    col = lax.broadcasted_iota(jnp.int32, (heads * seq_len, seq_len), 1)
    for g in range(groups):
        projected = mul(rows_in, wqkv[g])
        query = (projected[:, :LANES] + bias[g, 0:1, :]).astype(LOW)
        key = projected[:, LANES : 2 * LANES].astype(LOW)
        value = (projected[:, 2 * LANES :] + bias[g, 1:2, :]).astype(LOW)
        qkv_out[g, :, :LANES] = query
        qkv_out[g, :, LANES : 2 * LANES] = key
        qkv_out[g, :, 2 * LANES :] = value
        for t in range(per_step):
            part = slice(t * seq_len, (t + 1) * seq_len)
            scores = mul(stacked(query[part], masks), key[part], 1, 1) * (1.0 / math.sqrt(HEAD_DIM))
            scores = jnp.where(col < lengths[step * per_step + t], scores, masked)
            exponent = jnp.exp(scores - jnp.max(scores, -1, keepdims=True))
            prob = exponent * (1.0 / jnp.sum(exponent, -1, keepdims=True))
            prob_out[g, t] = prob
            low_prob = side_by_side(prob.astype(LOW), seq_len)
            context_out[part, g * LANES : (g + 1) * LANES] = mul(low_prob, stacked(value[part], masks)).astype(LOW)
    attn = mul(context_out[...], wout[...])
    pre_out[...] = rows_in.astype(F32) + attn + norm[0:1, :]


def run_attention_forward(meta, lengths, tokens, norm, weights, first, moved, given):
    rows, width = tokens.shape
    groups = width // LANES
    steps = rows // BLOCK
    seqs = BLOCK // LANES
    heads = LANES // HEAD_DIM
    args = (tokens, norm) + tuple(weights) + tuple(first) + tuple(moved)
    in_specs = [pl.BlockSpec((BLOCK, width), lambda i, *_: (i, 0))] + [whole(a) for a in args[1:]]
    out_shape = [
        pltpu.HBM((groups, rows, 3 * LANES), LOW),
        pltpu.HBM((groups, rows // LANES, heads * LANES, LANES), F32),
        pltpu.HBM((rows, width), LOW),
        pltpu.HBM((rows, width), F32),
    ]
    out_specs = [
        pl.BlockSpec((groups, BLOCK, 3 * LANES), lambda i, *_: (0, i, 0)),
        pl.BlockSpec((groups, seqs, heads * LANES, LANES), lambda i, *_: (0, i, 0, 0)),
        pl.BlockSpec((BLOCK, width), lambda i, *_: (i, 0)),
        pl.BlockSpec((BLOCK, width), lambda i, *_: (i, 0)),
    ]
    scratch = []
    if not given:
        extra = [shape((groups, width, 3 * LANES), LOW), shape((width, width), LOW)]
        out_shape += extra
        out_specs += [whole(e) for e in extra]
        scratch = [pltpu.VMEM((groups, 8, LANES), F32)]
    flops = 2 * rows * width * 4 * width + 4 * rows * LANES * width * 2
    return pl.pallas_call(
        functools.partial(attention_forward, len(first), given),
        grid_spec=pltpu.PrefetchScalarGridSpec(
            num_scalar_prefetch=2,
            grid=(steps,),
            in_specs=in_specs,
            out_specs=out_specs,
            scratch_shapes=scratch,
        ),
        out_shape=out_shape,
        compiler_params=params(32),
        cost_estimate=pl.CostEstimate(flops=flops, bytes_accessed=16 << 20, transcendentals=0),
        name="attention_forward",
    )(meta, lengths, *args)


def feed_kernel(count, given, meta, labels, tasks, *refs):
    pre_one_ref, out_grad_ref, norm, classes = refs[:4]
    step = pl.program_id(0)
    last = pl.num_programs(0) - 1
    if given:
        wup, wdown, bias = refs[4:7]
        output_ref, back_ref, norm_grad, class_grad, bias_grad, up_grad, down_grad = refs[7:14]
        act_keep, slope_keep, grad_keep = refs[14:]
    else:
        own_up, own_down, own_bias = refs[4:7]
        bias_refs = refs[7 : 7 + count]
        first_refs = refs[7 + count : 7 + 2 * count]
        moved = refs[7 + 2 * count : 16 + 2 * count]
        output_ref, back_ref, norm_grad, class_grad, bias_grad, keep, send = refs[16 + 2 * count : 23 + 2 * count]
        act_keep, slope_keep, grad_keep, wup, wdown, bias, up_grad, down_grad = refs[23 + 2 * count :]
    width = norm.shape[1]
    here = meta[0]

    @pl.when(step == 0)
    def start():
        norm_grad[...] = jnp.zeros_like(norm_grad)
        class_grad[...] = jnp.zeros_like(class_grad)
        bias_grad[...] = jnp.zeros_like(bias_grad)
        up_grad[...] = jnp.zeros_like(up_grad)
        down_grad[...] = jnp.zeros_like(down_grad)

    if not given:

        @pl.when(step == 0)
        def unpack():
            for r in range(4):
                wup[here, :, r * LANES : (r + 1) * LANES] = own_up[pl.ds(r, width, stride=4), :].astype(LOW)
                bias[here, 0:1, r * LANES : (r + 1) * LANES] = own_bias[2 + r : 3 + r, :]
            wdown[here] = own_down[...].astype(LOW)
            for j in range(1, count + 1):
                piece = bias_refs[j - 1]
                base = piece.shape[0] - 6
                for r in range(4):
                    bias[here ^ j, 0:1, r * LANES : (r + 1) * LANES] = piece[base + r : base + r + 1, :]
            rows = width // 8
            for place, shard, take in gathered(meta, moved, first_refs):
                for r in range(4):
                    wup[shard, at(place * rows, rows), r * LANES : (r + 1) * LANES] = take(r, rows, 4).astype(LOW)
                for b in range(width // LANES):
                    wdown[shard, at(place * rows, rows), b * LANES : (b + 1) * LANES] = take(
                        4 * rows + b * rows, rows
                    ).astype(LOW)

    shards = wup.shape[0]
    hat_one, scale_one = centred_parts(pre_one_ref[...])
    hidden = hat_one * norm[1:2, :] + norm[2:3, :]
    low_hidden = hidden.astype(LOW)
    ffn = None
    for s in range(shards):
        act, slope = gelu_parts(mul(low_hidden, wup[s]) + bias[s, 0:1, :])
        low_act = act.astype(LOW)
        act_keep[s] = low_act
        slope_keep[s] = slope
        term = mul(low_act, wdown[s])
        ffn = term if ffn is None else ffn + term
    hat_two, scale_two = centred_parts(hidden + ffn + norm[3:4, :])
    output = hat_two * norm[4:5, :] + norm[5:6, :]
    output_ref[...] = output

    grad = out_grad_ref[...]
    per_step = grad.shape[0] // LANES
    row = lax.broadcasted_iota(jnp.int32, grad.shape, 0)
    class_row = lax.broadcasted_iota(jnp.int32, (classes.shape[1], 1), 0)
    for t in range(per_step):
        task = tasks[step * per_step + t]
        table = classes[task]
        first_row = output[t * LANES : t * LANES + 1, :]
        logits = jnp.sum(table * first_row, -1, keepdims=True)
        logit_exp = jnp.exp(logits - jnp.max(logits, 0, keepdims=True))
        class_prob = logit_exp / jnp.sum(logit_exp, 0, keepdims=True)
        logit_grad = class_prob - (class_row == labels[step * per_step + t]).astype(F32)
        class_grad[task] += logit_grad * first_row
        grad = jnp.where(row == t * LANES, grad + jnp.sum(logit_grad * table, 0, keepdims=True), grad)

    norm_grad[4:5, :] += jnp.sum(grad * hat_two, 0, keepdims=True)
    norm_grad[5:6, :] += jnp.sum(grad, 0, keepdims=True)
    back_two = norm_back(grad, hat_two, scale_two, norm[4:5, :])
    norm_grad[3:4, :] += jnp.sum(back_two, 0, keepdims=True)
    low_back = back_two.astype(LOW)
    back_hidden = back_two
    for s in range(shards):
        up_back = (mul(low_back, wdown[s], 1, 1) * slope_keep[s]).astype(LOW)
        grad_keep[s] = up_back
        back_hidden = back_hidden + mul(up_back, wup[s], 1, 1)
    own_back = grad_keep[here]
    down_grad[...] += mul(act_keep[here], low_back, 0, 0)
    up_grad[...] += mul(low_hidden, own_back, 0, 0)
    bias_grad[0:1, :] += jnp.sum(own_back.astype(F32), 0, keepdims=True)

    norm_grad[1:2, :] += jnp.sum(back_hidden * hat_one, 0, keepdims=True)
    norm_grad[2:3, :] += jnp.sum(back_hidden, 0, keepdims=True)
    back_one = norm_back(back_hidden, hat_one, scale_one, norm[1:2, :])
    norm_grad[0:1, :] += jnp.sum(back_one, 0, keepdims=True)
    back_ref[...] = back_one

    if not given:

        def give_up(ref):
            for r in range(4):
                ref[pl.ds(r, width, stride=4), :] = up_grad[:, r * LANES : (r + 1) * LANES]

        def give_down(ref):
            for b in range(width // LANES):
                ref[b * 4 * LANES : (b + 1) * 4 * LANES, :] = down_grad[:, b * LANES : (b + 1) * LANES]

        @pl.when((step == last) & (meta[2] == 0))
        def give_first():
            give_up(keep)
            give_down(send)

        @pl.when((step == last) & (meta[2] == 1))
        def give_second():
            give_up(send)
            give_down(keep)


def run_feed(meta, labels, tasks, pre_one, out_grad, norm, classes, weights, biases, first, moved, given):
    rows, width = pre_one.shape
    steps = rows // BLOCK
    if given:
        shards, _, hidden = weights[0].shape
    else:
        shards, hidden = len(first) + 1, 4 * LANES
    args = (pre_one, out_grad, norm, classes) + tuple(weights) + tuple(biases) + tuple(first) + tuple(moved)
    by_rows = pl.BlockSpec((BLOCK, width), lambda i, *_: (i, 0))
    in_specs = [by_rows, by_rows] + [whole(a) for a in args[2:]]
    fixed = [shape((8, width)), shape(classes.shape), shape((8, hidden))]
    scratch = [
        pltpu.VMEM((shards, BLOCK, hidden), LOW),
        pltpu.VMEM((shards, BLOCK, hidden), F32),
        pltpu.VMEM((shards, BLOCK, hidden), LOW),
    ]
    if given:
        fixed += [shape((width, hidden)), shape((hidden, width))]
    else:
        half = hidden * width // LANES
        fixed += [pltpu.HBM((half, LANES), F32), pltpu.HBM((half, LANES), F32)]
        scratch += [
            pltpu.VMEM((shards, width, hidden), LOW),
            pltpu.VMEM((shards, hidden, width), LOW),
            pltpu.VMEM((shards, 8, hidden), F32),
            pltpu.VMEM((width, hidden), F32),
            pltpu.VMEM((hidden, width), F32),
        ]
    flops = 2 * rows * width * hidden * (4 * shards + 2)
    return pl.pallas_call(
        functools.partial(feed_kernel, len(first), given),
        grid_spec=pltpu.PrefetchScalarGridSpec(
            num_scalar_prefetch=3,
            grid=(steps,),
            in_specs=in_specs,
            out_specs=[by_rows, by_rows] + [whole(f) for f in fixed],
            scratch_shapes=scratch,
        ),
        out_shape=[pltpu.HBM((rows, width), F32), pltpu.HBM((rows, width), F32)] + fixed,
        compiler_params=params(44),
        cost_estimate=pl.CostEstimate(flops=4 * flops, bytes_accessed=20 << 20, transcendentals=0),
        name="feed_both",
    )(meta, labels, tasks, *args)


def pairs_back(items, masks):
    wide = [stacked(back, masks) for _, _, back in items]
    prob_back = [mul(w, qkv[:, 2 * LANES :], 1, 1) for w, (qkv, _, _) in zip(wide, items)]
    value_back = [mul(prob.astype(LOW), w, 0, 0).astype(LOW) for w, (_, prob, _) in zip(wide, items)]
    inner = [jnp.sum(prob * b, -1, keepdims=True) for b, (_, prob, _) in zip(prob_back, items)]
    raw = [
        (prob * (b - n) * (1.0 / math.sqrt(HEAD_DIM))).astype(LOW) for b, n, (_, prob, _) in zip(prob_back, inner, items)
    ]
    query_back = [
        mul(side_by_side(r, LANES), stacked(qkv[:, LANES : 2 * LANES], masks)).astype(LOW)
        for r, (qkv, _, _) in zip(raw, items)
    ]
    key_back = [mul(r, stacked(qkv[:, :LANES], masks), 0, 0).astype(LOW) for r, (qkv, _, _) in zip(raw, items)]
    return zip(query_back, key_back, value_back)


def groups_back(low_back, sources, masks):
    seqs = low_back.shape[0] // LANES
    parts = [slice(t * LANES, (t + 1) * LANES) for t in range(seqs)]
    backs = [mul(low_back, wout, 1, 1).astype(LOW) for _, _, wout, _ in sources]
    for t, part in enumerate(parts):
        items = [(qkv[part, :], prob[t], back[part]) for (qkv, prob, _, _), back in zip(sources, backs)]
        for source, grads in zip(sources, pairs_back(items, masks)):
            for j, grad in enumerate(grads):
                source[3][part, j * LANES : (j + 1) * LANES] = grad


def own_kernel(given, meta, back_ref, tokens, qkv, prob, context, wout, *refs):
    if given:
        grads, qkv_grad, out_grad, split_grad = refs
    else:
        norm_grad, class_grad, up_bias, grads, keep, send, qkv_grad, out_grad, split_grad, packed = refs
    step = pl.program_id(0)
    last = pl.num_programs(0) - 1

    @pl.when(step == 0)
    def start():
        qkv_grad[...] = jnp.zeros_like(qkv_grad)
        out_grad[...] = jnp.zeros_like(out_grad)
        split_grad[...] = jnp.zeros_like(split_grad)

    masks = head_masks()
    low_back = back_ref[...].astype(LOW)

    groups_back(low_back, [(qkv.at[0], prob.at[0], wout[...], grads)], masks)
    out_grad[...] += mul(context[...], low_back, 0, 0)
    both = grads[...]
    qkv_grad[...] += mul(tokens[...], both, 0, 0)
    split_grad[0:1, :] += jnp.sum(both[:, :LANES].astype(F32), 0, keepdims=True)
    split_grad[1:2, :] += jnp.sum(both[:, 2 * LANES :].astype(F32), 0, keepdims=True)

    if not given:
        width = back_ref.shape[1]
        blocks = width // LANES

        @pl.when(step == last)
        def fill():
            for j in range(3):
                packed[j * width : (j + 1) * width, :] = qkv_grad[:, j * LANES : (j + 1) * LANES]
            base = 3 * width
            for b in range(blocks):
                packed[base + b * LANES : base + (b + 1) * LANES, :] = out_grad[:, b * LANES : (b + 1) * LANES]
            base += width
            packed[base:, :] = jnp.zeros((packed.shape[0] - base, LANES), F32)
            packed[base : base + 2, :] = split_grad[0:2, :]
            for r in range(4):
                packed[base + 2 + r : base + 3 + r, :] = up_bias[0:1, r * LANES : (r + 1) * LANES]
            base += 8
            for b in range(blocks):
                packed[base + 8 * b : base + 8 * b + 6, :] = norm_grad[0:6, b * LANES : (b + 1) * LANES]
            base += 8 * blocks
            tasks, kinds, _ = class_grad.shape
            each = small_rows(tasks, kinds)
            for b in range(blocks):
                for t in range(tasks):
                    row = base + each * b + kinds * t
                    packed[row : row + kinds, :] = class_grad[t, :, b * LANES : (b + 1) * LANES]

        half = keep.shape[0]

        @pl.when((step == last) & (meta[2] == 0))
        def give_first():
            keep[...] = packed[:half, :]
            send[...] = packed[half:, :]

        @pl.when((step == last) & (meta[2] == 1))
        def give_second():
            keep[...] = packed[half:, :]
            send[...] = packed[:half, :]


def small_rows(tasks, kinds):
    return -(-tasks * kinds // 8) * 8


def packed_rows(width, tasks, kinds):
    blocks = width // LANES
    rows = 4 * width + 8 + 8 * blocks + blocks * small_rows(tasks, kinds)
    return -(-rows // 64) * 64


def run_own(meta, back, tokens, qkv, prob, context, wout, smalls, given):
    rows, width = back.shape
    steps = rows // BLOCK
    seqs = BLOCK // LANES
    heads = LANES // HEAD_DIM
    by_rows = pl.BlockSpec((BLOCK, width), lambda i, m: (i, 0))
    in_specs = [
        by_rows,
        by_rows,
        pl.BlockSpec((1, BLOCK, 3 * LANES), lambda i, m: (m[3], i, 0)),
        pl.BlockSpec((1, seqs, heads * LANES, LANES), lambda i, m: (m[3], i, 0, 0)),
        pl.BlockSpec((BLOCK, LANES), lambda i, m: (i, m[3])),
        pl.BlockSpec((LANES, width), lambda i, m: (m[3], 0)),
    ] + [whole(s) for s in smalls]
    out_shape = [pltpu.HBM((rows, 3 * LANES), LOW)]
    out_specs = [pl.BlockSpec((BLOCK, 3 * LANES), lambda i, m: (i, 0))]
    sums = [shape((width, 3 * LANES)), shape((LANES, width)), shape((8, LANES))]
    scratch = []
    if given:
        fixed = sums
    else:
        count = packed_rows(width, *smalls[1].shape[:2])
        fixed = [pltpu.HBM((count // 2, LANES), F32)] * 2
        scratch = [pltpu.VMEM(s.shape, F32) for s in sums] + [pltpu.VMEM((count, LANES), F32)]
    return pl.pallas_call(
        functools.partial(own_kernel, given),
        grid_spec=pltpu.PrefetchScalarGridSpec(
            num_scalar_prefetch=1,
            grid=(steps,),
            in_specs=in_specs,
            out_specs=out_specs + [whole(f) for f in fixed],
            scratch_shapes=scratch,
        ),
        out_shape=out_shape + fixed,
        compiler_params=params(28),
        cost_estimate=pl.CostEstimate(flops=4 << 30, bytes_accessed=8 << 20, transcendentals=0),
        name="attention_own",
    )(meta, in_hbm(back), tokens, in_hbm(qkv), in_hbm(prob), in_hbm(context), wout, *smalls)


def rest_kernel(meta, back_ref, qkv, prob, wout, wqkv, own, *refs):
    input_grad, grads = refs[-2:]
    group = meta[3]
    groups = qkv.shape[0]
    back = back_ref[...]
    grads[group] = own[...]
    sources = []
    for r in range(1, groups):
        g = group ^ r
        sources.append((qkv.at[g], prob.at[g], wout[at(g * LANES, LANES), :], grads.at[g]))
    groups_back(back.astype(LOW), sources, head_masks())
    total = None
    for g in range(groups):
        term = mul(grads[g], wqkv[g], 1, 1)
        total = term if total is None else total + term
    input_grad[...] = back + total


def run_rest(meta, back, qkv, prob, wout, wqkv, own, block, before=None):
    rows, width = back.shape
    groups = width // LANES
    few = BLOCK // 2
    seqs = few // LANES
    heads = LANES // HEAD_DIM
    by_rows = pl.BlockSpec((few, width), lambda i, m: (2 * block + i, 0))
    held = () if before is None else (before,)
    return pl.pallas_call(
        rest_kernel,
        grid_spec=pltpu.PrefetchScalarGridSpec(
            num_scalar_prefetch=1,
            grid=(2,),
            in_specs=[
                by_rows,
                pl.BlockSpec((groups, few, 3 * LANES), lambda i, m: (0, 2 * block + i, 0)),
                pl.BlockSpec((groups, seqs, heads * LANES, LANES), lambda i, m: (0, 2 * block + i, 0, 0)),
                whole(wout),
                whole(wqkv),
                pl.BlockSpec((few, 3 * LANES), lambda i, m: (2 * block + i, 0)),
            ]
            + [pl.BlockSpec(memory_space=pl.ANY)] * len(held),
            out_specs=by_rows,
            scratch_shapes=[pltpu.VMEM((groups, few, 3 * LANES), LOW)],
        ),
        out_shape=shape((rows, width)),
        input_output_aliases={7: 0} if held else {},
        compiler_params=params(28),
        cost_estimate=pl.CostEstimate(flops=68719476736, bytes_accessed=1 << 10, transcendentals=0),
        name="attention_rest",
    )(meta, in_hbm(back), in_hbm(qkv), in_hbm(prob), wout, wqkv, in_hbm(own), *held)


def places_of(meta):
    return [(meta[2] ^ half) * 4 + (meta[4] ^ bits) for half in range(2) for bits in range(4)]


def halves_of(refs):
    each = len(refs) // 2
    parts = []
    for half in range(2):
        own = refs[half * each : (half + 1) * each]
        few = own[0].shape[0] // 2
        parts += [(ref.at[:few], ref.at[few:]) for ref in own[: 4 if each == 4 else 3]]
        parts += [tuple(own[3:])] if each == 5 else []
    return parts


def squares_kernel(split_rows, count, meta, *refs):
    parts, before, out, sums = refs[:count], refs[count:-2], refs[-2], refs[-1]
    rows = 2 * halves_of(parts)[0][0].shape[0]
    row = lax.broadcasted_iota(jnp.int32, (rows // 2, LANES), 0)
    for place, pieces in zip(places_of(meta), halves_of(parts)):
        split = shared = 0.0
        for n, piece in enumerate(pieces):
            square = piece[...] * piece[...]
            if split_rows < 8 * rows:
                is_split = row < split_rows - place * rows - n * (rows // 2)
                shared = shared + jnp.sum(jnp.where(is_split, 0.0, square), 0, keepdims=True)
                square = jnp.where(is_split, square, 0.0)
            split = split + jnp.sum(square, 0, keepdims=True)
        sums[place, 0:1, :] = split
        if split_rows < 8 * rows:
            sums[place, 1:2, :] = shared
    out[...] = jnp.zeros_like(out)
    for kind in range(1 if split_rows == 8 * rows else 2):
        total = before[0][kind : kind + 1, :] if before else None
        for n in range(8):
            term = sums[n, kind : kind + 1, :]
            total = term if total is None else total + term
        out[kind : kind + 1, :] = total


def squares_of(meta, parts, split_rows=None, before=()):
    out = shape((8, LANES))
    return pl.pallas_call(
        functools.partial(squares_kernel, split_rows or 8 * parts[0].shape[0], len(parts)),
        grid_spec=pltpu.PrefetchScalarGridSpec(
            num_scalar_prefetch=1,
            grid=(1,),
            in_specs=[whole(p) for p in tuple(parts) + before],
            out_specs=whole(out),
            scratch_shapes=[pltpu.VMEM((8, 8, LANES), F32)],
        ),
        out_shape=out,
        compiler_params=params(16),
        name="squares",
    )(meta, *parts, *before)


def adam_kernel(count, meta, squares, *refs):
    moved = refs[:count]
    a_parts, b_parts = refs[count : count + 8], refs[count + 8 : count + 18]
    refs = refs[count + 18 :]
    states, norm_ref, targets = list(refs[:21]), refs[21], refs[22:43]
    sums, a_full, fetched, done = refs[43:47]
    outs, weights = refs[47:68], refs[68:]
    fetch = [pltpu.make_async_copy(states[3 * n + 2], weights[n], fetched.at[n]) for n in range(4)]
    for copy in fetch:
        copy.start()
    for n in range(4):
        states[3 * n + 2] = weights[n]
    rows = a_parts[0].shape[0]
    for place, part in zip(places_of(meta), a_parts):
        a_full[pl.ds(pl.multiple_of(place * rows, 8), rows), :] = part[...]
    sums[meta[0]] = squares[...]
    for r in range(1, count + 1):
        sums[meta[0] ^ r] = moved[r - 1][...]
    total = sums[0]
    for s in range(1, count + 1):
        total = total + sums[s]
    all_squares = jnp.sum(total[0:1, :], -1, keepdims=True) + jnp.sum(squares[1:2, :], -1, keepdims=True)
    grad_norm = jnp.sqrt(all_squares)
    norm_ref[...] = grad_norm
    factor = jnp.minimum(1.0, clip_at / (grad_norm + 1e-06))
    width = states[5 * 3].shape[1]
    blocks = width // LANES
    copies = []

    def update(index, where, grad, with_decay):
        first, second, weight = (states[3 * index + j][where] for j in range(3))
        for j, value in enumerate(adam_math(weight, first, second, grad, factor, with_decay)):
            outs[3 * index + j][where] = value

    def give(index, where=None):
        for j in range(3 * index, 3 * index + 3):
            source, target = outs[j], targets[j]
            if where is not None:
                source, target = source.at[where], target.at[where]
            copies.append(pltpu.make_async_copy(source, target, done.at[len(copies)]))
            copies[-1].start()

    pieces = halves_of(b_parts)
    few = width // 2
    lower = meta[2] == 0
    every = slice(None)
    fetch[2].wait()
    for bits in range(4):
        place = meta[4] ^ bits
        for n in range(2):
            grad = jnp.where(lower, pieces[bits][n][...], pieces[4 + bits][n][...])
            update(2, (at(place * width + n * few, few), every), grad, True)
        give(2, (at(place * width, width), every))
    fetch[3].wait()
    for bits in range(4):
        lanes = at((meta[4] ^ bits) * LANES, LANES)
        for n in range(2):
            grad = jnp.where(lower, pieces[4 + bits][n][...], pieces[bits][n][...])
            update(3, (slice(n * few, (n + 1) * few), lanes), grad, True)
        give(3, (every, lanes))
    fetch[0].wait()
    for j in range(3):
        update(0, (j,), a_full[j * width : (j + 1) * width, :], True)
        give(0, j)
    fetch[1].wait()
    base = 3 * width
    for b in range(blocks):
        lanes = slice(b * LANES, (b + 1) * LANES)
        update(1, (every, lanes), a_full[base + b * LANES : base + (b + 1) * LANES, :], True)
    give(1)
    base += width
    update(4, (every, every), a_full[base : base + 6, :], False)
    give(4)
    base += 8
    for b in range(blocks):
        lanes = slice(b * LANES, (b + 1) * LANES)
        update(5, (every, lanes), a_full[base + 8 * b : base + 8 * b + 6, :], False)
    give(5)
    base += 8 * blocks
    tasks, kinds, _ = states[6 * 3].shape
    each = small_rows(tasks, kinds)
    for b in range(blocks):
        lanes = slice(b * LANES, (b + 1) * LANES)
        for t in range(tasks):
            row = base + each * b + kinds * t
            update(6, (t, every, lanes), a_full[row : row + kinds, :], True)
    give(6)
    for copy in copies:
        copy.wait()


def run_adam(meta, squares, moved, a_parts, b_parts, states):
    held = pl.BlockSpec(memory_space=pltpu.HBM)
    here = pl.BlockSpec(memory_space=pltpu.VMEM)
    blocks = states[-4].shape[1] // LANES
    args = (squares,) + tuple(moved) + tuple(a_parts) + tuple(b_parts)
    late = [n < 12 and n % 3 == 2 for n in range(len(states))]
    return pl.pallas_call(
        functools.partial(adam_kernel, len(moved)),
        in_specs=[pl.BlockSpec(memory_space=pltpu.SMEM)]
        + [here] * len(args)
        + [held if later else here for later in late],
        out_specs=[here] + [held] * len(states),
        out_shape=[shape((1, 1))] + [shape(s.shape) for s in states],
        scratch_shapes=[
            pltpu.VMEM((len(moved) + 1, 8, LANES), F32),
            pltpu.VMEM((8 * a_parts[0].shape[0], LANES), F32),
            pltpu.SemaphoreType.DMA((4,)),
            pltpu.SemaphoreType.DMA((6 * blocks + 3 * 3 + 3 * 4,)),
        ]
        + [pltpu.VMEM(s.shape, F32) for s in states]
        + [pltpu.VMEM(s.shape, F32) for s, later in zip(states, late) if later],
        compiler_params=params(24),
        name="adam",
    )(meta, *args, *(in_hbm(s) if later else s if n % 3 == 2 else in_vmem(s) for n, (s, later) in enumerate(zip(states, late))))


def shares(mesh, *args):
    fast = (
        mesh.shape["head"] == 4
        and mesh.shape["batch"] == 4
        and mesh.shape["rep"] == 2
        and args[5].shape[2] == LANES
        and args[0].shape[0] == 2 * BLOCK
        and mesh.shape["head"] * LANES == args[0].shape[1]
    )
    return (by_permutes if fast else by_gathers)(mesh, *args)


def by_permutes(
    mesh,
    tokens_in,
    out_grad,
    lengths,
    labels,
    task_id,
    qkv_weight,
    qkv_first,
    qkv_second,
    out_weight,
    out_first,
    out_second,
    up_weight,
    up_first,
    up_second,
    down_weight,
    down_first,
    down_second,
    split_bias,
    split_first,
    split_second,
    norm_params,
    norm_first,
    norm_second,
    class_weight,
    class_first,
    class_second,
):
    plane = Plane(mesh)
    width = tokens_in.shape[1]
    here = lax.axis_index("head")
    batch = lax.axis_index("batch")
    rep = lax.axis_index("rep")
    quarter = (batch // 2) * 2 + rep
    meta = jnp.stack([here, batch * plane.rep + rep, batch % 2, here, quarter]).astype(jnp.int32)

    def flat_up(value):
        return value.reshape(-1, LANES)

    def flat_down(value):
        return value.reshape(-1, width)

    def flat_class(value):
        return jnp.transpose(value, (0, 2, 1))

    up_flat, down_flat, classes = flat_up(up_weight), flat_down(down_weight), flat_class(class_weight)
    a_send, b_send = pack(meta, qkv_weight, out_weight, split_bias, up_flat, down_flat)
    turns = range(1, plane.heads)
    a_first = [plane.along(a_send, r) for r in turns]
    b_first = plane.round(b_send)
    a_near = plane.spread(after(jnp.concatenate([v[:-8] for v in a_first], 0), b_first[0]))
    b_first = plane.round_on(b_first)
    a_corner = plane.corners(a_near)
    b_near = plane.spread(after(jnp.concatenate(b_first, 0), a_near))
    a_moved = plane.shared(a_near, a_corner)

    qkv, prob, context, pre_one, wqkv, wout = run_attention_forward(
        meta, lengths, tokens_in, norm_params, (qkv_weight, out_weight, split_bias), a_first, a_moved, False
    )
    b_near = after(b_near, pre_one)
    b_moved = plane.shared(b_near, plane.corners(b_near))
    output, back_one, norm_grad, class_grad, up_bias_grad, b_keep, b_give = run_feed(
        meta,
        labels,
        task_id,
        pre_one,
        out_grad,
        norm_params,
        classes,
        (up_flat, down_flat, split_bias),
        a_first,
        b_first,
        b_moved,
        False,
    )
    b_parts = plane.quarters(b_keep, b_give, quarter)
    back_one = after(back_one, b_parts)
    own, a_keep, a_give = run_own(
        meta, back_one, tokens_in, qkv, prob, context, wout, (norm_grad, class_grad, up_bias_grad), False
    )
    b_own = plane.scatter(b_parts, a_give)
    b_crossed, b_near = plane.core(b_own), plane.spread(b_own)
    a_parts = plane.quarters(a_keep, a_give, quarter)
    back_one = after(back_one, a_parts, b_crossed)
    input_grad = run_rest(meta, back_one, qkv, prob, wout, wqkv, own, 0)
    a_own = plane.scatter(a_parts, input_grad)
    b_near = after(b_near, input_grad)
    b_corner = plane.corners(b_near)
    a_crossed, a_near = plane.rejoin(a_own)
    input_grad = run_rest(meta, after(back_one, a_crossed), qkv, prob, wout, wqkv, own, 1, input_grad)
    b_near, b_corner, a_near = after((b_near, b_corner, a_near), input_grad)
    b_parts = plane.rejoin_on(b_own, b_crossed, (b_near[2], b_near[1]) + b_corner)
    a_parts = plane.rejoin_on(a_own, a_crossed, a_near)
    squares = squares_of(meta, a_parts, 4 * width + 8, (squares_of(meta, b_parts),))
    moved = tuple(plane.along(squares, r) for r in turns)
    states = (
        (qkv_first, qkv_second, qkv_weight)
        + (out_first, out_second, out_weight)
        + (flat_up(up_first), flat_up(up_second), up_flat)
        + (flat_down(down_first), flat_down(down_second), down_flat)
        + (split_first, split_second, split_bias)
        + (norm_first, norm_second, norm_params)
        + (flat_class(class_first), flat_class(class_second), classes)
    )
    grad_norm, *new = run_adam(meta, squares, moved, a_parts, b_parts, states)
    new[6:9] = [v.reshape(up_weight.shape) for v in new[6:9]]
    new[9:12] = [v.reshape(down_weight.shape) for v in new[9:12]]
    new[18:21] = [jnp.transpose(v, (0, 2, 1)) for v in new[18:21]]
    return (output, input_grad, grad_norm[0, 0]) + tuple(new)


def lower_kernel(source, target):
    target[...] = source[...].astype(LOW)


def lowered(value):
    flat = value.reshape(-1, value.shape[-1])
    out = pl.pallas_call(
        lower_kernel, out_shape=shape(flat.shape, LOW), compiler_params=params(), name="lowered"
    )(flat)
    return out.reshape(value.shape)


def by_gathers(
    mesh,
    tokens_in,
    out_grad,
    lengths,
    labels,
    task_id,
    qkv_weight,
    qkv_first,
    qkv_second,
    out_weight,
    out_first,
    out_second,
    up_weight,
    up_first,
    up_second,
    down_weight,
    down_first,
    down_second,
    split_bias,
    split_first,
    split_second,
    norm_params,
    norm_first,
    norm_second,
    class_weight,
    class_first,
    class_second,
):
    width = tokens_in.shape[1]
    cols = qkv_weight.shape[2]
    groups = width // LANES
    hidden = 4 * cols
    here = lax.axis_index("head")
    zero = jnp.zeros_like(here)
    meta = jnp.stack([here, zero, zero, here * cols // LANES, zero]).astype(jnp.int32)
    full_qkv = lax.all_gather(qkv_weight, "head", axis=2, tiled=True)
    full_out = lax.all_gather(out_weight, "head", axis=0, tiled=True)
    full_up = lax.all_gather(up_weight.reshape(width, hidden), "head", axis=0)
    full_down = lax.all_gather(down_weight.reshape(hidden, width), "head", axis=0)
    full_bias = lax.all_gather(split_bias, "head", axis=1, tiled=True)
    wqkv = full_qkv.reshape(3, width, groups, LANES).transpose(2, 1, 0, 3).reshape(groups, width, 3 * LANES)
    wqkv, wout = lowered(wqkv), lowered(full_out)
    qv_bias = jnp.pad(full_bias[:2].reshape(2, groups, LANES).transpose(1, 0, 2), ((0, 0), (0, 6), (0, 0)))
    shards = width // cols
    up_bias = full_bias[2:].reshape(4, shards, cols).transpose(1, 0, 2).reshape(shards, 1, hidden)
    up_bias = jnp.pad(up_bias, ((0, 0), (0, 7), (0, 0)))
    classes = jnp.transpose(class_weight, (0, 2, 1))

    qkv, prob, context, pre_one = run_attention_forward(
        meta, lengths, tokens_in, norm_params, (wqkv, wout, qv_bias), (), (), True
    )
    output, back_one, norm_grad, class_grad, up_bias_grad, up_grad, down_grad = run_feed(
        meta,
        labels,
        task_id,
        pre_one,
        out_grad,
        norm_params,
        classes,
        (lowered(full_up), lowered(full_down), up_bias),
        (),
        (),
        (),
        True,
    )
    own, qkv_grad, out_w_grad, split_grad = run_own(meta, back_one, tokens_in, qkv, prob, context, wout, (), True)
    input_grad = None
    for block in range(tokens_in.shape[0] // BLOCK):
        input_grad = run_rest(meta, back_one, qkv, prob, wout, wqkv, own, block, input_grad)
    start = here * cols % LANES
    qkv_grad = qkv_grad.reshape(width, 3, LANES).transpose(1, 0, 2)
    qkv_grad = lax.dynamic_slice_in_dim(qkv_grad, start, cols, 2)
    out_w_grad = lax.dynamic_slice_in_dim(out_w_grad, start, cols, 0)
    split_grad = lax.dynamic_slice_in_dim(split_grad[:2], start, cols, 1)
    split_grad = jnp.concatenate([split_grad, up_bias_grad[0].reshape(4, cols)], 0)
    summed = lax.psum(
        (
            qkv_grad,
            out_w_grad,
            up_grad.reshape(up_weight.shape),
            down_grad.reshape(down_weight.shape),
            split_grad,
            norm_grad[:6],
            jnp.transpose(class_grad, (0, 2, 1)),
        ),
        ("batch", "rep"),
    )
    split_square = lax.psum(sum(jnp.sum(v * v) for v in summed[:5]), "head")
    grad_norm = jnp.sqrt(split_square + sum(jnp.sum(v * v) for v in summed[5:]))
    factor = jnp.minimum(1.0, clip_at / (grad_norm + 1e-06))
    states = (
        (qkv_weight, qkv_first, qkv_second, True),
        (out_weight, out_first, out_second, True),
        (up_weight, up_first, up_second, True),
        (down_weight, down_first, down_second, True),
        (split_bias, split_first, split_second, False),
        (norm_params, norm_first, norm_second, False),
        (class_weight, class_first, class_second, True),
    )
    results = ()
    for grad, (weight, first, second, decay) in zip(summed, states):
        results += adam_math(weight, first, second, grad, factor, decay)
    return (output, input_grad, grad_norm) + results


def solution(mesh):
    rows = P(("batch", "rep"), None)
    seqs = P(("batch", "rep"))
    kinds = (
        (P(None, None, "head"),) * 3
        + (P("head", None),) * 3
        + (P(None, None, "head"),) * 3
        + (P(None, "head", None),) * 3
        + (P(None, "head"),) * 3
        + (P(),) * 6
    )
    return jax.shard_map(
        functools.partial(shares, mesh),
        mesh=mesh,
        in_specs=(rows, rows, seqs, seqs, seqs) + kinds,
        out_specs=(rows, rows, P()) + kinds,
        check_vma=False,
    )
```

```python
import functools
import math

import jax
import jax.numpy as jnp
from jax import lax
from jax.experimental import pallas as pl
from jax.experimental.pallas import tpu as pltpu
from jax.sharding import PartitionSpec as P

HEAD_DIM = 64
STEP = 10
LANES = 128
BLOCK = 512

F32 = jnp.float32
LOW = jnp.bfloat16

beta_one = 0.9
beta_two = 0.999
learn_rate = 0.05
vector_rate = 0.4
weight_decay = 0.01
adam_eps = 1e-08
clip_at = 1.0
norm_eps = 1e-12
masked = -1e30


def mul(left, right, left_dim=1, right_dim=0):
    return lax.dot_general(
        left, right, (((left_dim,), (right_dim,)), ((), ())), preferred_element_type=F32
    )


def whole(array):
    rank = len(array.shape)
    return pl.BlockSpec(array.shape, lambda *_: (0,) * rank, pipeline_mode=pl.Buffered(1))


def resident(array):
    return pl.BlockSpec(memory_space=pltpu.VMEM)


def params(mib=52):
    return pltpu.CompilerParams(vmem_limit_bytes=mib << 20)


def in_hbm(value):
    return pltpu.with_memory_space_constraint(value, pltpu.HBM)


def in_vmem(value):
    return pltpu.with_memory_space_constraint(value, pltpu.VMEM)


def shape(dims, kind=F32):
    return jax.ShapeDtypeStruct(tuple(dims), kind)


def centred_parts(values):
    centred = values - jnp.mean(values, -1, keepdims=True)
    spread = jnp.mean(centred * centred, -1, keepdims=True)
    scale = lax.rsqrt(spread + norm_eps)
    return centred * scale, scale


def norm_back(grad, hat, scale, gain):
    scaled = grad * gain
    inner = jnp.mean(scaled * hat, -1, keepdims=True)
    return scale * (scaled - jnp.mean(scaled, -1, keepdims=True) - hat * inner)


def gelu_parts(x):
    below = lax.erf(x * math.sqrt(0.5)) * 0.5 + 0.5
    density = jnp.exp2(x * x * (-0.5 * math.log2(math.e))) * (1.0 / math.sqrt(2.0 * math.pi))
    return x * below, below + x * density


def head_masks():
    lane = lax.broadcasted_iota(jnp.int32, (1, LANES), 1)
    return [(lane // HEAD_DIM == h).astype(LOW) for h in range(LANES // HEAD_DIM)]


def stacked(matrix, masks):
    return jnp.concatenate([matrix * m for m in masks], 0)


def side_by_side(matrix, rows):
    return jnp.concatenate([matrix[:rows], matrix[rows:]], 1)


def adam_math(weight, first, second, grad, factor, with_decay):
    clipped = grad * factor
    first_new = beta_one * first + (1.0 - beta_one) * clipped
    second_new = beta_two * second + (1.0 - beta_two) * clipped * clipped
    first_hat = first_new / (1.0 - beta_one**STEP)
    second_hat = second_new / (1.0 - beta_two**STEP)
    update = first_hat / (jnp.sqrt(second_hat) + adam_eps)
    if with_decay:
        return first_new, second_new, weight - learn_rate * (update + weight_decay * weight)
    return first_new, second_new, weight - vector_rate * update


def pairs(size, bit):
    return [(i, i ^ bit) for i in range(size)]


class Plane:
    def __init__(self, mesh):
        self.heads = mesh.shape["head"]
        self.batch = mesh.shape["batch"]
        self.rep = mesh.shape["rep"]

    def core(self, value):
        return lax.ppermute(value, "batch", pairs(self.batch, 1))

    def side(self, value):
        return lax.ppermute(value, "batch", pairs(self.batch, 2))

    def other(self, value):
        return lax.ppermute(value, "rep", pairs(self.rep, 1))

    def corner(self, value):
        return lax.ppermute(value, ("batch", "rep"), pairs(self.batch * self.rep, 2 * self.rep + 1))

    def along(self, value, bit):
        return lax.ppermute(value, "head", pairs(self.heads, bit))

    def round(self, block):
        return self.along(block, 1), self.along(block, 2), lax.ppermute(block, "head", [(1, 2), (2, 1)])

    def round_on(self, got):
        near, far, last = got
        return near, far, last + lax.ppermute(far, "head", [(1, 0), (2, 3)])

    def spread(self, block):
        return block, self.side(block), self.other(block)

    def corners(self, near):
        block, from_side, from_other = near
        half = block.shape[0] // 2
        return self.other(from_side[:half]), self.side(from_other[half:])

    def shared(self, near, corner):
        near = near + corner
        return near[1:] + tuple(self.core(v) for v in near)

    def quarters(self, keep, send, quarter, *others):
        both = keep + after(self.core(send), *others)
        rows = both.shape[0] // 4
        return tuple(lax.dynamic_slice_in_dim(both, (quarter ^ bits) * rows, rows, 0) for bits in range(4))

    def scatter(self, parts, *others):
        moved = (self.side(parts[2]), self.other(parts[1]), self.corner(parts[3]))
        moved = after(moved, *others)
        return parts[0] + moved[0] + moved[1] + moved[2]

    def rejoin(self, own):
        return self.core(own), (self.other(own), self.side(own), self.corner(own))

    def rejoin_on(self, own, crossed, near):
        return (own,) + near + (crossed,) + tuple(self.core(v) for v in near)


def after(value, *others):
    return lax.optimization_barrier((value, others))[0]


def pack_kernel(meta, qkv, out, bias, up, down, a_send, b_send, done):
    place = meta[1]
    places = 8
    rows = qkv.shape[1] // places
    few = out.shape[0] // places
    moves = [(qkv.at[j, at(place * rows, rows), :], a_send.at[j * rows : (j + 1) * rows, :]) for j in range(3)]
    base = 3 * rows
    for b in range(out.shape[1] // LANES):
        lanes = slice(b * LANES, (b + 1) * LANES)
        moves.append((out.at[at(place * few, few), lanes], a_send.at[base + b * few : base + (b + 1) * few, :]))
    moves.append((bias, a_send.at[a_send.shape[0] - 8 : a_send.shape[0] - 2, :]))
    base = up.shape[0] // places
    moves.append((up.at[at(place * base, base), :], b_send.at[:base, :]))
    few = down.shape[0] // places
    for b in range(down.shape[1] // LANES):
        lanes = slice(b * LANES, (b + 1) * LANES)
        moves.append((down.at[at(place * few, few), lanes], b_send.at[base + b * few : base + (b + 1) * few, :]))
    copies = [pltpu.make_async_copy(source, target, done.at[n]) for n, (source, target) in enumerate(moves)]
    for copy in copies:
        copy.start()
    for copy in copies:
        copy.wait()


def pack(meta, qkv, out, bias, up, down):
    places = 8
    width = out.shape[1]
    outs = [
        shape((4 * width // places + 8, LANES)),
        shape(((up.shape[0] + down.shape[0] * width // LANES) // places, LANES)),
    ]
    held = pl.BlockSpec(memory_space=pltpu.HBM)
    return pl.pallas_call(
        pack_kernel,
        grid_spec=pltpu.PrefetchScalarGridSpec(
            num_scalar_prefetch=1,
            grid=(1,),
            in_specs=[held] * 5,
            out_specs=[held] * 2,
            scratch_shapes=[pltpu.SemaphoreType.DMA((5 + 2 * (width // LANES),))],
        ),
        out_shape=outs,
        compiler_params=params(),
        name="pack",
    )(meta, *(in_hbm(v) for v in (qkv, out, bias, up, down)))


def gathered(meta, refs, first_refs):
    here, place = meta[0], meta[1]
    side, other, corner_top, corner_end = refs[:4]
    far = refs[4:]
    groups = [
        (0, None, None),
        (4, side, None),
        (1, other, None),
        (5, corner_top, corner_end),
        (2, far[0], None),
        (6, far[1], None),
        (3, far[2], None),
        (7, far[3], far[4]),
    ]
    for bits, top, end in groups:
        for r in range(1, len(first_refs) + 1):

            def take(row, count, stride=1, top=top, end=end, r=r, bits=bits):
                def read(ref, start):
                    return ref[pl.ds(start, count, stride=stride), :] if stride > 1 else ref[start : start + count, :]

                if bits == 0:
                    return read(first_refs[r - 1], row)
                share = top.shape[0] // (len(first_refs) if end is None else 1)
                if end is None:
                    return read(top, (r - 1) * share + row)
                total = top.shape[0] + end.shape[0]
                start = (r - 1) * (total // len(first_refs)) + row
                if start < top.shape[0]:
                    return read(top, start)
                return read(end, start - top.shape[0])

            yield place ^ bits, here ^ r, take


def at(start, size):
    return pl.ds(pl.multiple_of(start, size), size)


def attention_forward(count, given, meta, lengths, *refs):
    tokens, norm = refs[0], refs[1]
    step = pl.program_id(0)
    if given:
        wqkv, wout, bias = refs[2:5]
        qkv_out, prob_out, context_out, pre_out = refs[5:]
    else:
        own_qkv, own_out, own_bias = refs[2:5]
        first_refs = refs[5 : 5 + count]
        moved = refs[5 + count : 14 + count]
        qkv_out, prob_out, context_out, pre_out, wqkv, wout, bias = refs[14 + count :]
    width = norm.shape[1]

    if not given:

        @pl.when(step == 0)
        def unpack():
            here = meta[0]
            for j in range(3):
                wqkv[here, :, j * LANES : (j + 1) * LANES] = own_qkv[j].astype(LOW)
            wout[at(here * LANES, LANES), :] = own_out[...].astype(LOW)
            bias[here, : own_bias.shape[0], :] = own_bias[...]
            for r in range(1, count + 1):
                piece = first_refs[r - 1]
                bias[here ^ r] = piece[piece.shape[0] - 8 :, :]
            places = 8
            rows = width // places
            few = LANES // places
            for place, shard, take in gathered(meta, moved, first_refs):
                for j in range(3):
                    wqkv[shard, at(place * rows, rows), j * LANES : (j + 1) * LANES] = take(j * rows, rows).astype(LOW)
                for b in range(width // LANES):
                    wout[at(shard * LANES + place * few, few), b * LANES : (b + 1) * LANES] = take(
                        3 * rows + b * few, few
                    ).astype(LOW)

    rows_in = tokens[...]
    groups = wqkv.shape[0]
    masks = head_masks()
    seq_len = LANES
    per_step = rows_in.shape[0] // seq_len
    heads = len(masks)
    col = lax.broadcasted_iota(jnp.int32, (heads * seq_len, seq_len), 1)
    for g in range(groups):
        projected = mul(rows_in, wqkv[g])
        query = (projected[:, :LANES] + bias[g, 0:1, :]).astype(LOW)
        key = projected[:, LANES : 2 * LANES].astype(LOW)
        value = (projected[:, 2 * LANES :] + bias[g, 1:2, :]).astype(LOW)
        qkv_out[g, :, :LANES] = query
        qkv_out[g, :, LANES : 2 * LANES] = key
        qkv_out[g, :, 2 * LANES :] = value
        for t in range(per_step):
            part = slice(t * seq_len, (t + 1) * seq_len)
            scores = mul(stacked(query[part], masks), key[part], 1, 1) * (1.0 / math.sqrt(HEAD_DIM))
            scores = jnp.where(col < lengths[step * per_step + t], scores, masked)
            exponent = jnp.exp(scores - jnp.max(scores, -1, keepdims=True))
            prob = exponent * (1.0 / jnp.sum(exponent, -1, keepdims=True))
            prob_out[g, t] = prob
            low_prob = side_by_side(prob.astype(LOW), seq_len)
            context_out[part, g * LANES : (g + 1) * LANES] = mul(low_prob, stacked(value[part], masks)).astype(LOW)
    attn = mul(context_out[...], wout[...])
    pre_out[...] = rows_in.astype(F32) + attn + norm[0:1, :]


def run_attention_forward(meta, lengths, tokens, norm, weights, first, moved, given):
    rows, width = tokens.shape
    groups = width // LANES
    steps = rows // BLOCK
    seqs = BLOCK // LANES
    heads = LANES // HEAD_DIM
    args = (tokens, norm) + tuple(weights) + tuple(first) + tuple(moved)
    in_specs = [pl.BlockSpec((BLOCK, width), lambda i, *_: (i, 0))] + [(whole if given else resident)(a) for a in args[1:]]
    out_shape = [
        pltpu.HBM((groups, rows, 3 * LANES), LOW),
        pltpu.HBM((groups, rows // LANES, heads * LANES, LANES), F32),
        pltpu.HBM((rows, width), LOW),
        (shape if given else pltpu.VMEM)((rows, width), F32),
    ]
    out_specs = [
        pl.BlockSpec((groups, BLOCK, 3 * LANES), lambda i, *_: (0, i, 0)),
        pl.BlockSpec((groups, seqs, heads * LANES, LANES), lambda i, *_: (0, i, 0, 0)),
        pl.BlockSpec((BLOCK, width), lambda i, *_: (i, 0)),
        pl.BlockSpec((BLOCK, width), lambda i, *_: (i, 0)),
    ]
    scratch = []
    if not given:
        extra = [pltpu.HBM((groups, width, 3 * LANES), LOW), pltpu.HBM((width, width), LOW)]
        out_shape += extra
        out_specs += [whole(e) for e in extra]
        scratch = [pltpu.VMEM((groups, 8, LANES), F32)]
    flops = 2 * rows * width * 4 * width + 4 * rows * LANES * width * 2
    return pl.pallas_call(
        functools.partial(attention_forward, len(first), given),
        grid_spec=pltpu.PrefetchScalarGridSpec(
            num_scalar_prefetch=2,
            grid=(steps,),
            in_specs=in_specs,
            out_specs=out_specs,
            scratch_shapes=scratch,
        ),
        out_shape=out_shape,
        compiler_params=params(32),
        cost_estimate=pl.CostEstimate(flops=flops, bytes_accessed=16 << 20, transcendentals=0),
        name="attention_forward",
    )(meta, lengths, *args)


def feed_kernel(count, given, meta, labels, tasks, *refs):
    pre_one_ref, out_grad_ref, norm, classes = refs[:4]
    step = pl.program_id(0)
    last = pl.num_programs(0) - 1
    if given:
        wup, wdown, bias = refs[4:7]
        output_ref, back_ref, norm_grad, class_grad, bias_grad, up_grad, down_grad = refs[7:14]
        act_keep, slope_keep, grad_keep = refs[14:]
    else:
        own_up, own_down, own_bias = refs[4:7]
        bias_refs = refs[7 : 7 + count]
        first_refs = refs[7 + count : 7 + 2 * count]
        moved = refs[7 + 2 * count : 16 + 2 * count]
        output_ref, back_ref, norm_grad, class_grad, bias_grad, keep, send = refs[16 + 2 * count : 23 + 2 * count]
        act_keep, slope_keep, grad_keep, wup, wdown, bias, up_grad, down_grad = refs[23 + 2 * count :]
    width = norm.shape[1]
    here = meta[0]

    @pl.when(step == 0)
    def start():
        norm_grad[...] = jnp.zeros_like(norm_grad)
        class_grad[...] = jnp.zeros_like(class_grad)
        bias_grad[...] = jnp.zeros_like(bias_grad)
        up_grad[...] = jnp.zeros_like(up_grad)
        down_grad[...] = jnp.zeros_like(down_grad)

    if not given:

        @pl.when(step == 0)
        def unpack():
            for r in range(4):
                wup[here, :, r * LANES : (r + 1) * LANES] = own_up[pl.ds(r, width, stride=4), :].astype(LOW)
                bias[here, 0:1, r * LANES : (r + 1) * LANES] = own_bias[2 + r : 3 + r, :]
            wdown[here] = own_down[...].astype(LOW)
            for j in range(1, count + 1):
                piece = bias_refs[j - 1]
                base = piece.shape[0] - 6
                for r in range(4):
                    bias[here ^ j, 0:1, r * LANES : (r + 1) * LANES] = piece[base + r : base + r + 1, :]
            rows = width // 8
            for place, shard, take in gathered(meta, moved, first_refs):
                for r in range(4):
                    wup[shard, at(place * rows, rows), r * LANES : (r + 1) * LANES] = take(r, rows, 4).astype(LOW)
                for b in range(width // LANES):
                    wdown[shard, at(place * rows, rows), b * LANES : (b + 1) * LANES] = take(
                        4 * rows + b * rows, rows
                    ).astype(LOW)

    shards = wup.shape[0]
    hat_one, scale_one = centred_parts(pre_one_ref[...])
    hidden = hat_one * norm[1:2, :] + norm[2:3, :]
    low_hidden = hidden.astype(LOW)
    ffn = None
    for s in range(shards):
        act, slope = gelu_parts(mul(low_hidden, wup[s]) + bias[s, 0:1, :])
        low_act = act.astype(LOW)
        act_keep[s] = low_act
        slope_keep[s] = slope
        term = mul(low_act, wdown[s])
        ffn = term if ffn is None else ffn + term
    hat_two, scale_two = centred_parts(hidden + ffn + norm[3:4, :])
    output = hat_two * norm[4:5, :] + norm[5:6, :]
    output_ref[...] = output

    grad = out_grad_ref[...]
    per_step = grad.shape[0] // LANES
    row = lax.broadcasted_iota(jnp.int32, grad.shape, 0)
    class_row = lax.broadcasted_iota(jnp.int32, (classes.shape[1], 1), 0)
    for t in range(per_step):
        task = tasks[step * per_step + t]
        table = classes[task]
        first_row = output[t * LANES : t * LANES + 1, :]
        logits = jnp.sum(table * first_row, -1, keepdims=True)
        logit_exp = jnp.exp(logits - jnp.max(logits, 0, keepdims=True))
        class_prob = logit_exp / jnp.sum(logit_exp, 0, keepdims=True)
        logit_grad = class_prob - (class_row == labels[step * per_step + t]).astype(F32)
        class_grad[task] += logit_grad * first_row
        grad = jnp.where(row == t * LANES, grad + jnp.sum(logit_grad * table, 0, keepdims=True), grad)

    norm_grad[4:5, :] += jnp.sum(grad * hat_two, 0, keepdims=True)
    norm_grad[5:6, :] += jnp.sum(grad, 0, keepdims=True)
    back_two = norm_back(grad, hat_two, scale_two, norm[4:5, :])
    norm_grad[3:4, :] += jnp.sum(back_two, 0, keepdims=True)
    low_back = back_two.astype(LOW)
    back_hidden = back_two
    for s in range(shards):
        up_back = (mul(low_back, wdown[s], 1, 1) * slope_keep[s]).astype(LOW)
        grad_keep[s] = up_back
        back_hidden = back_hidden + mul(up_back, wup[s], 1, 1)
    own_back = grad_keep[here]
    down_grad[...] += mul(act_keep[here], low_back, 0, 0)
    up_grad[...] += mul(low_hidden, own_back, 0, 0)
    bias_grad[0:1, :] += jnp.sum(own_back.astype(F32), 0, keepdims=True)

    norm_grad[1:2, :] += jnp.sum(back_hidden * hat_one, 0, keepdims=True)
    norm_grad[2:3, :] += jnp.sum(back_hidden, 0, keepdims=True)
    back_one = norm_back(back_hidden, hat_one, scale_one, norm[1:2, :])
    norm_grad[0:1, :] += jnp.sum(back_one, 0, keepdims=True)
    back_ref[...] = back_one

    if not given:

        def give_up(ref):
            for r in range(4):
                ref[pl.ds(r, width, stride=4), :] = up_grad[:, r * LANES : (r + 1) * LANES]

        def give_down(ref):
            for b in range(width // LANES):
                ref[b * 4 * LANES : (b + 1) * 4 * LANES, :] = down_grad[:, b * LANES : (b + 1) * LANES]

        @pl.when((step == last) & (meta[2] == 0))
        def give_first():
            give_up(keep)
            give_down(send)

        @pl.when((step == last) & (meta[2] == 1))
        def give_second():
            give_up(send)
            give_down(keep)


def run_feed(meta, labels, tasks, pre_one, out_grad, norm, classes, weights, biases, first, moved, given):
    rows, width = pre_one.shape
    steps = rows // BLOCK
    if given:
        shards, _, hidden = weights[0].shape
    else:
        shards, hidden = len(first) + 1, 4 * LANES
    args = (pre_one, out_grad, norm, classes) + tuple(weights) + tuple(biases) + tuple(first) + tuple(moved)
    by_rows = pl.BlockSpec((BLOCK, width), lambda i, *_: (i, 0))
    in_specs = [by_rows, by_rows] + [(whole if given else resident)(a) for a in args[2:]]
    fixed = [shape((8, width)), shape(classes.shape), shape((8, hidden))]
    scratch = [
        pltpu.VMEM((shards, BLOCK, hidden), LOW),
        pltpu.VMEM((shards, BLOCK, hidden), F32),
        pltpu.VMEM((shards, BLOCK, hidden), LOW),
    ]
    if given:
        fixed += [shape((width, hidden)), shape((hidden, width))]
    else:
        half = hidden * width // LANES
        fixed += [pltpu.VMEM((half, LANES), F32), pltpu.VMEM((half, LANES), F32)]
        scratch += [
            pltpu.VMEM((shards, width, hidden), LOW),
            pltpu.VMEM((shards, hidden, width), LOW),
            pltpu.VMEM((shards, 8, hidden), F32),
            pltpu.VMEM((width, hidden), F32),
            pltpu.VMEM((hidden, width), F32),
        ]
    flops = 2 * rows * width * hidden * (4 * shards + 2)
    return pl.pallas_call(
        functools.partial(feed_kernel, len(first), given),
        grid_spec=pltpu.PrefetchScalarGridSpec(
            num_scalar_prefetch=3,
            grid=(steps,),
            in_specs=in_specs,
            out_specs=[by_rows, by_rows] + [whole(f) for f in fixed],
            scratch_shapes=scratch,
        ),
        out_shape=[pltpu.HBM((rows, width), F32), pltpu.HBM((rows, width), F32)] + fixed,
        compiler_params=params(36),
        cost_estimate=pl.CostEstimate(flops=4 * flops, bytes_accessed=20 << 20, transcendentals=0),
        name="feed_both",
    )(meta, labels, tasks, *args)


def pairs_back(items, masks):
    wide = [stacked(back, masks) for _, _, back in items]
    prob_back = [mul(w, qkv[:, 2 * LANES :], 1, 1) for w, (qkv, _, _) in zip(wide, items)]
    value_back = [mul(prob.astype(LOW), w, 0, 0).astype(LOW) for w, (_, prob, _) in zip(wide, items)]
    inner = [jnp.sum(prob * b, -1, keepdims=True) for b, (_, prob, _) in zip(prob_back, items)]
    raw = [
        (prob * (b - n) * (1.0 / math.sqrt(HEAD_DIM))).astype(LOW) for b, n, (_, prob, _) in zip(prob_back, inner, items)
    ]
    query_back = [
        mul(side_by_side(r, LANES), stacked(qkv[:, LANES : 2 * LANES], masks)).astype(LOW)
        for r, (qkv, _, _) in zip(raw, items)
    ]
    key_back = [mul(r, stacked(qkv[:, :LANES], masks), 0, 0).astype(LOW) for r, (qkv, _, _) in zip(raw, items)]
    return zip(query_back, key_back, value_back)


def groups_back(low_back, sources, masks):
    seqs = low_back.shape[0] // LANES
    parts = [slice(t * LANES, (t + 1) * LANES) for t in range(seqs)]
    backs = [mul(low_back, wout, 1, 1).astype(LOW) for _, _, wout, _ in sources]
    for t, part in enumerate(parts):
        items = [(qkv[part, :], prob[t], back[part]) for (qkv, prob, _, _), back in zip(sources, backs)]
        for source, grads in zip(sources, pairs_back(items, masks)):
            for j, grad in enumerate(grads):
                source[3][part, j * LANES : (j + 1) * LANES] = grad


def own_kernel(given, meta, back_ref, tokens, qkv, prob, context, wout, *refs):
    if given:
        grads, qkv_grad, out_grad, split_grad = refs
    else:
        norm_grad, class_grad, up_bias, grads, keep, send, qkv_grad, out_grad, split_grad, packed = refs
    step = pl.program_id(0)
    last = pl.num_programs(0) - 1

    @pl.when(step == 0)
    def start():
        qkv_grad[...] = jnp.zeros_like(qkv_grad)
        out_grad[...] = jnp.zeros_like(out_grad)
        split_grad[...] = jnp.zeros_like(split_grad)

    masks = head_masks()
    low_back = back_ref[...].astype(LOW)

    groups_back(low_back, [(qkv.at[0], prob.at[0], wout[...], grads)], masks)
    out_grad[...] += mul(context[...], low_back, 0, 0)
    both = grads[...]
    qkv_grad[...] += mul(tokens[...], both, 0, 0)
    split_grad[0:1, :] += jnp.sum(both[:, :LANES].astype(F32), 0, keepdims=True)
    split_grad[1:2, :] += jnp.sum(both[:, 2 * LANES :].astype(F32), 0, keepdims=True)

    if not given:
        width = back_ref.shape[1]
        blocks = width // LANES

        @pl.when(step == last)
        def fill():
            for j in range(3):
                packed[j * width : (j + 1) * width, :] = qkv_grad[:, j * LANES : (j + 1) * LANES]
            base = 3 * width
            for b in range(blocks):
                packed[base + b * LANES : base + (b + 1) * LANES, :] = out_grad[:, b * LANES : (b + 1) * LANES]
            base += width
            packed[base:, :] = jnp.zeros((packed.shape[0] - base, LANES), F32)
            packed[base : base + 2, :] = split_grad[0:2, :]
            for r in range(4):
                packed[base + 2 + r : base + 3 + r, :] = up_bias[0:1, r * LANES : (r + 1) * LANES]
            base += 8
            for b in range(blocks):
                packed[base + 8 * b : base + 8 * b + 6, :] = norm_grad[0:6, b * LANES : (b + 1) * LANES]
            base += 8 * blocks
            tasks, kinds, _ = class_grad.shape
            each = small_rows(tasks, kinds)
            for b in range(blocks):
                for t in range(tasks):
                    row = base + each * b + kinds * t
                    packed[row : row + kinds, :] = class_grad[t, :, b * LANES : (b + 1) * LANES]

        half = keep.shape[0]

        @pl.when((step == last) & (meta[2] == 0))
        def give_first():
            keep[...] = packed[:half, :]
            send[...] = packed[half:, :]

        @pl.when((step == last) & (meta[2] == 1))
        def give_second():
            keep[...] = packed[half:, :]
            send[...] = packed[:half, :]


def small_rows(tasks, kinds):
    return -(-tasks * kinds // 8) * 8


def packed_rows(width, tasks, kinds):
    blocks = width // LANES
    rows = 4 * width + 8 + 8 * blocks + blocks * small_rows(tasks, kinds)
    return -(-rows // 64) * 64


def run_own(meta, back, tokens, qkv, prob, context, wout, smalls, given):
    rows, width = back.shape
    steps = rows // BLOCK
    seqs = BLOCK // LANES
    heads = LANES // HEAD_DIM
    by_rows = pl.BlockSpec((BLOCK, width), lambda i, m: (i, 0))
    in_specs = [
        by_rows,
        by_rows,
        pl.BlockSpec((1, BLOCK, 3 * LANES), lambda i, m: (m[3], i, 0)),
        pl.BlockSpec((1, seqs, heads * LANES, LANES), lambda i, m: (m[3], i, 0, 0)),
        pl.BlockSpec((BLOCK, LANES), lambda i, m: (i, m[3])),
        pl.BlockSpec((LANES, width), lambda i, m: (m[3], 0)),
    ] + [whole(s) for s in smalls]
    out_shape = [pltpu.HBM((rows, 3 * LANES), LOW)]
    out_specs = [pl.BlockSpec((BLOCK, 3 * LANES), lambda i, m: (i, 0))]
    sums = [shape((width, 3 * LANES)), shape((LANES, width)), shape((8, LANES))]
    scratch = []
    if given:
        fixed = sums
    else:
        count = packed_rows(width, *smalls[1].shape[:2])
        fixed = [pltpu.VMEM((count // 2, LANES), F32)] * 2
        scratch = [pltpu.VMEM(s.shape, F32) for s in sums] + [pltpu.VMEM((count, LANES), F32)]
    return pl.pallas_call(
        functools.partial(own_kernel, given),
        grid_spec=pltpu.PrefetchScalarGridSpec(
            num_scalar_prefetch=1,
            grid=(steps,),
            in_specs=in_specs,
            out_specs=out_specs + [whole(f) for f in fixed],
            scratch_shapes=scratch,
        ),
        out_shape=out_shape + fixed,
        compiler_params=params(28),
        cost_estimate=pl.CostEstimate(flops=4 << 30, bytes_accessed=8 << 20, transcendentals=0),
        name="attention_own",
    )(meta, in_hbm(back), tokens, in_hbm(qkv), in_hbm(prob), in_hbm(context), in_hbm(wout), *smalls)


def rest_kernel(meta, back_ref, qkv, prob, wout, wqkv, own, *refs):
    input_grad, grads = refs[-2:]
    group = meta[3]
    groups = qkv.shape[0]
    back = back_ref[...]
    grads[group] = own[...]
    sources = []
    for r in range(1, groups):
        g = group ^ r
        sources.append((qkv.at[g], prob.at[g], wout[at(g * LANES, LANES), :], grads.at[g]))
    groups_back(back.astype(LOW), sources, head_masks())
    total = None
    for g in range(groups):
        term = mul(grads[g], wqkv[g], 1, 1)
        total = term if total is None else total + term
    input_grad[...] = back + total


def run_rest(meta, back, qkv, prob, wout, wqkv, own, block, before=None):
    rows, width = back.shape
    groups = width // LANES
    few = BLOCK // 2
    seqs = few // LANES
    heads = LANES // HEAD_DIM
    by_rows = pl.BlockSpec((few, width), lambda i, m: (2 * block + i, 0))
    held = () if before is None else (before,)
    return pl.pallas_call(
        rest_kernel,
        grid_spec=pltpu.PrefetchScalarGridSpec(
            num_scalar_prefetch=1,
            grid=(2,),
            in_specs=[
                by_rows,
                pl.BlockSpec((groups, few, 3 * LANES), lambda i, m: (0, 2 * block + i, 0)),
                pl.BlockSpec((groups, seqs, heads * LANES, LANES), lambda i, m: (0, 2 * block + i, 0, 0)),
                whole(wout),
                whole(wqkv),
                pl.BlockSpec((few, 3 * LANES), lambda i, m: (2 * block + i, 0)),
            ]
            + [pl.BlockSpec(memory_space=pl.ANY)] * len(held),
            out_specs=by_rows,
            scratch_shapes=[pltpu.VMEM((groups, few, 3 * LANES), LOW)],
        ),
        out_shape=shape((rows, width)),
        input_output_aliases={7: 0} if held else {},
        compiler_params=params(28),
        cost_estimate=pl.CostEstimate(flops=68719476736, bytes_accessed=1 << 10, transcendentals=0),
        name="attention_rest",
    )(meta, in_hbm(back), in_hbm(qkv), in_hbm(prob), in_hbm(wout), in_hbm(wqkv), in_hbm(own), *held)


def places_of(meta):
    return [(meta[2] ^ half) * 4 + (meta[4] ^ bits) for half in range(2) for bits in range(4)]


def halves_of(refs):
    each = len(refs) // 2
    parts = []
    for half in range(2):
        own = refs[half * each : (half + 1) * each]
        few = own[0].shape[0] // 2
        parts += [(ref.at[:few], ref.at[few:]) for ref in own[: 4 if each == 4 else 3]]
        parts += [tuple(own[3:])] if each == 5 else []
    return parts


def squares_kernel(split_rows, count, meta, *refs):
    out, sums = refs[-2:]
    sums[...] = jnp.zeros_like(sums)
    places = places_of(meta)
    for base, parts, limit in ((0, refs[:count], split_rows), (8, refs[count:-2], None)):
        halves = halves_of(parts)
        few = halves[0][0].shape[0]
        row = lax.broadcasted_iota(jnp.int32, (few, LANES), 0)
        for place, pieces in zip(places, halves):
            split = shared = 0.0
            for n, piece in enumerate(pieces):
                square = piece[...] * piece[...]
                if limit is not None:
                    is_split = row < limit - (2 * place + n) * few
                    shared = shared + jnp.sum(jnp.where(is_split, 0.0, square), 0, keepdims=True)
                    square = jnp.where(is_split, square, 0.0)
                split = split + jnp.sum(square, 0, keepdims=True)
            sums[base + place, 0:1, :] = split
            if limit is not None:
                sums[base + place, 1:2, :] = shared
    total = sums[0]
    for n in range(1, 16):
        total = total + sums[n]
    out[...] = total


def squares_of(meta, a_parts, b_parts, split_rows):
    out = shape((8, LANES))
    parts = tuple(a_parts) + tuple(b_parts)
    return pl.pallas_call(
        functools.partial(squares_kernel, split_rows, len(a_parts)),
        grid_spec=pltpu.PrefetchScalarGridSpec(
            num_scalar_prefetch=1,
            grid=(1,),
            in_specs=[whole(p) for p in parts],
            out_specs=whole(out),
            scratch_shapes=[pltpu.VMEM((16, 8, LANES), F32)],
        ),
        out_shape=out,
        compiler_params=params(16),
        name="squares",
    )(meta, *parts)


def ready_kernel(count, meta, *refs):
    a_parts, b_parts, weights = refs[:count], refs[count:-11], refs[-11:-7]
    a_full, b_full = refs[-7:-5]
    held, fetched = refs[-5:-1], refs[-1]
    fetch = [pltpu.make_async_copy(weights[n], held[n], fetched.at[n]) for n in range(4)]
    for copy in fetch:
        copy.start()
    for parts, full in ((a_parts, a_full), (b_parts, b_full)):
        for place, pieces in zip(places_of(meta), halves_of(parts)):
            few = pieces[0].shape[0]
            for n, piece in enumerate(pieces):
                full[pl.ds(pl.multiple_of((2 * place + n) * few, 4), few), :] = piece[...]
    for copy in fetch:
        copy.wait()


def run_ready(meta, a_parts, b_parts, weights):
    here = pl.BlockSpec(memory_space=pltpu.VMEM)
    parts = tuple(a_parts) + tuple(b_parts)
    outs = [pltpu.VMEM((8 * p[0].shape[0], LANES), F32) for p in (a_parts, b_parts)]
    outs += [pltpu.VMEM(w.shape, F32) for w in weights]
    return pl.pallas_call(
        functools.partial(ready_kernel, len(a_parts)),
        in_specs=[pl.BlockSpec(memory_space=pltpu.SMEM)]
        + [here] * len(parts)
        + [pl.BlockSpec(memory_space=pltpu.HBM)] * len(weights),
        out_specs=[here] * len(outs),
        out_shape=outs,
        scratch_shapes=[pltpu.SemaphoreType.DMA((4,))],
        compiler_params=params(16),
        cost_estimate=pl.CostEstimate(flops=64 << 30, bytes_accessed=1 << 10, transcendentals=0),
        name="ready",
    )(meta, *parts, *(in_hbm(w) for w in weights))


def adam_kernel(count, meta, squares, *refs):
    moved = refs[:count]
    a_full, b_full = refs[count : count + 2]
    refs = refs[count + 2 :]
    states, norm_ref, targets = refs[:21], refs[21], refs[22:43]
    sums, done = refs[43:45]
    outs = refs[45:]
    sums[meta[0]] = squares[...]
    for r in range(1, count + 1):
        sums[meta[0] ^ r] = moved[r - 1][...]
    total = sums[0]
    for s in range(1, count + 1):
        total = total + sums[s]
    all_squares = jnp.sum(total[0:1, :], -1, keepdims=True) + jnp.sum(squares[1:2, :], -1, keepdims=True)
    grad_norm = jnp.sqrt(all_squares)
    norm_ref[...] = grad_norm
    factor = jnp.minimum(1.0, clip_at / (grad_norm + 1e-06))
    width = states[5 * 3].shape[1]
    blocks = width // LANES
    copies = []

    def update(index, where, grad, with_decay):
        first, second, weight = (states[3 * index + j][where] for j in range(3))
        for j, value in enumerate(adam_math(weight, first, second, grad, factor, with_decay)):
            outs[3 * index + j][where] = value

    def give(index, where=None):
        for j in range(3 * index, 3 * index + 3):
            source, target = outs[j], targets[j]
            if where is not None:
                source, target = source.at[where], target.at[where]
            copies.append(pltpu.make_async_copy(source, target, done.at[len(copies)]))
            copies[-1].start()

    rows = 4 * width
    for b in range(blocks):
        part = slice(b * width, (b + 1) * width)
        update(2, (part, slice(None)), b_full[part, :], True)
        give(2, part)
    for r in range(blocks):
        part = slice(r * LANES, (r + 1) * LANES)
        for b in range(blocks):
            start = rows + b * width + r * LANES
            update(3, (part, slice(b * LANES, (b + 1) * LANES)), b_full[start : start + LANES, :], True)
        give(3, part)
    for j in range(3):
        update(0, (j,), a_full[j * width : (j + 1) * width, :], True)
        give(0, j)
    base = 3 * width
    for b in range(blocks):
        lanes = slice(b * LANES, (b + 1) * LANES)
        update(1, (slice(None), lanes), a_full[base + b * LANES : base + (b + 1) * LANES, :], True)
    give(1)
    base += width
    update(4, (slice(None), slice(None)), a_full[base : base + 6, :], False)
    give(4)
    base += 8
    for b in range(blocks):
        lanes = slice(b * LANES, (b + 1) * LANES)
        update(5, (slice(None), lanes), a_full[base + 8 * b : base + 8 * b + 6, :], False)
    give(5)
    base += 8 * blocks
    tasks, kinds, _ = states[6 * 3].shape
    each = small_rows(tasks, kinds)
    for b in range(blocks):
        lanes = slice(b * LANES, (b + 1) * LANES)
        for t in range(tasks):
            row = base + each * b + kinds * t
            update(6, (t, slice(None), lanes), a_full[row : row + kinds, :], True)
    give(6)
    for copy in copies:
        copy.wait()


def run_adam(meta, squares, moved, a_full, b_full, states):
    held = pl.BlockSpec(memory_space=pltpu.HBM)
    here = pl.BlockSpec(memory_space=pltpu.VMEM)
    blocks = states[-4].shape[1] // LANES
    args = (squares,) + tuple(moved) + (in_vmem(a_full), in_vmem(b_full))
    return pl.pallas_call(
        functools.partial(adam_kernel, len(moved)),
        in_specs=[pl.BlockSpec(memory_space=pltpu.SMEM)] + [here] * (len(args) + len(states)),
        out_specs=[here] + [held] * len(states),
        out_shape=[shape((1, 1))] + [shape(s.shape) for s in states],
        scratch_shapes=[
            pltpu.VMEM((len(moved) + 1, 8, LANES), F32),
            pltpu.SemaphoreType.DMA((6 * blocks + 3 * 3 + 3 * 4,)),
        ]
        + [pltpu.VMEM(s.shape, F32) for s in states],
        compiler_params=params(18),
        name="adam",
    )(meta, *args, *(in_vmem(s) if n < 12 or n % 3 < 2 else s for n, s in enumerate(states)))


def shares(mesh, *args):
    fast = (
        mesh.shape["head"] == 4
        and mesh.shape["batch"] == 4
        and mesh.shape["rep"] == 2
        and args[5].shape[2] == LANES
        and args[0].shape[0] == 2 * BLOCK
        and mesh.shape["head"] * LANES == args[0].shape[1]
    )
    return (by_permutes if fast else by_gathers)(mesh, *args)


def by_permutes(
    mesh,
    tokens_in,
    out_grad,
    lengths,
    labels,
    task_id,
    qkv_weight,
    qkv_first,
    qkv_second,
    out_weight,
    out_first,
    out_second,
    up_weight,
    up_first,
    up_second,
    down_weight,
    down_first,
    down_second,
    split_bias,
    split_first,
    split_second,
    norm_params,
    norm_first,
    norm_second,
    class_weight,
    class_first,
    class_second,
):
    plane = Plane(mesh)
    width = tokens_in.shape[1]
    here = lax.axis_index("head")
    batch = lax.axis_index("batch")
    rep = lax.axis_index("rep")
    quarter = (batch // 2) * 2 + rep
    meta = jnp.stack([here, batch * plane.rep + rep, batch % 2, here, quarter]).astype(jnp.int32)

    def flat_up(value):
        return value.reshape(-1, LANES)

    def flat_down(value):
        return value.reshape(-1, width)

    def flat_class(value):
        return jnp.transpose(value, (0, 2, 1))

    up_flat, down_flat, classes = flat_up(up_weight), flat_down(down_weight), flat_class(class_weight)
    a_send, b_send = pack(meta, qkv_weight, out_weight, split_bias, up_flat, down_flat)
    turns = range(1, plane.heads)
    a_first = plane.round_on(plane.round(a_send))
    b_first = plane.round(b_send)
    a_near = plane.spread(after(jnp.concatenate([v[:-8] for v in a_first], 0), b_first[0]))
    b_first = plane.round_on(b_first)
    a_corner = plane.corners(a_near)
    b_near = plane.spread(after(jnp.concatenate(b_first, 0), a_near))
    a_moved = plane.shared(a_near, a_corner)

    qkv, prob, context, pre_one, wqkv, wout = run_attention_forward(
        meta, lengths, tokens_in, norm_params, (qkv_weight, out_weight, split_bias), a_first, a_moved, False
    )
    b_near = after(b_near, pre_one)
    b_moved = plane.shared(b_near, plane.corners(b_near))
    output, back_one, norm_grad, class_grad, up_bias_grad, b_keep, b_give = run_feed(
        meta,
        labels,
        task_id,
        in_vmem(pre_one),
        out_grad,
        norm_params,
        classes,
        (up_flat, down_flat, split_bias),
        a_first,
        b_first,
        b_moved,
        False,
    )
    b_parts = plane.quarters(b_keep, b_give, quarter)
    back_one = after(back_one, b_parts)
    own, a_keep, a_give = run_own(
        meta, back_one, tokens_in, qkv, prob, context, wout, (norm_grad, class_grad, up_bias_grad), False
    )
    b_own = plane.scatter(b_parts, a_give)
    b_crossed, b_near = plane.core(b_own), plane.spread(b_own)
    a_parts = plane.quarters(a_keep, a_give, quarter)
    back_one = after(back_one, a_parts, b_crossed)
    input_grad = run_rest(meta, back_one, qkv, prob, wout, wqkv, own, 0)
    a_own = plane.scatter(a_parts, input_grad)
    b_near = after(b_near, input_grad)
    b_corner = plane.corners(b_near)
    a_crossed, a_near = plane.rejoin(a_own)
    input_grad = run_rest(meta, after(back_one, a_crossed), qkv, prob, wout, wqkv, own, 1, input_grad)
    b_near, b_corner, a_near = after((b_near, b_corner, a_near), input_grad)
    b_parts = plane.rejoin_on(b_own, b_crossed, (b_near[2], b_near[1]) + b_corner)
    a_parts = plane.rejoin_on(a_own, a_crossed, a_near)
    squares = squares_of(meta, a_parts, b_parts, 4 * width + 8)
    a_full, b_full, *held = run_ready(
        meta, after(a_parts, squares), b_parts, (qkv_weight, out_weight, up_flat, down_flat)
    )
    moved = after(tuple(plane.along(squares, r) for r in turns), b_full)
    states = (
        (qkv_first, qkv_second, held[0])
        + (out_first, out_second, held[1])
        + (flat_up(up_first), flat_up(up_second), held[2])
        + (flat_down(down_first), flat_down(down_second), held[3])
        + (split_first, split_second, split_bias)
        + (norm_first, norm_second, norm_params)
        + (flat_class(class_first), flat_class(class_second), classes)
    )
    grad_norm, *new = run_adam(meta, squares, moved, a_full, b_full, states)
    new[6:9] = [v.reshape(up_weight.shape) for v in new[6:9]]
    new[9:12] = [v.reshape(down_weight.shape) for v in new[9:12]]
    new[18:21] = [jnp.transpose(v, (0, 2, 1)) for v in new[18:21]]
    return (output, input_grad, grad_norm[0, 0]) + tuple(new)


def lower_kernel(source, target):
    target[...] = source[...].astype(LOW)


def lowered(value):
    flat = value.reshape(-1, value.shape[-1])
    out = pl.pallas_call(
        lower_kernel, out_shape=shape(flat.shape, LOW), compiler_params=params(), name="lowered"
    )(flat)
    return out.reshape(value.shape)


def by_gathers(
    mesh,
    tokens_in,
    out_grad,
    lengths,
    labels,
    task_id,
    qkv_weight,
    qkv_first,
    qkv_second,
    out_weight,
    out_first,
    out_second,
    up_weight,
    up_first,
    up_second,
    down_weight,
    down_first,
    down_second,
    split_bias,
    split_first,
    split_second,
    norm_params,
    norm_first,
    norm_second,
    class_weight,
    class_first,
    class_second,
):
    width = tokens_in.shape[1]
    cols = qkv_weight.shape[2]
    groups = width // LANES
    hidden = 4 * cols
    here = lax.axis_index("head")
    zero = jnp.zeros_like(here)
    meta = jnp.stack([here, zero, zero, here * cols // LANES, zero]).astype(jnp.int32)
    full_qkv = lax.all_gather(qkv_weight, "head", axis=2, tiled=True)
    full_out = lax.all_gather(out_weight, "head", axis=0, tiled=True)
    full_up = lax.all_gather(up_weight.reshape(width, hidden), "head", axis=0)
    full_down = lax.all_gather(down_weight.reshape(hidden, width), "head", axis=0)
    full_bias = lax.all_gather(split_bias, "head", axis=1, tiled=True)
    wqkv = full_qkv.reshape(3, width, groups, LANES).transpose(2, 1, 0, 3).reshape(groups, width, 3 * LANES)
    wqkv, wout = lowered(wqkv), lowered(full_out)
    qv_bias = jnp.pad(full_bias[:2].reshape(2, groups, LANES).transpose(1, 0, 2), ((0, 0), (0, 6), (0, 0)))
    shards = width // cols
    up_bias = full_bias[2:].reshape(4, shards, cols).transpose(1, 0, 2).reshape(shards, 1, hidden)
    up_bias = jnp.pad(up_bias, ((0, 0), (0, 7), (0, 0)))
    classes = jnp.transpose(class_weight, (0, 2, 1))

    qkv, prob, context, pre_one = run_attention_forward(
        meta, lengths, tokens_in, norm_params, (wqkv, wout, qv_bias), (), (), True
    )
    output, back_one, norm_grad, class_grad, up_bias_grad, up_grad, down_grad = run_feed(
        meta,
        labels,
        task_id,
        pre_one,
        out_grad,
        norm_params,
        classes,
        (lowered(full_up), lowered(full_down), up_bias),
        (),
        (),
        (),
        True,
    )
    own, qkv_grad, out_w_grad, split_grad = run_own(meta, back_one, tokens_in, qkv, prob, context, wout, (), True)
    input_grad = None
    for block in range(tokens_in.shape[0] // BLOCK):
        input_grad = run_rest(meta, back_one, qkv, prob, wout, wqkv, own, block, input_grad)
    start = here * cols % LANES
    qkv_grad = qkv_grad.reshape(width, 3, LANES).transpose(1, 0, 2)
    qkv_grad = lax.dynamic_slice_in_dim(qkv_grad, start, cols, 2)
    out_w_grad = lax.dynamic_slice_in_dim(out_w_grad, start, cols, 0)
    split_grad = lax.dynamic_slice_in_dim(split_grad[:2], start, cols, 1)
    split_grad = jnp.concatenate([split_grad, up_bias_grad[0].reshape(4, cols)], 0)
    summed = lax.psum(
        (
            qkv_grad,
            out_w_grad,
            up_grad.reshape(up_weight.shape),
            down_grad.reshape(down_weight.shape),
            split_grad,
            norm_grad[:6],
            jnp.transpose(class_grad, (0, 2, 1)),
        ),
        ("batch", "rep"),
    )
    split_square = lax.psum(sum(jnp.sum(v * v) for v in summed[:5]), "head")
    grad_norm = jnp.sqrt(split_square + sum(jnp.sum(v * v) for v in summed[5:]))
    factor = jnp.minimum(1.0, clip_at / (grad_norm + 1e-06))
    states = (
        (qkv_weight, qkv_first, qkv_second, True),
        (out_weight, out_first, out_second, True),
        (up_weight, up_first, up_second, True),
        (down_weight, down_first, down_second, True),
        (split_bias, split_first, split_second, False),
        (norm_params, norm_first, norm_second, False),
        (class_weight, class_first, class_second, True),
    )
    results = ()
    for grad, (weight, first, second, decay) in zip(summed, states):
        results += adam_math(weight, first, second, grad, factor, decay)
    return (output, input_grad, grad_norm) + results


def solution(mesh):
    rows = P(("batch", "rep"), None)
    seqs = P(("batch", "rep"))
    kinds = (
        (P(None, None, "head"),) * 3
        + (P("head", None),) * 3
        + (P(None, None, "head"),) * 3
        + (P(None, "head", None),) * 3
        + (P(None, "head"),) * 3
        + (P(),) * 6
    )
    return jax.shard_map(
        functools.partial(shares, mesh),
        mesh=mesh,
        in_specs=(rows, rows, seqs, seqs, seqs) + kinds,
        out_specs=(rows, rows, P()) + kinds,
        check_vma=False,
    )
```

```python
import functools
import math

import jax
import jax.numpy as jnp
from jax import lax
from jax.experimental import pallas as pl
from jax.experimental.pallas import tpu as pltpu
from jax.sharding import PartitionSpec as P

HEAD_DIM = 64
STEP = 10
LANES = 128
BLOCK = 512

F32 = jnp.float32
LOW = jnp.bfloat16

beta_one = 0.9
beta_two = 0.999
learn_rate = 0.05
vector_rate = 0.4
weight_decay = 0.01
adam_eps = 1e-08
clip_at = 1.0
norm_eps = 1e-12
masked = -1e30


def mul(left, right, left_dim=1, right_dim=0):
    return lax.dot_general(
        left, right, (((left_dim,), (right_dim,)), ((), ())), preferred_element_type=F32
    )


def whole(array):
    rank = len(array.shape)
    return pl.BlockSpec(array.shape, lambda *_: (0,) * rank, pipeline_mode=pl.Buffered(1))


def resident(array):
    return pl.BlockSpec(memory_space=pltpu.VMEM)


def params(mib=52):
    return pltpu.CompilerParams(vmem_limit_bytes=mib << 20)


def in_hbm(value):
    return pltpu.with_memory_space_constraint(value, pltpu.HBM)


def in_vmem(value):
    return pltpu.with_memory_space_constraint(value, pltpu.VMEM)


def shape(dims, kind=F32):
    return jax.ShapeDtypeStruct(tuple(dims), kind)


def centred_parts(values):
    centred = values - jnp.mean(values, -1, keepdims=True)
    spread = jnp.mean(centred * centred, -1, keepdims=True)
    scale = lax.rsqrt(spread + norm_eps)
    return centred * scale, scale


def norm_back(grad, hat, scale, gain):
    scaled = grad * gain
    inner = jnp.mean(scaled * hat, -1, keepdims=True)
    return scale * (scaled - jnp.mean(scaled, -1, keepdims=True) - hat * inner)


def gelu_parts(x):
    below = lax.erf(x * math.sqrt(0.5)) * 0.5 + 0.5
    density = jnp.exp2(x * x * (-0.5 * math.log2(math.e))) * (1.0 / math.sqrt(2.0 * math.pi))
    return x * below, below + x * density


def head_masks():
    lane = lax.broadcasted_iota(jnp.int32, (1, LANES), 1)
    return [(lane // HEAD_DIM == h).astype(LOW) for h in range(LANES // HEAD_DIM)]


def stacked(matrix, masks):
    return jnp.concatenate([matrix * m for m in masks], 0)


def side_by_side(matrix, rows):
    return jnp.concatenate([matrix[:rows], matrix[rows:]], 1)


def adam_math(weight, first, second, grad, factor, with_decay):
    clipped = grad * factor
    first_new = beta_one * first + (1.0 - beta_one) * clipped
    second_new = beta_two * second + (1.0 - beta_two) * clipped * clipped
    first_hat = first_new / (1.0 - beta_one**STEP)
    second_hat = second_new / (1.0 - beta_two**STEP)
    update = first_hat / (jnp.sqrt(second_hat) + adam_eps)
    if with_decay:
        return first_new, second_new, weight - learn_rate * (update + weight_decay * weight)
    return first_new, second_new, weight - vector_rate * update


def pairs(size, bit):
    return [(i, i ^ bit) for i in range(size)]


class Plane:
    def __init__(self, mesh):
        self.heads = mesh.shape["head"]
        self.batch = mesh.shape["batch"]
        self.rep = mesh.shape["rep"]

    def core(self, value):
        return lax.ppermute(value, "batch", pairs(self.batch, 1))

    def side(self, value):
        return lax.ppermute(value, "batch", pairs(self.batch, 2))

    def other(self, value):
        return lax.ppermute(value, "rep", pairs(self.rep, 1))

    def corner(self, value):
        return lax.ppermute(value, ("batch", "rep"), pairs(self.batch * self.rep, 2 * self.rep + 1))

    def along(self, value, bit):
        return lax.ppermute(value, "head", pairs(self.heads, bit))

    def round(self, block):
        return self.along(block, 1), self.along(block, 2), lax.ppermute(block, "head", [(1, 2), (2, 1)])

    def round_on(self, got):
        near, far, last = got
        return near, far, last + lax.ppermute(far, "head", [(1, 0), (2, 3)])

    def spread(self, block):
        return block, self.side(block), self.other(block)

    def corners(self, near):
        block, from_side, from_other = near
        half = block.shape[0] // 2
        return self.other(from_side[:half]), self.side(from_other[half:])

    def shared(self, near, corner):
        near = near + corner
        return near[1:] + tuple(self.core(v) for v in near)

    def quarters(self, keep, send, quarter, *others):
        both = keep + after(self.core(send), *others)
        rows = both.shape[0] // 4
        return tuple(lax.dynamic_slice_in_dim(both, (quarter ^ bits) * rows, rows, 0) for bits in range(4))

    def scatter(self, parts, *others):
        moved = (self.side(parts[2]), self.other(parts[1]), self.corner(parts[3]))
        moved = after(moved, *others)
        return parts[0] + moved[0] + moved[1] + moved[2]

    def rejoin(self, own):
        return self.core(own), (self.other(own), self.side(own), self.corner(own))

    def rejoin_on(self, own, crossed, near):
        return (own,) + near + (crossed,) + tuple(self.core(v) for v in near)


def after(value, *others):
    return lax.optimization_barrier((value, others))[0]


def pack_kernel(meta, qkv, out, bias, up, down, a_send, b_send, done):
    place = meta[1]
    places = 8
    rows = qkv.shape[1] // places
    few = out.shape[0] // places
    moves = [(qkv.at[j, at(place * rows, rows), :], a_send.at[j * rows : (j + 1) * rows, :]) for j in range(3)]
    base = 3 * rows
    for b in range(out.shape[1] // LANES):
        lanes = slice(b * LANES, (b + 1) * LANES)
        moves.append((out.at[at(place * few, few), lanes], a_send.at[base + b * few : base + (b + 1) * few, :]))
    moves.append((bias, a_send.at[a_send.shape[0] - 8 : a_send.shape[0] - 2, :]))
    base = up.shape[0] // places
    moves.append((up.at[at(place * base, base), :], b_send.at[:base, :]))
    few = down.shape[0] // places
    for b in range(down.shape[1] // LANES):
        lanes = slice(b * LANES, (b + 1) * LANES)
        moves.append((down.at[at(place * few, few), lanes], b_send.at[base + b * few : base + (b + 1) * few, :]))
    copies = [pltpu.make_async_copy(source, target, done.at[n]) for n, (source, target) in enumerate(moves)]
    for copy in copies:
        copy.start()
    for copy in copies:
        copy.wait()


def pack(meta, qkv, out, bias, up, down):
    places = 8
    width = out.shape[1]
    outs = [
        pltpu.VMEM((4 * width // places + 8, LANES), F32),
        pltpu.VMEM(((up.shape[0] + down.shape[0] * width // LANES) // places, LANES), F32),
    ]
    held = pl.BlockSpec(memory_space=pltpu.HBM)
    return pl.pallas_call(
        pack_kernel,
        grid_spec=pltpu.PrefetchScalarGridSpec(
            num_scalar_prefetch=1,
            grid=(1,),
            in_specs=[held] * 5,
            out_specs=[pl.BlockSpec(memory_space=pltpu.VMEM)] * 2,
            scratch_shapes=[pltpu.SemaphoreType.DMA((5 + 2 * (width // LANES),))],
        ),
        out_shape=outs,
        compiler_params=params(),
        name="pack",
    )(meta, *(in_hbm(v) for v in (qkv, out, bias, up, down)))


def gathered(meta, refs, first_refs):
    here, place = meta[0], meta[1]
    side, other, corner_top, corner_end = refs[:4]
    far = refs[4:]
    groups = [
        (0, None, None),
        (4, side, None),
        (1, other, None),
        (5, corner_top, corner_end),
        (2, far[0], None),
        (6, far[1], None),
        (3, far[2], None),
        (7, far[3], far[4]),
    ]
    for bits, top, end in groups:
        for r in range(1, len(first_refs) + 1):

            def take(row, count, stride=1, top=top, end=end, r=r, bits=bits):
                def read(ref, start):
                    return ref[pl.ds(start, count, stride=stride), :] if stride > 1 else ref[start : start + count, :]

                if bits == 0:
                    return read(first_refs[r - 1], row)
                share = top.shape[0] // (len(first_refs) if end is None else 1)
                if end is None:
                    return read(top, (r - 1) * share + row)
                total = top.shape[0] + end.shape[0]
                start = (r - 1) * (total // len(first_refs)) + row
                if start < top.shape[0]:
                    return read(top, start)
                return read(end, start - top.shape[0])

            yield place ^ bits, here ^ r, take


def at(start, size):
    return pl.ds(pl.multiple_of(start, size), size)


def attention_forward(count, given, meta, lengths, *refs):
    tokens, norm = refs[0], refs[1]
    step = pl.program_id(0)
    if given:
        wqkv, wout, bias = refs[2:5]
        qkv_out, prob_out, context_out, pre_out = refs[5:]
    else:
        own_qkv, own_out, own_bias = refs[2:5]
        first_refs = refs[5 : 5 + count]
        moved = refs[5 + count : 14 + count]
        qkv_out, prob_out, context_out, pre_out, wqkv, wout, bias = refs[14 + count :]
    width = norm.shape[1]

    if not given:

        @pl.when(step == 0)
        def unpack():
            here = meta[0]
            for j in range(3):
                wqkv[here, :, j * LANES : (j + 1) * LANES] = own_qkv[j].astype(LOW)
            wout[at(here * LANES, LANES), :] = own_out[...].astype(LOW)
            bias[here, : own_bias.shape[0], :] = own_bias[...]
            for r in range(1, count + 1):
                piece = first_refs[r - 1]
                bias[here ^ r] = piece[piece.shape[0] - 8 :, :]
            places = 8
            rows = width // places
            few = LANES // places
            for place, shard, take in gathered(meta, moved, first_refs):
                for j in range(3):
                    wqkv[shard, at(place * rows, rows), j * LANES : (j + 1) * LANES] = take(j * rows, rows).astype(LOW)
                for b in range(width // LANES):
                    wout[at(shard * LANES + place * few, few), b * LANES : (b + 1) * LANES] = take(
                        3 * rows + b * few, few
                    ).astype(LOW)

    rows_in = tokens[...]
    groups = wqkv.shape[0]
    masks = head_masks()
    seq_len = LANES
    per_step = rows_in.shape[0] // seq_len
    heads = len(masks)
    col = lax.broadcasted_iota(jnp.int32, (heads * seq_len, seq_len), 1)
    for g in range(groups):
        projected = mul(rows_in, wqkv[g])
        query = (projected[:, :LANES] + bias[g, 0:1, :]).astype(LOW)
        key = projected[:, LANES : 2 * LANES].astype(LOW)
        value = (projected[:, 2 * LANES :] + bias[g, 1:2, :]).astype(LOW)
        qkv_out[g, :, :LANES] = query
        qkv_out[g, :, LANES : 2 * LANES] = key
        qkv_out[g, :, 2 * LANES :] = value
        for t in range(per_step):
            part = slice(t * seq_len, (t + 1) * seq_len)
            scores = mul(stacked(query[part], masks), key[part], 1, 1) * (1.0 / math.sqrt(HEAD_DIM))
            scores = jnp.where(col < lengths[step * per_step + t], scores, masked)
            exponent = jnp.exp(scores - jnp.max(scores, -1, keepdims=True))
            prob = exponent * (1.0 / jnp.sum(exponent, -1, keepdims=True))
            prob_out[g, t] = prob
            low_prob = side_by_side(prob.astype(LOW), seq_len)
            context_out[part, g * LANES : (g + 1) * LANES] = mul(low_prob, stacked(value[part], masks)).astype(LOW)
    attn = mul(context_out[...], wout[...])
    pre_out[...] = rows_in.astype(F32) + attn + norm[0:1, :]


def run_attention_forward(meta, lengths, tokens, norm, weights, first, moved, given):
    rows, width = tokens.shape
    groups = width // LANES
    steps = rows // BLOCK
    seqs = BLOCK // LANES
    heads = LANES // HEAD_DIM
    args = (tokens, norm) + tuple(weights) + tuple(first) + tuple(moved)
    in_specs = [pl.BlockSpec((BLOCK, width), lambda i, *_: (i, 0))] + [(whole if given else resident)(a) for a in args[1:]]
    out_shape = [
        pltpu.HBM((groups, rows, 3 * LANES), LOW),
        pltpu.HBM((groups, rows // LANES, heads * LANES, LANES), F32),
        pltpu.HBM((rows, width), LOW),
        (shape if given else pltpu.VMEM)((rows, width), F32),
    ]
    out_specs = [
        pl.BlockSpec((groups, BLOCK, 3 * LANES), lambda i, *_: (0, i, 0)),
        pl.BlockSpec((groups, seqs, heads * LANES, LANES), lambda i, *_: (0, i, 0, 0)),
        pl.BlockSpec((BLOCK, width), lambda i, *_: (i, 0)),
        pl.BlockSpec((BLOCK, width), lambda i, *_: (i, 0)),
    ]
    scratch = []
    if not given:
        extra = [pltpu.VMEM((groups, width, 3 * LANES), LOW), pltpu.VMEM((width, width), LOW)]
        out_shape += extra
        out_specs += [whole(e) for e in extra]
        scratch = [pltpu.VMEM((groups, 8, LANES), F32)]
    flops = 2 * rows * width * 4 * width + 4 * rows * LANES * width * 2
    return pl.pallas_call(
        functools.partial(attention_forward, len(first), given),
        grid_spec=pltpu.PrefetchScalarGridSpec(
            num_scalar_prefetch=2,
            grid=(steps,),
            in_specs=in_specs,
            out_specs=out_specs,
            scratch_shapes=scratch,
        ),
        out_shape=out_shape,
        compiler_params=params(32),
        cost_estimate=pl.CostEstimate(flops=flops, bytes_accessed=16 << 20, transcendentals=0),
        name="attention_forward",
    )(meta, lengths, *args)


def feed_kernel(count, given, meta, labels, tasks, *refs):
    pre_one_ref, out_grad_ref, norm, classes = refs[:4]
    step = pl.program_id(0)
    last = pl.num_programs(0) - 1
    if given:
        wup, wdown, bias = refs[4:7]
        output_ref, back_ref, norm_grad, class_grad, bias_grad, up_grad, down_grad = refs[7:14]
        act_keep, slope_keep, grad_keep = refs[14:]
    else:
        own_up, own_down, own_bias = refs[4:7]
        bias_refs = refs[7 : 7 + count]
        first_refs = refs[7 + count : 7 + 2 * count]
        moved = refs[7 + 2 * count : 16 + 2 * count]
        output_ref, back_ref, norm_grad, class_grad, bias_grad, keep, send = refs[16 + 2 * count : 23 + 2 * count]
        act_keep, slope_keep, grad_keep, wup, wdown, bias, up_grad, down_grad = refs[23 + 2 * count :]
    width = norm.shape[1]
    here = meta[0]

    @pl.when(step == 0)
    def start():
        norm_grad[...] = jnp.zeros_like(norm_grad)
        class_grad[...] = jnp.zeros_like(class_grad)
        bias_grad[...] = jnp.zeros_like(bias_grad)
        up_grad[...] = jnp.zeros_like(up_grad)
        down_grad[...] = jnp.zeros_like(down_grad)

    if not given:

        @pl.when(step == 0)
        def unpack():
            for r in range(4):
                wup[here, :, r * LANES : (r + 1) * LANES] = own_up[pl.ds(r, width, stride=4), :].astype(LOW)
                bias[here, 0:1, r * LANES : (r + 1) * LANES] = own_bias[2 + r : 3 + r, :]
            wdown[here] = own_down[...].astype(LOW)
            for j in range(1, count + 1):
                piece = bias_refs[j - 1]
                base = piece.shape[0] - 6
                for r in range(4):
                    bias[here ^ j, 0:1, r * LANES : (r + 1) * LANES] = piece[base + r : base + r + 1, :]
            rows = width // 8
            for place, shard, take in gathered(meta, moved, first_refs):
                for r in range(4):
                    wup[shard, at(place * rows, rows), r * LANES : (r + 1) * LANES] = take(r, rows, 4).astype(LOW)
                for b in range(width // LANES):
                    wdown[shard, at(place * rows, rows), b * LANES : (b + 1) * LANES] = take(
                        4 * rows + b * rows, rows
                    ).astype(LOW)

    shards = wup.shape[0]
    hat_one, scale_one = centred_parts(pre_one_ref[...])
    hidden = hat_one * norm[1:2, :] + norm[2:3, :]
    low_hidden = hidden.astype(LOW)
    ffn = None
    for s in range(shards):
        act, slope = gelu_parts(mul(low_hidden, wup[s]) + bias[s, 0:1, :])
        low_act = act.astype(LOW)
        act_keep[s] = low_act
        slope_keep[s] = slope
        term = mul(low_act, wdown[s])
        ffn = term if ffn is None else ffn + term
    hat_two, scale_two = centred_parts(hidden + ffn + norm[3:4, :])
    output = hat_two * norm[4:5, :] + norm[5:6, :]
    output_ref[...] = output

    grad = out_grad_ref[...]
    per_step = grad.shape[0] // LANES
    row = lax.broadcasted_iota(jnp.int32, grad.shape, 0)
    class_row = lax.broadcasted_iota(jnp.int32, (classes.shape[1], 1), 0)
    for t in range(per_step):
        task = tasks[step * per_step + t]
        table = classes[task]
        first_row = output[t * LANES : t * LANES + 1, :]
        logits = jnp.sum(table * first_row, -1, keepdims=True)
        logit_exp = jnp.exp(logits - jnp.max(logits, 0, keepdims=True))
        class_prob = logit_exp / jnp.sum(logit_exp, 0, keepdims=True)
        logit_grad = class_prob - (class_row == labels[step * per_step + t]).astype(F32)
        class_grad[task] += logit_grad * first_row
        grad = jnp.where(row == t * LANES, grad + jnp.sum(logit_grad * table, 0, keepdims=True), grad)

    norm_grad[4:5, :] += jnp.sum(grad * hat_two, 0, keepdims=True)
    norm_grad[5:6, :] += jnp.sum(grad, 0, keepdims=True)
    back_two = norm_back(grad, hat_two, scale_two, norm[4:5, :])
    norm_grad[3:4, :] += jnp.sum(back_two, 0, keepdims=True)
    low_back = back_two.astype(LOW)
    back_hidden = back_two
    for s in range(shards):
        up_back = (mul(low_back, wdown[s], 1, 1) * slope_keep[s]).astype(LOW)
        grad_keep[s] = up_back
        back_hidden = back_hidden + mul(up_back, wup[s], 1, 1)
    own_back = grad_keep[here]
    down_grad[...] += mul(act_keep[here], low_back, 0, 0)
    up_grad[...] += mul(low_hidden, own_back, 0, 0)
    bias_grad[0:1, :] += jnp.sum(own_back.astype(F32), 0, keepdims=True)

    norm_grad[1:2, :] += jnp.sum(back_hidden * hat_one, 0, keepdims=True)
    norm_grad[2:3, :] += jnp.sum(back_hidden, 0, keepdims=True)
    back_one = norm_back(back_hidden, hat_one, scale_one, norm[1:2, :])
    norm_grad[0:1, :] += jnp.sum(back_one, 0, keepdims=True)
    back_ref[...] = back_one

    if not given:

        def give_up(ref):
            for r in range(4):
                ref[pl.ds(r, width, stride=4), :] = up_grad[:, r * LANES : (r + 1) * LANES]

        def give_down(ref):
            for b in range(width // LANES):
                ref[b * 4 * LANES : (b + 1) * 4 * LANES, :] = down_grad[:, b * LANES : (b + 1) * LANES]

        @pl.when((step == last) & (meta[2] == 0))
        def give_first():
            give_up(keep)
            give_down(send)

        @pl.when((step == last) & (meta[2] == 1))
        def give_second():
            give_up(send)
            give_down(keep)


def run_feed(meta, labels, tasks, pre_one, out_grad, norm, classes, weights, biases, first, moved, given):
    rows, width = pre_one.shape
    steps = rows // BLOCK
    if given:
        shards, _, hidden = weights[0].shape
    else:
        shards, hidden = len(first) + 1, 4 * LANES
    args = (pre_one, out_grad, norm, classes) + tuple(weights) + tuple(biases) + tuple(first) + tuple(moved)
    by_rows = pl.BlockSpec((BLOCK, width), lambda i, *_: (i, 0))
    in_specs = [by_rows, by_rows] + [(whole if given else resident)(a) for a in args[2:]]
    fixed = [shape((8, width)), shape(classes.shape), shape((8, hidden))]
    scratch = [
        pltpu.VMEM((shards, BLOCK, hidden), LOW),
        pltpu.VMEM((shards, BLOCK, hidden), F32),
        pltpu.VMEM((shards, BLOCK, hidden), LOW),
    ]
    if given:
        fixed += [shape((width, hidden)), shape((hidden, width))]
    else:
        half = hidden * width // LANES
        fixed += [pltpu.VMEM((half, LANES), F32), pltpu.VMEM((half, LANES), F32)]
        scratch += [
            pltpu.VMEM((shards, width, hidden), LOW),
            pltpu.VMEM((shards, hidden, width), LOW),
            pltpu.VMEM((shards, 8, hidden), F32),
            pltpu.VMEM((width, hidden), F32),
            pltpu.VMEM((hidden, width), F32),
        ]
    flops = 2 * rows * width * hidden * (4 * shards + 2)
    return pl.pallas_call(
        functools.partial(feed_kernel, len(first), given),
        grid_spec=pltpu.PrefetchScalarGridSpec(
            num_scalar_prefetch=3,
            grid=(steps,),
            in_specs=in_specs,
            out_specs=[by_rows, by_rows] + [whole(f) for f in fixed],
            scratch_shapes=scratch,
        ),
        out_shape=[pltpu.HBM((rows, width), F32), pltpu.HBM((rows, width), F32)] + fixed,
        compiler_params=params(36),
        cost_estimate=pl.CostEstimate(flops=4 * flops, bytes_accessed=20 << 20, transcendentals=0),
        name="feed_both",
    )(meta, labels, tasks, *args)


def pairs_back(items, masks):
    wide = [stacked(back, masks) for _, _, back in items]
    prob_back = [mul(w, qkv[:, 2 * LANES :], 1, 1) for w, (qkv, _, _) in zip(wide, items)]
    value_back = [mul(prob.astype(LOW), w, 0, 0).astype(LOW) for w, (_, prob, _) in zip(wide, items)]
    inner = [jnp.sum(prob * b, -1, keepdims=True) for b, (_, prob, _) in zip(prob_back, items)]
    raw = [
        (prob * (b - n) * (1.0 / math.sqrt(HEAD_DIM))).astype(LOW) for b, n, (_, prob, _) in zip(prob_back, inner, items)
    ]
    query_back = [
        mul(side_by_side(r, LANES), stacked(qkv[:, LANES : 2 * LANES], masks)).astype(LOW)
        for r, (qkv, _, _) in zip(raw, items)
    ]
    key_back = [mul(r, stacked(qkv[:, :LANES], masks), 0, 0).astype(LOW) for r, (qkv, _, _) in zip(raw, items)]
    return zip(query_back, key_back, value_back)


def groups_back(low_back, sources, masks):
    seqs = low_back.shape[0] // LANES
    parts = [slice(t * LANES, (t + 1) * LANES) for t in range(seqs)]
    backs = [mul(low_back, wout, 1, 1).astype(LOW) for _, _, wout, _ in sources]
    for t, part in enumerate(parts):
        items = [(qkv[part, :], prob[t], back[part]) for (qkv, prob, _, _), back in zip(sources, backs)]
        for source, grads in zip(sources, pairs_back(items, masks)):
            for j, grad in enumerate(grads):
                source[3][part, j * LANES : (j + 1) * LANES] = grad


def own_kernel(given, meta, back_ref, tokens, qkv, prob, context, wout, *refs):
    if given:
        grads, qkv_grad, out_grad, split_grad = refs
    else:
        norm_grad, class_grad, up_bias, grads, keep, send, qkv_grad, out_grad, split_grad, packed = refs
    step = pl.program_id(0)
    last = pl.num_programs(0) - 1

    @pl.when(step == 0)
    def start():
        qkv_grad[...] = jnp.zeros_like(qkv_grad)
        out_grad[...] = jnp.zeros_like(out_grad)
        split_grad[...] = jnp.zeros_like(split_grad)

    masks = head_masks()
    low_back = back_ref[...].astype(LOW)

    groups_back(low_back, [(qkv.at[0], prob.at[0], wout[...], grads)], masks)
    out_grad[...] += mul(context[...], low_back, 0, 0)
    both = grads[...]
    qkv_grad[...] += mul(tokens[...], both, 0, 0)
    split_grad[0:1, :] += jnp.sum(both[:, :LANES].astype(F32), 0, keepdims=True)
    split_grad[1:2, :] += jnp.sum(both[:, 2 * LANES :].astype(F32), 0, keepdims=True)

    if not given:
        width = back_ref.shape[1]
        blocks = width // LANES

        @pl.when(step == last)
        def fill():
            for j in range(3):
                packed[j * width : (j + 1) * width, :] = qkv_grad[:, j * LANES : (j + 1) * LANES]
            base = 3 * width
            for b in range(blocks):
                packed[base + b * LANES : base + (b + 1) * LANES, :] = out_grad[:, b * LANES : (b + 1) * LANES]
            base += width
            packed[base:, :] = jnp.zeros((packed.shape[0] - base, LANES), F32)
            packed[base : base + 2, :] = split_grad[0:2, :]
            for r in range(4):
                packed[base + 2 + r : base + 3 + r, :] = up_bias[0:1, r * LANES : (r + 1) * LANES]
            base += 8
            for b in range(blocks):
                packed[base + 8 * b : base + 8 * b + 6, :] = norm_grad[0:6, b * LANES : (b + 1) * LANES]
            base += 8 * blocks
            tasks, kinds, _ = class_grad.shape
            each = small_rows(tasks, kinds)
            for b in range(blocks):
                for t in range(tasks):
                    row = base + each * b + kinds * t
                    packed[row : row + kinds, :] = class_grad[t, :, b * LANES : (b + 1) * LANES]

        half = keep.shape[0]

        @pl.when((step == last) & (meta[2] == 0))
        def give_first():
            keep[...] = packed[:half, :]
            send[...] = packed[half:, :]

        @pl.when((step == last) & (meta[2] == 1))
        def give_second():
            keep[...] = packed[half:, :]
            send[...] = packed[:half, :]


def small_rows(tasks, kinds):
    return -(-tasks * kinds // 8) * 8


def packed_rows(width, tasks, kinds):
    blocks = width // LANES
    rows = 4 * width + 8 + 8 * blocks + blocks * small_rows(tasks, kinds)
    return -(-rows // 64) * 64


def run_own(meta, back, tokens, qkv, prob, context, wout, smalls, given):
    rows, width = back.shape
    steps = rows // BLOCK
    seqs = BLOCK // LANES
    heads = LANES // HEAD_DIM
    by_rows = pl.BlockSpec((BLOCK, width), lambda i, m: (i, 0))
    in_specs = [
        by_rows,
        by_rows,
        pl.BlockSpec((1, BLOCK, 3 * LANES), lambda i, m: (m[3], i, 0)),
        pl.BlockSpec((1, seqs, heads * LANES, LANES), lambda i, m: (m[3], i, 0, 0)),
        pl.BlockSpec((BLOCK, LANES), lambda i, m: (i, m[3])),
        pl.BlockSpec((LANES, width), lambda i, m: (m[3], 0)),
    ] + [whole(s) for s in smalls]
    out_shape = [pltpu.HBM((rows, 3 * LANES), LOW)]
    out_specs = [pl.BlockSpec((BLOCK, 3 * LANES), lambda i, m: (i, 0))]
    sums = [shape((width, 3 * LANES)), shape((LANES, width)), shape((8, LANES))]
    scratch = []
    if given:
        fixed = sums
    else:
        count = packed_rows(width, *smalls[1].shape[:2])
        fixed = [pltpu.VMEM((count // 2, LANES), F32)] * 2
        scratch = [pltpu.VMEM(s.shape, F32) for s in sums] + [pltpu.VMEM((count, LANES), F32)]
    return pl.pallas_call(
        functools.partial(own_kernel, given),
        grid_spec=pltpu.PrefetchScalarGridSpec(
            num_scalar_prefetch=1,
            grid=(steps,),
            in_specs=in_specs,
            out_specs=out_specs + [whole(f) for f in fixed],
            scratch_shapes=scratch,
        ),
        out_shape=out_shape + fixed,
        compiler_params=params(28),
        cost_estimate=pl.CostEstimate(flops=1073741824, bytes_accessed=1 << 10, transcendentals=0),
        name="attention_own",
    )(meta, in_hbm(back), tokens, in_hbm(qkv), in_hbm(prob), in_hbm(context), wout, *smalls)


def rest_kernel(meta, back_ref, qkv, prob, wout, wqkv, own, *refs):
    input_grad, grads = refs[-2:]
    group = meta[3]
    groups = qkv.shape[0]
    back = back_ref[...]
    grads[group] = own[...]
    sources = []
    for r in range(1, groups):
        g = group ^ r
        sources.append((qkv.at[g], prob.at[g], wout[at(g * LANES, LANES), :], grads.at[g]))
    groups_back(back.astype(LOW), sources, head_masks())
    total = None
    for g in range(groups):
        term = mul(grads[g], wqkv[g], 1, 1)
        total = term if total is None else total + term
    input_grad[...] = back + total


def run_rest(meta, back, qkv, prob, wout, wqkv, own, block, before=None):
    rows, width = back.shape
    groups = width // LANES
    few = BLOCK // 2
    seqs = few // LANES
    heads = LANES // HEAD_DIM
    by_rows = pl.BlockSpec((few, width), lambda i, m: (2 * block + i, 0))
    held = () if before is None else (before,)
    return pl.pallas_call(
        rest_kernel,
        grid_spec=pltpu.PrefetchScalarGridSpec(
            num_scalar_prefetch=1,
            grid=(2,),
            in_specs=[
                by_rows,
                pl.BlockSpec((groups, few, 3 * LANES), lambda i, m: (0, 2 * block + i, 0)),
                pl.BlockSpec((groups, seqs, heads * LANES, LANES), lambda i, m: (0, 2 * block + i, 0, 0)),
                resident(wout),
                resident(wqkv),
                pl.BlockSpec((few, 3 * LANES), lambda i, m: (2 * block + i, 0)),
            ]
            + [pl.BlockSpec(memory_space=pl.ANY)] * len(held),
            out_specs=by_rows,
            scratch_shapes=[pltpu.VMEM((groups, few, 3 * LANES), LOW)],
        ),
        out_shape=shape((rows, width)),
        input_output_aliases={7: 0} if held else {},
        compiler_params=params(28),
        cost_estimate=pl.CostEstimate(flops=68719476736, bytes_accessed=1 << 10, transcendentals=0),
        name="attention_rest",
    )(meta, in_hbm(back), in_hbm(qkv), in_hbm(prob), wout, wqkv, in_hbm(own), *held)


def places_of(meta):
    return [(meta[2] ^ half) * 4 + (meta[4] ^ bits) for half in range(2) for bits in range(4)]


def halves_of(refs):
    each = len(refs) // 2
    parts = []
    for half in range(2):
        own = refs[half * each : (half + 1) * each]
        few = own[0].shape[0] // 2
        parts += [(ref.at[:few], ref.at[few:]) for ref in own[: 4 if each == 4 else 3]]
        parts += [tuple(own[3:])] if each == 5 else []
    return parts


def squares_kernel(split_rows, count, meta, *refs):
    out, sums = refs[-2:]
    sums[...] = jnp.zeros_like(sums)
    places = places_of(meta)
    for base, parts, limit in ((0, refs[:count], split_rows), (8, refs[count:-2], None)):
        halves = halves_of(parts)
        few = halves[0][0].shape[0]
        row = lax.broadcasted_iota(jnp.int32, (few, LANES), 0)
        for place, pieces in zip(places, halves):
            split = shared = 0.0
            for n, piece in enumerate(pieces):
                square = piece[...] * piece[...]
                if limit is not None:
                    is_split = row < limit - (2 * place + n) * few
                    shared = shared + jnp.sum(jnp.where(is_split, 0.0, square), 0, keepdims=True)
                    square = jnp.where(is_split, square, 0.0)
                split = split + jnp.sum(square, 0, keepdims=True)
            sums[base + place, 0:1, :] = split
            if limit is not None:
                sums[base + place, 1:2, :] = shared
    total = sums[0]
    for n in range(1, 16):
        total = total + sums[n]
    out[...] = total


def squares_of(meta, a_parts, b_parts, split_rows):
    out = shape((8, LANES))
    parts = tuple(a_parts) + tuple(b_parts)
    return pl.pallas_call(
        functools.partial(squares_kernel, split_rows, len(a_parts)),
        grid_spec=pltpu.PrefetchScalarGridSpec(
            num_scalar_prefetch=1,
            grid=(1,),
            in_specs=[whole(p) for p in parts],
            out_specs=whole(out),
            scratch_shapes=[pltpu.VMEM((16, 8, LANES), F32)],
        ),
        out_shape=out,
        compiler_params=params(16),
        name="squares",
    )(meta, *parts)


def ready_kernel(count, meta, *refs):
    a_parts, b_parts, weights = refs[:count], refs[count:-11], refs[-11:-7]
    a_full, b_full = refs[-7:-5]
    held, fetched = refs[-5:-1], refs[-1]
    fetch = [pltpu.make_async_copy(weights[n], held[n], fetched.at[n]) for n in range(4)]
    for copy in fetch:
        copy.start()
    for parts, full in ((a_parts, a_full), (b_parts, b_full)):
        for place, pieces in zip(places_of(meta), halves_of(parts)):
            few = pieces[0].shape[0]
            for n, piece in enumerate(pieces):
                full[pl.ds(pl.multiple_of((2 * place + n) * few, 4), few), :] = piece[...]
    for copy in fetch:
        copy.wait()


def run_ready(meta, a_parts, b_parts, weights):
    here = pl.BlockSpec(memory_space=pltpu.VMEM)
    parts = tuple(a_parts) + tuple(b_parts)
    outs = [pltpu.VMEM((8 * p[0].shape[0], LANES), F32) for p in (a_parts, b_parts)]
    outs += [pltpu.VMEM(w.shape, F32) for w in weights]
    return pl.pallas_call(
        functools.partial(ready_kernel, len(a_parts)),
        in_specs=[pl.BlockSpec(memory_space=pltpu.SMEM)]
        + [here] * len(parts)
        + [pl.BlockSpec(memory_space=pltpu.HBM)] * len(weights),
        out_specs=[here] * len(outs),
        out_shape=outs,
        scratch_shapes=[pltpu.SemaphoreType.DMA((4,))],
        compiler_params=params(16),
        cost_estimate=pl.CostEstimate(flops=64 << 30, bytes_accessed=1 << 10, transcendentals=0),
        name="ready",
    )(meta, *parts, *(in_hbm(w) for w in weights))


def adam_kernel(count, meta, squares, *refs):
    moved = refs[:count]
    a_full, b_full = refs[count : count + 2]
    refs = refs[count + 2 :]
    states, norm_ref, targets = refs[:21], refs[21], refs[22:43]
    sums, done = refs[43:45]
    outs = refs[45:]
    sums[meta[0]] = squares[...]
    for r in range(1, count + 1):
        sums[meta[0] ^ r] = moved[r - 1][...]
    total = sums[0]
    for s in range(1, count + 1):
        total = total + sums[s]
    all_squares = jnp.sum(total[0:1, :], -1, keepdims=True) + jnp.sum(squares[1:2, :], -1, keepdims=True)
    grad_norm = jnp.sqrt(all_squares)
    norm_ref[...] = grad_norm
    factor = jnp.minimum(1.0, clip_at / (grad_norm + 1e-06))
    width = states[5 * 3].shape[1]
    blocks = width // LANES
    copies = []

    def update(index, where, grad, with_decay):
        first, second, weight = (states[3 * index + j][where] for j in range(3))
        for j, value in enumerate(adam_math(weight, first, second, grad, factor, with_decay)):
            outs[3 * index + j][where] = value

    def give(index, where=None):
        for j in range(3 * index, 3 * index + 3):
            source, target = outs[j], targets[j]
            if where is not None:
                source, target = source.at[where], target.at[where]
            copies.append(pltpu.make_async_copy(source, target, done.at[len(copies)]))
            copies[-1].start()

    rows = 4 * width
    for b in range(blocks):
        part = slice(b * width, (b + 1) * width)
        update(2, (part, slice(None)), b_full[part, :], True)
        give(2, part)
    for r in range(blocks):
        part = slice(r * LANES, (r + 1) * LANES)
        for b in range(blocks):
            start = rows + b * width + r * LANES
            update(3, (part, slice(b * LANES, (b + 1) * LANES)), b_full[start : start + LANES, :], True)
        give(3, part)
    for j in range(3):
        update(0, (j,), a_full[j * width : (j + 1) * width, :], True)
        give(0, j)
    base = 3 * width
    for b in range(blocks):
        lanes = slice(b * LANES, (b + 1) * LANES)
        update(1, (slice(None), lanes), a_full[base + b * LANES : base + (b + 1) * LANES, :], True)
    give(1)
    base += width
    update(4, (slice(None), slice(None)), a_full[base : base + 6, :], False)
    give(4)
    base += 8
    for b in range(blocks):
        lanes = slice(b * LANES, (b + 1) * LANES)
        update(5, (slice(None), lanes), a_full[base + 8 * b : base + 8 * b + 6, :], False)
    give(5)
    base += 8 * blocks
    tasks, kinds, _ = states[6 * 3].shape
    each = small_rows(tasks, kinds)
    for b in range(blocks):
        lanes = slice(b * LANES, (b + 1) * LANES)
        for t in range(tasks):
            row = base + each * b + kinds * t
            update(6, (t, slice(None), lanes), a_full[row : row + kinds, :], True)
    give(6)
    for copy in copies:
        copy.wait()


def run_adam(meta, squares, moved, a_full, b_full, states):
    held = pl.BlockSpec(memory_space=pltpu.HBM)
    here = pl.BlockSpec(memory_space=pltpu.VMEM)
    blocks = states[-4].shape[1] // LANES
    args = (squares,) + tuple(moved) + (in_vmem(a_full), in_vmem(b_full))
    return pl.pallas_call(
        functools.partial(adam_kernel, len(moved)),
        in_specs=[pl.BlockSpec(memory_space=pltpu.SMEM)] + [here] * (len(args) + len(states)),
        out_specs=[here] + [held] * len(states),
        out_shape=[shape((1, 1))] + [shape(s.shape) for s in states],
        scratch_shapes=[
            pltpu.VMEM((len(moved) + 1, 8, LANES), F32),
            pltpu.SemaphoreType.DMA((6 * blocks + 3 * 3 + 3 * 4,)),
        ]
        + [pltpu.VMEM(s.shape, F32) for s in states],
        compiler_params=params(18),
        name="adam",
    )(meta, *args, *(in_vmem(s) if n < 12 or n % 3 < 2 else s for n, s in enumerate(states)))


def shares(mesh, *args):
    fast = (
        mesh.shape["head"] == 4
        and mesh.shape["batch"] == 4
        and mesh.shape["rep"] == 2
        and args[5].shape[2] == LANES
        and args[0].shape[0] == 2 * BLOCK
        and mesh.shape["head"] * LANES == args[0].shape[1]
    )
    return (by_permutes if fast else by_gathers)(mesh, *args)


def by_permutes(
    mesh,
    tokens_in,
    out_grad,
    lengths,
    labels,
    task_id,
    qkv_weight,
    qkv_first,
    qkv_second,
    out_weight,
    out_first,
    out_second,
    up_weight,
    up_first,
    up_second,
    down_weight,
    down_first,
    down_second,
    split_bias,
    split_first,
    split_second,
    norm_params,
    norm_first,
    norm_second,
    class_weight,
    class_first,
    class_second,
):
    plane = Plane(mesh)
    width = tokens_in.shape[1]
    here = lax.axis_index("head")
    batch = lax.axis_index("batch")
    rep = lax.axis_index("rep")
    quarter = (batch // 2) * 2 + rep
    meta = jnp.stack([here, batch * plane.rep + rep, batch % 2, here, quarter]).astype(jnp.int32)

    def flat_up(value):
        return value.reshape(-1, LANES)

    def flat_down(value):
        return value.reshape(-1, width)

    def flat_class(value):
        return jnp.transpose(value, (0, 2, 1))

    up_flat, down_flat, classes = flat_up(up_weight), flat_down(down_weight), flat_class(class_weight)
    a_send, b_send = pack(meta, qkv_weight, out_weight, split_bias, up_flat, down_flat)
    turns = range(1, plane.heads)
    a_first = plane.round_on(plane.round(a_send))
    b_first = plane.round(b_send)
    a_near = plane.spread(after(jnp.concatenate([v[:-8] for v in a_first], 0), b_first[0]))
    b_first = plane.round_on(b_first)
    a_corner = plane.corners(a_near)
    b_near = plane.spread(after(jnp.concatenate(b_first, 0), a_near))
    a_moved = plane.shared(a_near, a_corner)

    qkv, prob, context, pre_one, wqkv, wout = run_attention_forward(
        meta, lengths, tokens_in, norm_params, (qkv_weight, out_weight, split_bias), a_first, a_moved, False
    )
    b_near = after(b_near, pre_one)
    b_moved = plane.shared(b_near, plane.corners(b_near))
    output, back_one, norm_grad, class_grad, up_bias_grad, b_keep, b_give = run_feed(
        meta,
        labels,
        task_id,
        in_vmem(pre_one),
        out_grad,
        norm_params,
        classes,
        (up_flat, down_flat, split_bias),
        a_first,
        b_first,
        b_moved,
        False,
    )
    b_parts = plane.quarters(b_keep, b_give, quarter)
    back_one = after(back_one, b_parts)
    own, a_keep, a_give = run_own(
        meta, back_one, tokens_in, qkv, prob, context, wout, (norm_grad, class_grad, up_bias_grad), False
    )
    b_own = plane.scatter(b_parts, a_give)
    b_crossed, b_near = plane.core(b_own), plane.spread(b_own)
    a_parts = plane.quarters(a_keep, a_give, quarter)
    back_one = after(back_one, a_parts, b_crossed)
    input_grad = run_rest(meta, back_one, qkv, prob, wout, wqkv, own, 0)
    a_own = plane.scatter(a_parts, input_grad)
    b_near = after(b_near, input_grad)
    b_corner = plane.corners(b_near)
    a_crossed, a_near = plane.rejoin(a_own)
    input_grad = run_rest(meta, after(back_one, a_crossed), qkv, prob, wout, wqkv, own, 1, input_grad)
    b_near, b_corner, a_near = after((b_near, b_corner, a_near), input_grad)
    b_parts = plane.rejoin_on(b_own, b_crossed, (b_near[2], b_near[1]) + b_corner)
    a_parts = plane.rejoin_on(a_own, a_crossed, a_near)
    squares = squares_of(meta, a_parts, b_parts, 4 * width + 8)
    a_full, b_full, *held = run_ready(
        meta, after(a_parts, squares), b_parts, (qkv_weight, out_weight, up_flat, down_flat)
    )
    moved = after(tuple(plane.along(squares, r) for r in turns), b_full)
    states = (
        (qkv_first, qkv_second, held[0])
        + (out_first, out_second, held[1])
        + (flat_up(up_first), flat_up(up_second), held[2])
        + (flat_down(down_first), flat_down(down_second), held[3])
        + (split_first, split_second, split_bias)
        + (norm_first, norm_second, norm_params)
        + (flat_class(class_first), flat_class(class_second), classes)
    )
    grad_norm, *new = run_adam(meta, squares, moved, a_full, b_full, states)
    new[6:9] = [v.reshape(up_weight.shape) for v in new[6:9]]
    new[9:12] = [v.reshape(down_weight.shape) for v in new[9:12]]
    new[18:21] = [jnp.transpose(v, (0, 2, 1)) for v in new[18:21]]
    return (output, input_grad, grad_norm[0, 0]) + tuple(new)


def lower_kernel(source, target):
    target[...] = source[...].astype(LOW)


def lowered(value):
    flat = value.reshape(-1, value.shape[-1])
    out = pl.pallas_call(
        lower_kernel, out_shape=shape(flat.shape, LOW), compiler_params=params(), name="lowered"
    )(flat)
    return out.reshape(value.shape)


def by_gathers(
    mesh,
    tokens_in,
    out_grad,
    lengths,
    labels,
    task_id,
    qkv_weight,
    qkv_first,
    qkv_second,
    out_weight,
    out_first,
    out_second,
    up_weight,
    up_first,
    up_second,
    down_weight,
    down_first,
    down_second,
    split_bias,
    split_first,
    split_second,
    norm_params,
    norm_first,
    norm_second,
    class_weight,
    class_first,
    class_second,
):
    width = tokens_in.shape[1]
    cols = qkv_weight.shape[2]
    groups = width // LANES
    hidden = 4 * cols
    here = lax.axis_index("head")
    zero = jnp.zeros_like(here)
    meta = jnp.stack([here, zero, zero, here * cols // LANES, zero]).astype(jnp.int32)
    full_qkv = lax.all_gather(qkv_weight, "head", axis=2, tiled=True)
    full_out = lax.all_gather(out_weight, "head", axis=0, tiled=True)
    full_up = lax.all_gather(up_weight.reshape(width, hidden), "head", axis=0)
    full_down = lax.all_gather(down_weight.reshape(hidden, width), "head", axis=0)
    full_bias = lax.all_gather(split_bias, "head", axis=1, tiled=True)
    wqkv = full_qkv.reshape(3, width, groups, LANES).transpose(2, 1, 0, 3).reshape(groups, width, 3 * LANES)
    wqkv, wout = lowered(wqkv), lowered(full_out)
    qv_bias = jnp.pad(full_bias[:2].reshape(2, groups, LANES).transpose(1, 0, 2), ((0, 0), (0, 6), (0, 0)))
    shards = width // cols
    up_bias = full_bias[2:].reshape(4, shards, cols).transpose(1, 0, 2).reshape(shards, 1, hidden)
    up_bias = jnp.pad(up_bias, ((0, 0), (0, 7), (0, 0)))
    classes = jnp.transpose(class_weight, (0, 2, 1))

    qkv, prob, context, pre_one = run_attention_forward(
        meta, lengths, tokens_in, norm_params, (wqkv, wout, qv_bias), (), (), True
    )
    output, back_one, norm_grad, class_grad, up_bias_grad, up_grad, down_grad = run_feed(
        meta,
        labels,
        task_id,
        pre_one,
        out_grad,
        norm_params,
        classes,
        (lowered(full_up), lowered(full_down), up_bias),
        (),
        (),
        (),
        True,
    )
    own, qkv_grad, out_w_grad, split_grad = run_own(meta, back_one, tokens_in, qkv, prob, context, wout, (), True)
    input_grad = None
    for block in range(tokens_in.shape[0] // BLOCK):
        input_grad = run_rest(meta, back_one, qkv, prob, wout, wqkv, own, block, input_grad)
    start = here * cols % LANES
    qkv_grad = qkv_grad.reshape(width, 3, LANES).transpose(1, 0, 2)
    qkv_grad = lax.dynamic_slice_in_dim(qkv_grad, start, cols, 2)
    out_w_grad = lax.dynamic_slice_in_dim(out_w_grad, start, cols, 0)
    split_grad = lax.dynamic_slice_in_dim(split_grad[:2], start, cols, 1)
    split_grad = jnp.concatenate([split_grad, up_bias_grad[0].reshape(4, cols)], 0)
    summed = lax.psum(
        (
            qkv_grad,
            out_w_grad,
            up_grad.reshape(up_weight.shape),
            down_grad.reshape(down_weight.shape),
            split_grad,
            norm_grad[:6],
            jnp.transpose(class_grad, (0, 2, 1)),
        ),
        ("batch", "rep"),
    )
    split_square = lax.psum(sum(jnp.sum(v * v) for v in summed[:5]), "head")
    grad_norm = jnp.sqrt(split_square + sum(jnp.sum(v * v) for v in summed[5:]))
    factor = jnp.minimum(1.0, clip_at / (grad_norm + 1e-06))
    states = (
        (qkv_weight, qkv_first, qkv_second, True),
        (out_weight, out_first, out_second, True),
        (up_weight, up_first, up_second, True),
        (down_weight, down_first, down_second, True),
        (split_bias, split_first, split_second, False),
        (norm_params, norm_first, norm_second, False),
        (class_weight, class_first, class_second, True),
    )
    results = ()
    for grad, (weight, first, second, decay) in zip(summed, states):
        results += adam_math(weight, first, second, grad, factor, decay)
    return (output, input_grad, grad_norm) + results


def solution(mesh):
    rows = P(("batch", "rep"), None)
    seqs = P(("batch", "rep"))
    kinds = (
        (P(None, None, "head"),) * 3
        + (P("head", None),) * 3
        + (P(None, None, "head"),) * 3
        + (P(None, "head", None),) * 3
        + (P(None, "head"),) * 3
        + (P(),) * 6
    )
    return jax.shard_map(
        functools.partial(shares, mesh),
        mesh=mesh,
        in_specs=(rows, rows, seqs, seqs, seqs) + kinds,
        out_specs=(rows, rows, P()) + kinds,
        check_vma=False,
    )
```
